128 devices in a mesh: dp: 64 (over y, x_hi, z, core), mp: 2 (over x_lo).
Axes of the slice: x: 4 (x_hi: 2, x_lo: 2; x = x_hi * 2 + x_lo), y: 4, z: 4, core: 2. Of those that a mesh axis runs over, the one named last changes fastest.
Arguments:
- tokens: bfloat16 [16384, 2048], P('dp'), may hold values from -6 to 6
- lengths: int32 [64], P('dp'), may hold values from 64 to 256, as said below
- cotangent: bfloat16 [16384, 2048], P('dp'), may hold values from -6 to 6
- gain_attn: float32 [2048], replicated, may hold values from 0.1 to 1.9
- gain_ffn: float32 [2048], replicated, may hold values from 0.1 to 1.9
- w_query: bfloat16 [2048, 2048], P(None, 'mp'), may hold values from -0.125 to 0.125
- w_key: bfloat16 [2048, 2048], P(None, 'mp'), may hold values from -0.125 to 0.125
- w_value: bfloat16 [2048, 2048], P(None, 'mp'), may hold values from -0.125 to 0.125
- output_weight: bfloat16 [2048, 2048], P('mp'), may hold values from -0.125 to 0.125
- w_gate: bfloat16 [2048, 5632], P(None, 'mp'), may hold values from -0.125 to 0.125
- w_up: bfloat16 [2048, 5632], P(None, 'mp'), may hold values from -0.125 to 0.125
- w_down: bfloat16 [5632, 2048], P(('mp', 'dp')), may hold values from -0.078125 to 0.078125
- left_query: float32 [2048, 16], replicated, may hold values from -0.125 to 0.125
- right_query: float32 [16, 2048], P(None, 'mp'), may hold values from -0.375 to 0.375
- magnitude_query: float32 [2048], P('mp'), may hold values from 0.8 to 2
- left_key: float32 [2048, 16], replicated, may hold values from -0.125 to 0.125
- right_key: float32 [16, 2048], P(None, 'mp'), may hold values from -0.375 to 0.375
- magnitude_key: float32 [2048], P('mp'), may hold values from 0.8 to 2
- left_value: float32 [2048, 16], replicated, may hold values from -0.125 to 0.125
- right_value: float32 [16, 2048], P(None, 'mp'), may hold values from -0.375 to 0.375
- magnitude_value: float32 [2048], P('mp'), may hold values from 0.5 to 2
- output_left_factor: float32 [2048, 16], P('mp'), may hold values from -0.125 to 0.125
- output_right_factor: float32 [16, 2048], replicated, may hold values from -0.375 to 0.375
- magnitude_output: float32 [2048], replicated, may hold values from 2 to 6
- left_gate: float32 [2048, 16], replicated, may hold values from -0.125 to 0.125
- right_gate: float32 [16, 5632], P(None, 'mp'), may hold values from -0.375 to 0.375
- magnitude_gate: float32 [5632], P('mp'), may hold values from 0.5 to 2
- left_up: float32 [2048, 16], replicated, may hold values from -0.125 to 0.125
- right_up: float32 [16, 5632], P(None, 'mp'), may hold values from -0.375 to 0.375
- magnitude_up: float32 [5632], P('mp'), may hold values from 0.5 to 2
- down_left_factor: float32 [5632, 16], P('mp'), may hold values from -0.078125 to 0.078125
- down_right_factor: float32 [16, 2048], replicated, may hold values from -0.375 to 0.375
- magnitude_down: float32 [2048], replicated, may hold values from 1 to 4
Outputs:
- layer_out: bfloat16 [16384, 2048], P('dp')
- grad_tokens: bfloat16 [16384, 2048], P('dp')
- grad_left_query: float32 [2048, 16], replicated
- grad_right_query: float32 [16, 2048], P(None, 'mp')
- grad_magnitude_query: float32 [2048], P('mp')
- grad_left_key: float32 [2048, 16], replicated
- grad_right_key: float32 [16, 2048], P(None, 'mp')
- grad_magnitude_key: float32 [2048], P('mp')
- grad_left_value: float32 [2048, 16], replicated
- grad_right_value: float32 [16, 2048], P(None, 'mp')
- grad_magnitude_value: float32 [2048], P('mp')
- grad_left_output: float32 [2048, 16], P('mp')
- grad_right_output: float32 [16, 2048], replicated
- grad_magnitude_output: float32 [2048], replicated
- grad_left_gate: float32 [2048, 16], replicated
- grad_right_gate: float32 [16, 5632], P(None, 'mp')
- grad_magnitude_gate: float32 [5632], P('mp')
- grad_left_up: float32 [2048, 16], replicated
- grad_right_up: float32 [16, 5632], P(None, 'mp')
- grad_magnitude_up: float32 [5632], P('mp')
- grad_left_down: float32 [5632, 16], P('mp')
- grad_right_down: float32 [16, 2048], replicated
- grad_magnitude_down: float32 [2048], replicated
The draws below stay inside these ranges and needn't reach their ends.
Inputs may be any that keep to these rules, and one draw needn't show every extreme that they name: `lengths`: key positions at or past a sequence's length are padding. In every draw some sequence has length 256 and some other one 256 // 4.
All inputs are finite; a program needn't handle non-finite values.
Results may differ from the reference program's by a relative error of at most 0.023.
Values may be sent and summed in bfloat16 or wider, within the bound.
No kernel may reach another device: no remote copies, remote signals or barrier semaphores. Data moves between devices by JAX's collectives and lax.ppermute only.
A program may use at most 384 MiB of HBM per device.

```python
import math
import jax
import jax.numpy as jnp
from jax import lax

D = 2048
HEADS = 16
HEAD_DIM = 128
FF = 5632
ADAPTER_RANK = 16
ADAPTER_NUMERATOR = 32
SEQ_LEN = 256
SEQS = 64
TOKENS = 16384


def draw_lengths(key, part):
    key = jax.random.fold_in(key, 11)
    first_key, second_key, third_key = jax.random.split(key, 3)
    drawn = jax.random.randint(first_key, (SEQS,), SEQ_LEN // 4, SEQ_LEN + 1)
    longest = jax.random.randint(second_key, (), 0, SEQS)
    shortest = (longest + 1 + jax.random.randint(third_key, (), 0, SEQS - 1)) % SEQS
    slots = jnp.arange(SEQS)
    drawn = jnp.where(slots == longest, SEQ_LEN, drawn)
    return jnp.where(slots == shortest, SEQ_LEN // 4, drawn).astype(jnp.int32)


def block_levels(stream_key, extent, pieces, least, top_value):
    gain, own = 1.0, jax.random.fold_in(stream_key, 6)
    for position, parts in pieces:
        steps = jnp.exp(jax.random.uniform(jax.random.fold_in(own, position), (parts,), jnp.float32, least / len(pieces), top_value / len(pieces)))
        gain = gain * jnp.repeat(steps, extent[position] // parts).reshape([-1 if axis == position else 1 for axis in range(len(extent))])
    return gain


def scatter_about(key, dims, deviation, reach, pieces=(), kind=jnp.bfloat16):
    factor_of = block_levels(key, dims, pieces, -0.22, 0.18) if pieces else 1.0
    values = jax.random.normal(key, dims, jnp.float32) * deviation * factor_of
    return jnp.minimum(jnp.maximum(values, -reach), reach).astype(kind)


def setup_inputs(seed: int = 0) -> dict:
    key_of = jax.random.split(jax.random.key(seed), 34)
    return {
        "tokens": scatter_about(key_of[0], (TOKENS, D), 1.0, 6.0, ((0, 64),)),
        "lengths": draw_lengths(jax.random.fold_in(key_of[33], 71), 0),
        "cotangent": scatter_about(key_of[2], (TOKENS, D), 1.0, 6.0, ((0, 64),)),
        "gain_attn": jnp.clip(1.0 + 0.18 * jax.random.normal(key_of[3], (D,), jnp.float32), 0.1, 1.9),
        "gain_ffn": jnp.clip(1.0 + 0.18 * jax.random.normal(key_of[4], (D,), jnp.float32), 0.1, 1.9),
        "w_query": scatter_about(key_of[5], (D, D), D ** -0.5, 0.125, ((1, 2),)),
        "w_key": scatter_about(key_of[6], (D, D), D ** -0.5, 0.125, ((1, 2),)),
        "w_value": scatter_about(key_of[7], (D, D), D ** -0.5, 0.125, ((1, 2),)),
        "output_weight": scatter_about(key_of[8], (D, D), D ** -0.5, 0.125, ((0, 2),)),
        "w_gate": scatter_about(key_of[9], (D, FF), D ** -0.5, 0.125, ((1, 2),)),
        "w_up": scatter_about(key_of[10], (D, FF), D ** -0.5, 0.125, ((1, 2),)),
        "w_down": scatter_about(key_of[11], (FF, D), FF ** -0.5, 0.078125, ((0, 128),)),
        "left_query": scatter_about(key_of[12], (D, ADAPTER_RANK), D ** -0.5, 0.125, (), jnp.float32),
        "right_query": scatter_about(key_of[13], (ADAPTER_RANK, D), (4 * ADAPTER_NUMERATOR * ADAPTER_NUMERATOR // ADAPTER_RANK) ** -0.5, 0.375, ((1, 2),), jnp.float32),
        "magnitude_query": jnp.clip(jnp.exp(math.log(2.0) - 0.9162907 * jax.random.uniform(key_of[14], (D,), jnp.float32) ** block_levels(key_of[14], (D,), ((0, 2),), -0.2, 0.2)), 0.8, 2.0),
        "left_key": scatter_about(key_of[15], (D, ADAPTER_RANK), D ** -0.5, 0.125, (), jnp.float32),
        "right_key": scatter_about(key_of[16], (ADAPTER_RANK, D), (4 * ADAPTER_NUMERATOR * ADAPTER_NUMERATOR // ADAPTER_RANK) ** -0.5, 0.375, ((1, 2),), jnp.float32),
        "magnitude_key": jnp.clip(jnp.exp(math.log(2.0) - 0.9162907 * jax.random.uniform(key_of[17], (D,), jnp.float32) ** block_levels(key_of[17], (D,), ((0, 2),), -0.2, 0.2)), 0.8, 2.0),
        "left_value": scatter_about(key_of[18], (D, ADAPTER_RANK), D ** -0.5, 0.125, (), jnp.float32),
        "right_value": scatter_about(key_of[19], (ADAPTER_RANK, D), (4 * ADAPTER_NUMERATOR * ADAPTER_NUMERATOR // ADAPTER_RANK) ** -0.5, 0.375, ((1, 2),), jnp.float32),
        "magnitude_value": jnp.clip(jnp.exp(math.log(2.0) - 1.3862944 * jax.random.uniform(key_of[20], (D,), jnp.float32) ** block_levels(key_of[20], (D,), ((0, 2),), -0.2, 0.2)), 0.5, 2.0),
        "output_left_factor": scatter_about(key_of[21], (D, ADAPTER_RANK), D ** -0.5, 0.125, ((0, 2),), jnp.float32),
        "output_right_factor": scatter_about(key_of[22], (ADAPTER_RANK, D), (4 * ADAPTER_NUMERATOR * ADAPTER_NUMERATOR // ADAPTER_RANK) ** -0.5, 0.375, (), jnp.float32),
        "magnitude_output": jnp.clip(jnp.exp(jax.random.uniform(key_of[23], (D,), jnp.float32, math.log(2.0), math.log(6.0))), 2.0, 6.0),
        "left_gate": scatter_about(key_of[24], (D, ADAPTER_RANK), D ** -0.5, 0.125, (), jnp.float32),
        "right_gate": scatter_about(key_of[25], (ADAPTER_RANK, FF), (4 * ADAPTER_NUMERATOR * ADAPTER_NUMERATOR // ADAPTER_RANK) ** -0.5, 0.375, ((1, 2),), jnp.float32),
        "magnitude_gate": jnp.clip(jnp.exp(math.log(2.0) - 1.3862944 * jax.random.uniform(key_of[26], (FF,), jnp.float32) ** block_levels(key_of[26], (FF,), ((0, 2),), -0.2, 0.2)), 0.5, 2.0),
        "left_up": scatter_about(key_of[27], (D, ADAPTER_RANK), D ** -0.5, 0.125, (), jnp.float32),
        "right_up": scatter_about(key_of[28], (ADAPTER_RANK, FF), (4 * ADAPTER_NUMERATOR * ADAPTER_NUMERATOR // ADAPTER_RANK) ** -0.5, 0.375, ((1, 2),), jnp.float32),
        "magnitude_up": jnp.clip(jnp.exp(math.log(2.0) - 1.3862944 * jax.random.uniform(key_of[29], (FF,), jnp.float32) ** block_levels(key_of[29], (FF,), ((0, 2),), -0.2, 0.2)), 0.5, 2.0),
        "down_left_factor": scatter_about(key_of[30], (FF, ADAPTER_RANK), FF ** -0.5, 0.078125, ((0, 2),), jnp.float32),
        "down_right_factor": scatter_about(key_of[31], (ADAPTER_RANK, D), (4 * ADAPTER_NUMERATOR * ADAPTER_NUMERATOR // ADAPTER_RANK) ** -0.5, 0.375, (), jnp.float32),
        "magnitude_down": jnp.clip(jnp.exp(jax.random.uniform(key_of[32], (D,), jnp.float32, math.log(1.0), math.log(4.0))), 1.0, 4.0),
    }


EPSILON = 1e-05
TOP_PRECISION = lax.Precision.HIGHEST

@jax.custom_vjp
def low(v):
    return lax.optimization_barrier(v.astype(jnp.bfloat16)).astype(jnp.float32)

@jax.custom_vjp
def low_back(v):
    return v

def low_keep(v):
    return (low(v), None)

def low_pass(kept, grad):
    return (grad,)

def back_keep(v):
    return (v, None)

def back_low(kept, grad):
    return (low(grad),)
low.defvjp(low_keep, low_pass)
low_back.defvjp(back_keep, back_low)

def rms_scale(values, gain_vector):
    inverse = lax.rsqrt(lax.optimization_barrier(jnp.mean(values * values, axis=-1, keepdims=True)) + EPSILON)
    return values * inverse * gain_vector

def rope_tables(seq_span, head_width):
    half_width = head_width // 2
    frequency = 10000.0 ** (-(jnp.arange(half_width, dtype=jnp.float32) * 2.0) / head_width)
    angles = jnp.arange(seq_span, dtype=jnp.float32)[:, None] * frequency[None, :]
    return (jnp.cos(angles)[:, None, :], jnp.sin(angles)[:, None, :])

def rotate(values, cosine, sine_table):
    half_width = values.shape[-1] // 2
    first_half = values[..., :half_width]
    second_half = values[..., half_width:]
    return jnp.concatenate([first_half * cosine - second_half * sine_table, second_half * cosine + first_half * sine_table], axis=-1)

def dora_weight(frozen_weight, factor_left, factor_right, magnitude):
    unit_direction = frozen_weight + ADAPTER_NUMERATOR / ADAPTER_RANK * jnp.dot(factor_left, factor_right, precision=TOP_PRECISION)
    col_norms = jnp.sqrt(lax.optimization_barrier(jnp.sum(unit_direction * unit_direction, axis=0)))
    return (low(unit_direction), magnitude / col_norms)

def apply_weight(input_rows, merged_pair):
    return low_back(jnp.dot(input_rows, merged_pair[0], precision=TOP_PRECISION)) * merged_pair[1]

def layer_sequence(sequence, seq_length, gain_attn, gain_ffn, merged, cosine, sine_table):
    seq_span = sequence.shape[0]
    head_shape = (seq_span, HEADS, HEAD_DIM)
    first_in = low(rms_scale(sequence, gain_attn))
    queries = apply_weight(first_in, merged[0]).reshape(head_shape)
    keys_all = apply_weight(first_in, merged[1]).reshape(head_shape)
    values_low = low(apply_weight(first_in, merged[2])).reshape(head_shape)
    query_low = low(rotate(queries, cosine, sine_table) * HEAD_DIM ** (-0.5))
    key_low = low(rotate(keys_all, cosine, sine_table))
    scores = low_back(jnp.einsum('shd,thd->hst', query_low, key_low, precision=TOP_PRECISION))
    positions = jnp.arange(seq_span)
    allowed = (positions[None, :] <= positions[:, None]) & (positions[None, :] < seq_length)
    attn_probs = jax.nn.softmax(jnp.where(allowed[None], scores, -1e+30), axis=-1)
    mixed_heads = jnp.einsum('hst,thd->shd', low(attn_probs), values_low, precision=TOP_PRECISION)
    attn_mix = low(low_back(mixed_heads.reshape(seq_span, D)))
    hidden = sequence + apply_weight(attn_mix, merged[3])
    second_in = low(rms_scale(hidden, gain_ffn))
    gate_value = apply_weight(second_in, merged[4])
    up_value = apply_weight(second_in, merged[5])
    act_low = low(jax.nn.silu(gate_value) * up_value)
    return hidden + apply_weight(act_low, merged[6])

def reference(tokens, lengths, cotangent, gain_attn, gain_ffn, w_query, w_key, w_value, output_weight, w_gate, w_up, w_down, left_query, right_query, magnitude_query, left_key, right_key, magnitude_key, left_value, right_value, magnitude_value, output_left_factor, output_right_factor, magnitude_output, left_gate, right_gate, magnitude_gate, left_up, right_up, magnitude_up, down_left_factor, down_right_factor, magnitude_down):
    frozen_weights = (w_query.astype(jnp.float32), w_key.astype(jnp.float32), w_value.astype(jnp.float32), output_weight.astype(jnp.float32), w_gate.astype(jnp.float32), w_up.astype(jnp.float32), w_down.astype(jnp.float32))
    left_factors = (left_query, left_key, left_value, output_left_factor, left_gate, left_up, down_left_factor)
    right_factors = (right_query, right_key, right_value, output_right_factor, right_gate, right_up, down_right_factor)
    magnitudes = (magnitude_query, magnitude_key, magnitude_value, magnitude_output, magnitude_gate, magnitude_up, magnitude_down)

    def forward(input_rows, left_all, right_all, magnitude_all):
        merged = tuple((dora_weight(frozen_weights[proj_index], left_all[proj_index], right_all[proj_index], magnitude_all[proj_index]) for proj_index in range(7)))
        cosine, sine_table = rope_tables(SEQ_LEN, HEAD_DIM)

        def scan_step(carry_value, item_pair):
            return (carry_value, layer_sequence(item_pair[0], item_pair[1], gain_attn, gain_ffn, merged, cosine, sine_table))
        carry_value, outputs = lax.scan(jax.checkpoint(scan_step), jnp.zeros((), jnp.float32), (input_rows.reshape(SEQS, SEQ_LEN, D), lengths))
        return outputs.reshape(SEQS * SEQ_LEN, D)
    result, pullback = jax.vjp(forward, tokens.astype(jnp.float32), left_factors, right_factors, magnitudes)
    grad_inputs, grad_lefts, grad_rights, grad_mags = pullback(cotangent.astype(jnp.float32))
    return (result.astype(jnp.bfloat16), grad_inputs.astype(jnp.bfloat16), grad_lefts[0], grad_rights[0], grad_mags[0], grad_lefts[1], grad_rights[1], grad_mags[1], grad_lefts[2], grad_rights[2], grad_mags[2], grad_lefts[3], grad_rights[3], grad_mags[3], grad_lefts[4], grad_rights[4], grad_mags[4], grad_lefts[5], grad_rights[5], grad_mags[5], grad_lefts[6], grad_rights[6], grad_mags[6])
```

```python
import jax
import jax.numpy as jnp
import numpy as np
from jax import lax
from jax.sharding import Mesh, PartitionSpec as P

HEAD_DIM = 128
RANK = 16
RATIO = 2.0
EPSILON = 1e-05
F32 = jnp.float32
BF16 = jnp.bfloat16
DP = ("y", "xh", "z", "core")
GROUP = ("xh", "core", "mp")


def dot(a, b, dims=((1,), (0,))):
    return lax.dot_general(a.astype(BF16), b.astype(BF16), (dims, ((), ())), preferred_element_type=F32)


def dot_nt(a, b):
    return dot(a, b, ((1,), (1,)))


def dot_tn(a, b):
    return dot(a, b, ((0,), (0,)))


def rope_tables(span):
    half = HEAD_DIM // 2
    frequency = 10000.0 ** (-(np.arange(half, dtype=np.float64) * 2.0) / HEAD_DIM)
    angles = np.arange(span, dtype=np.float64)[:, None] * frequency[None, :]
    return (np.cos(angles).astype(np.float32)[:, None, :], np.sin(angles).astype(np.float32)[:, None, :])


def rotate(values, cosine, sine):
    half = HEAD_DIM // 2
    first, second = values[..., :half], values[..., half:]
    return jnp.concatenate([first * cosine - second * sine, second * cosine + first * sine], axis=-1)


def swap(x, axis_name, k):
    n = lax.axis_size(axis_name)
    return lax.ppermute(x, axis_name, [(i, i ^ k) for i in range(n)])


def tree(parts):
    while len(parts) > 1:
        parts = [parts[i] + parts[i + 1] for i in range(0, len(parts), 2)]
    return parts[0]


def xor_sum(x, axis_name):
    n = lax.axis_size(axis_name)
    return tree([x] + [swap(x, axis_name, k) for k in range(1, n)])


def mp_sum(x):
    low = x.astype(BF16)
    return low.astype(F32) + swap(low, "mp", 1).astype(F32)


def stats(w, left, right):
    ww = w.astype(F32)
    lw = dot_tn(left, w)
    ld = lw + RATIO * dot(dot_tn(left, left), right)
    return jnp.sum(ww * ww, axis=0, keepdims=True) + RATIO * jnp.sum(right * (lw + ld), axis=0, keepdims=True), ld


def pad_cols(x, n):
    return jnp.pad(x, ((0, 0), (0, n - x.shape[1])))


def reduce_grads(local, mixed, vectors):
    flat = jnp.concatenate(vectors, axis=1)
    wide = -(-flat.shape[1] // 2048) * 128
    flat = pad_cols(flat, wide * 16).reshape(16, wide)
    loc = jnp.concatenate(local + [flat], axis=1)
    ln = loc.shape[1]
    share_l = -(-ln // 512) * 128
    loc = pad_cols(loc, share_l * 4).astype(BF16)
    mix = jnp.concatenate(mixed, axis=1).astype(BF16)
    share_m = mix.shape[1] // 8
    me_l = lax.axis_index(("xh", "core"))
    me = lax.axis_index(GROUP)

    def cut(k):
        m = lax.dynamic_slice_in_dim(mix, (me ^ k) * share_m, share_m, 1)
        if k & 1:
            return m
        part = lax.dynamic_slice_in_dim(loc, (me_l ^ (k >> 1)) * share_l, share_l, 1)
        return jnp.concatenate([m, part], axis=1)

    got = [cut(0)] + [swap(cut(k), GROUP, k) for k in range(1, 8)]
    got = [g.astype(F32) for g in got]
    own = jnp.concatenate([tree([g[:, :share_m] for g in got]), tree([got[k][:, share_m:] for k in (0, 2, 4, 6)])], axis=1)
    for name in ("z", "y"):
        own = xor_sum_low(own, name)
    own = own.astype(BF16)
    back = [own] + [swap(own if k % 2 == 0 else own[:, :share_m], GROUP, k) for k in range(1, 8)]
    stacked = jnp.stack([b[:, :share_m] for b in back])
    order = jnp.arange(8) ^ me
    mix = jnp.concatenate(list(jnp.take(stacked, order, axis=0)), axis=1).astype(F32)
    stacked = jnp.stack([back[k][:, share_m:] for k in (0, 2, 4, 6)])
    loc = jnp.concatenate(list(jnp.take(stacked, jnp.arange(4) ^ me_l, axis=0)), axis=1).astype(F32)
    outs_l, outs_m, outs_v, at = [], [], [], 0
    for x in local:
        outs_l.append(loc[:, at : at + x.shape[1]])
        at += x.shape[1]
    flat = loc[:, at : at + wide].reshape(1, wide * 16)
    at = 0
    for x in vectors:
        outs_v.append(flat[0, at : at + x.shape[1]])
        at += x.shape[1]
    at = 0
    for x in mixed:
        outs_m.append(mix[:, at : at + x.shape[1]])
        at += x.shape[1]
    return outs_l, outs_m, outs_v


def xor_sum_low(x, axis_name):
    n = lax.axis_size(axis_name)
    low = x.astype(BF16)
    return tree([low.astype(F32)] + [swap(low, axis_name, k).astype(F32) for k in range(1, n)])


def body(
    tokens, lengths, cotangent, gain_attn, gain_ffn,
    w_query, w_key, w_value, w_output, w_gate, w_up, w_down,
    left_query, right_query, mag_query,
    left_key, right_key, mag_key,
    left_value, right_value, mag_value,
    left_output, right_output, mag_output,
    left_gate, right_gate, mag_gate,
    left_up, right_up, mag_up,
    left_down, right_down, mag_down,
):
    rows = tokens.shape[0]
    heads = w_query.shape[1] // HEAD_DIM
    head_shape = (rows, heads, HEAD_DIM)
    x = tokens.astype(F32)
    down = lax.all_gather(w_down, DP, axis=0, tiled=True)
    weights = dict(query=w_query, key=w_key, value=w_value, output=w_output, gate=w_gate, up=w_up, down=down)
    lefts = dict(query=left_query, key=left_key, value=left_value, output=left_output, gate=left_gate, up=left_up, down=left_down)
    rights = dict(query=right_query, key=right_key, value=right_value, output=right_output, gate=right_gate, up=right_up, down=right_down)
    mags = dict(query=mag_query, key=mag_key, value=mag_value, output=mag_output, gate=mag_gate, up=mag_up, down=mag_down)
    mags = {p: m[None, :] for p, m in mags.items()}
    sq, ld = {}, {}
    for p in ("query", "key", "value", "output", "gate", "up"):
        sq[p], ld[p] = stats(weights[p], lefts[p], rights[p])
    shard = w_down.shape[0]
    left_shard = lax.dynamic_slice_in_dim(left_down, lax.axis_index(DP) * shard, shard, 0)
    sq_down, _ = stats(w_down, left_shard, right_down)
    for name in (GROUP, "z", "y"):
        sq_down = xor_sum(sq_down, name)
    sq["down"] = sq_down
    sq["output"] = sq["output"] + swap(sq["output"], "mp", 1)
    norm = {p: jnp.sqrt(s) for p, s in sq.items()}
    fac = {p: mags[p] / norm[p] for p in norm}

    def project(p, a):
        al = dot(a, lefts[p])
        return dot(a, weights[p]) + RATIO * dot(al, rights[p]), al

    def back(p, gp):
        z = dot_nt(gp, rights[p])
        return dot_nt(gp, weights[p]) + RATIO * dot_nt(z, lefts[p]), z

    def correction(p, ncoef):
        nr = ncoef * rights[p]
        return dot_nt(nr, weights[p]) + RATIO * dot_nt(dot_nt(nr, rights[p]), lefts[p])

    inv1 = lax.rsqrt(jnp.mean(x * x, axis=-1, keepdims=True) + EPSILON)
    u1 = x * inv1
    first_in = (u1 * gain_attn).astype(BF16)
    values, als = {}, {}
    for p in ("query", "key", "value"):
        prod, als[p] = project(p, first_in)
        values[p] = prod * fac[p]
    cosine, sine = rope_tables(rows)
    scale = HEAD_DIM ** (-0.5)
    q = (rotate(values["query"].reshape(head_shape), cosine, sine) * scale).astype(BF16)
    k = rotate(values["key"].reshape(head_shape), cosine, sine).astype(BF16)
    v = values["value"].astype(BF16).reshape(head_shape)
    pos = jnp.arange(rows)
    allowed = (pos[None, :] <= pos[:, None]) & (pos[None, :] < lengths[0])
    scores = jnp.einsum("shd,thd->hst", q, k, preferred_element_type=F32)
    scores = jnp.where(allowed[None], scores, -1e30)
    e = jnp.exp(scores - jnp.max(scores, axis=-1, keepdims=True))
    probs = e / jnp.sum(e, axis=-1, keepdims=True)
    probs_low = probs.astype(BF16)
    attn_mix = jnp.einsum("hst,thd->shd", probs_low, v, preferred_element_type=F32).reshape(rows, -1).astype(BF16)
    part, als["output"] = project("output", attn_mix)
    value_output = mp_sum(part) * fac["output"]
    hidden = x + value_output
    inv2 = lax.rsqrt(jnp.mean(hidden * hidden, axis=-1, keepdims=True) + EPSILON)
    u2 = hidden * inv2
    second_in = (u2 * gain_ffn).astype(BF16)
    for p in ("gate", "up"):
        prod, als[p] = project(p, second_in)
        values[p] = prod * fac[p]
    gv, uv = values["gate"], values["up"]
    sig = jax.nn.sigmoid(gv)
    act = (gv * sig * uv).astype(BF16)
    cot = cotangent.astype(F32)
    part_down, als["down"] = project("down", act)
    value_down = mp_sum(part_down) * fac["down"]
    layer_out = (hidden + value_down).astype(BF16)

    grad_left, grad_right, grad_mag = {}, {}, {}
    gps, sums = {}, {}

    def adapters(p, a, g, value, nrows=None):
        s = jnp.sum(g * value, axis=0, keepdims=True)
        grad_mag[p] = s / mags[p]
        ncoef = -s / sq[p]
        gp = (g * fac[p]).astype(BF16)
        z = dot_nt(gp, rights[p])
        grad_left[p] = RATIO * (dot_tn(z, a) + correction(p, ncoef))
        grad_right[p] = RATIO * (dot_tn(als[p], gp) + ld[p] * ncoef)
        return gp

    _, ld["down"] = stats(down, left_down, right_down)
    gp_down = adapters("down", act, cot, value_down)
    grad_act, _ = back("down", gp_down)
    grad_gate = grad_act * uv * sig * (1.0 + gv * (1.0 - sig))
    grad_up = grad_act * gv * sig
    gp_gate = adapters("gate", second_in, grad_gate, gv)
    gp_up = adapters("up", second_in, grad_up, uv)
    grad_second = mp_sum(back("gate", gp_gate)[0] + back("up", gp_up)[0])
    w2 = grad_second * gain_ffn
    grad_hidden = cot + inv2 * (w2 - u2 * jnp.mean(w2 * u2, axis=-1, keepdims=True))
    gp_output = adapters("output", attn_mix, grad_hidden, value_output)
    grad_attn = back("output", gp_output)[0].astype(BF16).reshape(head_shape)
    grad_probs = jnp.einsum("shd,thd->hst", grad_attn, v, preferred_element_type=F32)
    shared = jnp.sum(probs * grad_probs, axis=-1, keepdims=True)
    grad_scores = (probs * (grad_probs - shared)).astype(BF16)
    grad_qrot = jnp.einsum("hst,thd->shd", grad_scores, k, preferred_element_type=F32)
    grad_krot = jnp.einsum("hst,shd->thd", grad_scores, q, preferred_element_type=F32)
    grad_values = jnp.einsum("hst,shd->thd", probs_low, grad_attn, preferred_element_type=F32)
    grad_query = rotate(grad_qrot * scale, cosine, -sine).reshape(rows, -1)
    grad_key = rotate(grad_krot, cosine, -sine).reshape(rows, -1)
    gp_query = adapters("query", first_in, grad_query, values["query"])
    gp_key = adapters("key", first_in, grad_key, values["key"])
    gp_value = adapters("value", first_in, grad_values.reshape(rows, -1), values["value"])
    grad_first = mp_sum(back("query", gp_query)[0] + back("key", gp_key)[0] + back("value", gp_value)[0])
    w1 = grad_first * gain_attn
    grad_tokens = (grad_hidden + inv1 * (w1 - u1 * jnp.mean(w1 * u1, axis=-1, keepdims=True))).astype(BF16)

    early = reduce_grads(
        [grad_right["gate"], grad_right["up"], grad_left["down"]],
        [grad_left["gate"], grad_left["up"], grad_right["down"]],
        [grad_mag["gate"], grad_mag["up"], grad_mag["down"]],
    )
    late = reduce_grads(
        [grad_right["query"], grad_right["key"], grad_right["value"], grad_left["output"]],
        [grad_left["query"], grad_left["key"], grad_left["value"], grad_right["output"]],
        [grad_mag["query"], grad_mag["key"], grad_mag["value"], grad_mag["output"]],
    )
    (right_g, right_u, left_d), (left_g, left_u, right_d), (mag_g, mag_u, mag_d) = early
    (right_q, right_k, right_v, left_o), (left_q, left_k, left_v, right_o), (mag_q, mag_k, mag_v, mag_o) = late
    return (
        layer_out, grad_tokens,
        left_q.T, right_q, mag_q,
        left_k.T, right_k, mag_k,
        left_v.T, right_v, mag_v,
        left_o.T, right_o, mag_o,
        left_g.T, right_g, mag_g,
        left_u.T, right_u, mag_u,
        left_d.T, right_d, mag_d,
    )


def solution(mesh):
    fine = Mesh(mesh.devices.reshape(4, 2, 4, 2, 2), ("y", "xh", "z", "core", "mp"))
    col, row, vec, rep = P(None, "mp"), P("mp", None), P("mp"), P()
    tok = P(DP, None)
    split, merged = (rep, col, vec), (row, rep, rep)
    return jax.shard_map(
        body,
        mesh=fine,
        in_specs=(tok, P(DP), tok, rep, rep, col, col, col, row, col, col, P(("mp",) + DP, None))
        + split * 3 + merged + split * 2 + merged,
        out_specs=(tok, tok) + split * 3 + merged + split * 2 + merged,
        check_vma=False,
    )
```

```python
import functools
import jax
import jax.numpy as jnp
import numpy as np
from jax import lax
from jax.experimental import pallas as pl
from jax.experimental.pallas import tpu as pltpu
from jax.sharding import Mesh, PartitionSpec as P

HEAD_DIM = 128
RANK = 16
RATIO = 2.0
EPSILON = 1e-05
F32 = jnp.float32
BF16 = jnp.bfloat16
DP = ("y", "xh", "z", "core")
GROUP = ("xh", "core", "mp")
ANY = pl.BlockSpec(memory_space=pl.ANY)
MIB = 1024 * 1024


def dot(a, b, dims=((1,), (0,))):
    return lax.dot_general(a.astype(BF16), b.astype(BF16), (dims, ((), ())), preferred_element_type=F32)


def dot_nt(a, b):
    return dot(a, b, ((1,), (1,)))


def dot_tn(a, b):
    return dot(a, b, ((0,), (0,)))


def col_sum(v):
    return jnp.sum(v, axis=0, keepdims=True)


def row_chunks(n, size=64):
    return [slice(r, r + size) for r in range(0, n, size)]


def shape(dims, dtype=F32):
    return jax.ShapeDtypeStruct(dims, dtype)


def params(mib):
    return pltpu.CompilerParams(vmem_limit_bytes=mib * MIB)


def cols(rows, width=256, first=0):
    return pl.BlockSpec((rows, width), lambda j: (0, first + j))


def one(rows, width, index):
    return pl.BlockSpec((rows, width), lambda j: (0, index), pipeline_mode=pl.Buffered(1))


def rows_of(height, width):
    return pl.BlockSpec((height, width), lambda j: (j, 0))


def full(x):
    dims = x.shape
    return pl.BlockSpec(dims, lambda j: (0,) * len(dims), pipeline_mode=pl.Buffered(1))


def call(kernel, grid, ins, outs, scratch, name, work, traffic, mib=60):
    return pl.pallas_call(
        kernel,
        grid=(grid,),
        in_specs=[full(x) if block is None else block for x, block in ins],
        out_specs=[pl.BlockSpec(x.shape, lambda j, r=len(x.shape): (0,) * r) if block is None else block for x, block in outs],
        out_shape=[x for x, _ in outs],
        scratch_shapes=scratch,
        compiler_params=params(mib),
        cost_estimate=cost(work, traffic),
        name=name,
    )(*[x for x, _ in ins])


def cost(flops, size):
    return pl.CostEstimate(flops=int(flops), bytes_accessed=int(size), transcendentals=0)


def square_sum(w_ref):
    depth, width = w_ref.shape
    if depth % 128:
        v = w_ref[...].astype(F32)
        return col_sum(v * v)
    squares = jnp.zeros((8, width), F32)
    for r in range(0, depth, 128):
        chunk = w_ref[r : r + 128, :].astype(F32)
        squares = squares + jnp.sum((chunk * chunk).reshape(16, 8, width), axis=0)
    return col_sum(squares)


def stats_kernel(whole, parts, *refs):
    ins, outs = refs[: 4 * whole + 3 * parts], refs[4 * whole + 3 * parts :]

    def of(w_ref, left_ref, right_ref):
        left, right = left_ref[...], right_ref[...]
        lw = dot(left, w_ref[...])
        ld = lw + RATIO * dot(dot_nt(left, left), right)
        return square_sum(w_ref) + RATIO * col_sum(right * (lw + ld)), ld

    for i in range(whole):
        w_ref, left_ref, right_ref, mag_ref = ins[4 * i : 4 * i + 4]
        fac_ref, isq_ref, ld_ref = outs[3 * i : 3 * i + 3]
        total, ld_ref[...] = of(w_ref, left_ref, right_ref)
        isq_ref[...] = 1.0 / total
        fac_ref[...] = mag_ref[...] * lax.rsqrt(total)
    for i in range(parts):
        at, to = 4 * whole + 3 * i, 3 * whole + 2 * i
        outs[to][...], outs[to + 1][...] = of(*ins[at : at + 3])


def stats(whole, parts, steps):
    ins, outs, size = [], [], 0
    for w, left, right, mag, first in whole:
        width = w.shape[1] // steps
        ins += [(w, cols(w.shape[0], width)), (left, None), (right, cols(RANK, width)), (mag, cols(1, width, first))]
        outs += [(shape((1, w.shape[1])), cols(1, width))] * 2 + [(shape((RANK, w.shape[1])), cols(RANK, width))]
        size += w.size
    for w, left, right in parts:
        width = w.shape[1] // steps
        ins += [(w, cols(w.shape[0], width)), (left, None), (right, cols(RANK, width))]
        outs += [(shape((1, w.shape[1])), cols(1, width)), (shape((RANK, w.shape[1])), cols(RANK, width))]
        size += w.size
    flat = call(functools.partial(stats_kernel, len(whole), len(parts)), steps, ins, outs, [], "stats", 2 * RANK * size, 2 * size)
    at = 3 * len(whole)
    return [flat[3 * i : 3 * i + 3] for i in range(len(whole))] + [flat[at + 2 * i : at + 2 * i + 2] for i in range(len(parts))]


def unit_rows(v):
    return lax.rsqrt(jnp.mean(v * v, axis=-1, keepdims=True) + EPSILON)


def rotate(v, cosine, sine):
    return v * cosine + pltpu.roll(v, HEAD_DIM // 2, 1) * sine


def attend_kernel(
    length_ref, x_ref, gain_ref, lq_ref, lk_ref, lv_ref, cos_ref, sin_ref, right_o_ref,
    wq_ref, wk_ref, wv_ref, wo_ref, rq_ref, rk_ref, rv_ref, fq_ref, fk_ref, fv_ref, left_o_ref,
    first_ref, aq_ref, ak_ref, av_ref, part_ref, yo_ref, q_ref, k_ref, v_ref, probs_ref, mix_ref,
    acc, yacc,
):
    j = pl.program_id(0)
    n = x_ref.shape[0]

    @pl.when(j == 0)
    def _():
        for r in row_chunks(n):
            x = x_ref[r, :].astype(F32)
            first_ref[r, :] = (x * unit_rows(x) * gain_ref[...]).astype(BF16)
        first = first_ref[...]
        for left, out in ((lq_ref, aq_ref), (lk_ref, ak_ref), (lv_ref, av_ref)):
            out[...] = dot_nt(first, left[...]).astype(BF16)
        acc[...] = jnp.zeros_like(acc)
        yacc[...] = jnp.zeros_like(yacc)

    first = first_ref[...]

    def project(w, a, right, fac):
        return (dot(first, w[...]) + RATIO * dot(a[...], right[...])) * fac[...]

    vq = project(wq_ref, aq_ref, rq_ref, fq_ref)
    vk = project(wk_ref, ak_ref, rk_ref, fk_ref)
    v_ref[...] = project(wv_ref, av_ref, rv_ref, fv_ref).astype(BF16)
    cosine, sine = cos_ref[...], sin_ref[...]
    row = lax.broadcasted_iota(jnp.int32, (n, n), 0)
    col = lax.broadcasted_iota(jnp.int32, (n, n), 1)
    allowed = (col <= row) & (col < length_ref[0])
    for h in range(2):
        lanes = slice(h * HEAD_DIM, (h + 1) * HEAD_DIM)
        q = (rotate(vq[:, lanes], cosine, sine) * HEAD_DIM**-0.5).astype(BF16)
        k = rotate(vk[:, lanes], cosine, sine).astype(BF16)
        q_ref[:, lanes] = q
        k_ref[:, lanes] = k
        scores = jnp.where(allowed, dot_nt(q, k), -1e30)
        e = jnp.exp(scores - jnp.max(scores, axis=-1, keepdims=True))
        probs = (e * (1.0 / jnp.sum(e, axis=-1, keepdims=True))).astype(BF16)
        probs_ref[h] = probs
        mix_ref[:, lanes] = dot(probs, v_ref[:, lanes]).astype(BF16)
    mix = mix_ref[...]
    acc[...] += dot(mix, wo_ref[...])
    yacc[...] += dot_nt(mix, left_o_ref[...])

    @pl.when(j == pl.num_programs(0) - 1)
    def _():
        y = yacc[...].astype(BF16)
        yo_ref[...] = y
        for r in row_chunks(n):
            part_ref[r, :] = (acc[r, :] + RATIO * dot(y[r, :], right_o_ref[...])).astype(BF16)


def attend(length, tokens, vectors, lefts, cosine, sine, right_o, weights, rights, facs, left_o):
    n, d = tokens.shape
    h = weights[0].shape[1]
    wq, wk, wv, wo = weights
    ins = [(length, pl.BlockSpec(memory_space=pltpu.SMEM))]
    ins += [(tokens, None), (vectors, one(1, d, 0))] + [(x, None) for x in (*lefts, cosine, sine, right_o)]
    ins += [(wq, cols(d)), (wk, cols(d)), (wv, cols(d)), (wo, rows_of(256, d))]
    ins += [(x, cols(RANK)) for x in rights] + [(x, cols(1)) for x in facs] + [(left_o, cols(RANK))]
    outs = [(shape((n, d), BF16), None)] + [(shape((n, RANK), BF16), None)] * 3 + [(shape((n, d), BF16), None), (shape((n, RANK), BF16), None)]
    outs += [(shape((n, h), BF16), cols(n))] * 3
    outs += [(shape((h // HEAD_DIM, n, n), BF16), pl.BlockSpec((2, n, n), lambda j: (j, 0, 0))), (shape((n, h), BF16), cols(n))]
    scratch = [pltpu.VMEM((n, d), F32), pltpu.VMEM((n, RANK), F32)]
    return call(attend_kernel, h // 256, ins, outs, scratch, "attend", 8 * n * d * h, 8 * d * h)


def gate_kernel(
    x_ref, own_ref, got_ref, fo_ref, gain_ref, lg_ref, lu_ref, rg_ref, ru_ref, fg_ref, fu_ref, wg_ref, wu_ref,
    second_ref, ag_ref, au_ref, gv_ref, uv_ref,
    wg, wu, sems,
):
    j = pl.program_id(0)

    def copies(i):
        lanes = pl.ds(pl.multiple_of(i * 256, 256), 256)
        return [pltpu.make_async_copy(src.at[:, lanes], dst.at[:, lanes], sems.at[s, i]) for s, (src, dst) in enumerate(((wg_ref, wg), (wu_ref, wu)))]

    @pl.when(j == 0)
    def _():
        for i in range(wg_ref.shape[1] // 256):
            for c in copies(i):
                c.start()
        for r in row_chunks(x_ref.shape[0]):
            total = own_ref[r, :].astype(F32) + got_ref[r, :].astype(F32)
            hidden = x_ref[r, :].astype(F32) + total * fo_ref[...]
            second_ref[r, :] = (hidden * unit_rows(hidden) * gain_ref[...]).astype(BF16)
        second = second_ref[...]
        ag_ref[...] = dot_nt(second, lg_ref[...]).astype(BF16)
        au_ref[...] = dot_nt(second, lu_ref[...]).astype(BF16)

    for c in copies(j):
        c.wait()
    lanes = pl.ds(pl.multiple_of(j * 256, 256), 256)
    second = second_ref[...]
    gv_ref[...] = (dot(second, wg[:, lanes]) + RATIO * dot(ag_ref[...], rg_ref[...])) * fg_ref[...]
    uv_ref[...] = (dot(second, wu[:, lanes]) + RATIO * dot(au_ref[...], ru_ref[...])) * fu_ref[...]


def gate_up(tokens, own, got, fac_o, vectors, lefts, weights, rights, facs):
    n, d = tokens.shape
    f = weights[0].shape[1]
    ins = [(x, None) for x in (tokens, own, got, fac_o)] + [(vectors, one(1, d, 1))] + [(x, None) for x in lefts]
    ins += [(x, cols(RANK)) for x in rights] + [(x, cols(1)) for x in facs] + [(w, ANY) for w in weights]
    outs = [(shape((n, d), BF16), None)] + [(shape((n, RANK), BF16), None)] * 2 + [(shape((n, f)), cols(n))] * 2
    scratch = [pltpu.VMEM((d, f), BF16)] * 2 + [pltpu.SemaphoreType.DMA((2, f // 256))]
    return call(gate_kernel, f // 256, ins, outs, scratch, "gate_up", 4 * n * d * f, 4 * d * f)


def piece_of(shard):
    y, xh, zc = shard // 16, shard // 8 % 2, shard % 8
    return y * 8 + zc, xh


def ffn_kernel(
    raw_ref, cot_ref, md_ref, rd_ref, second_ref, ag_ref, au_ref, lg_ref, lu_ref,
    wg_ref, wu_ref, ldt_ref, gv_ref, uv_ref, rg_ref, ru_ref, fg_ref, fu_ref, ig_ref, iu_ref, dg_ref, du_ref, mg_ref, mu_ref,
    pd_ref, ps_ref, sd_ref, dd_ref, td_ref, fd_ref, id_ref, loc_ref, mix_ref, wd_ref, tl_ref,
    raw, wd, sems, gpd, zd, accd, accs, yd, gd, zg, zu, ng, nu, sg, su, vec,
):
    j = pl.program_id(0)
    n, d = cot_ref.shape
    f = wd.shape[0]

    @pl.when(j == 0)
    def _():
        pieces = raw_ref.shape[0]
        copies = [pltpu.make_async_copy(raw_ref.at[pl.ds(c, 4)], raw.at[pl.ds(c, 4)], sems.at[c // 4]) for c in range(0, pieces, 4)]
        for copy in copies:
            copy.start()
        for ref in (accd, accs, yd, gd, zg, zu, ng, nu, sg, su, vec):
            ref[...] = jnp.zeros_like(ref)
        shards, height = 2 * pieces, f // (2 * pieces)
        waited = set()
        totals = jnp.zeros((8, d), F32)
        for c in range(0, shards, 4):
            places = [piece_of(c + i) for i in range(4)]
            for i in sorted({p // 4 for p, _ in places} - waited):
                copies[i].wait()
                waited.add(i)
            wd[c * height : (c + 4) * height, :] = jnp.concatenate([raw[p, x, :height, :] for p, x in places], axis=0)
            for p, x in places:
                if x == 0:
                    totals = totals + raw[p, 0, 40:48, :].astype(F32)
        total = totals[4:5, :] + totals[5:6, :]
        id_ref[...] = 1.0 / total
        fd_ref[...] = md_ref[...] * lax.rsqrt(total)
        for r in row_chunks(n):
            gpd[r, :] = (cot_ref[r, :].astype(F32) * fd_ref[...]).astype(BF16)
        zd[...] = dot_nt(gpd[...], rd_ref[...]).astype(BF16)

    block = wd[pl.ds(pl.multiple_of(j * 256, 256), 256), :]
    wd_ref[...] = block
    ldt = ldt_ref[...].astype(BF16)
    grad_act = dot_nt(gpd[...], block) + RATIO * dot(zd[...], ldt)
    gv, uv = gv_ref[...], uv_ref[...]
    sig = 1.0 / (1.0 + jnp.exp(-gv))
    silu = gv * sig
    act = (silu * uv).astype(BF16)
    accd[...] += dot(jnp.concatenate([act, ldt], axis=0), block)
    yd[...] += dot_nt(act, ldt)
    gd[...] += dot_nt(ldt, ldt)
    tl_ref[...] = dot_tn(zd[...], act)
    grad_gate = grad_act * uv * (sig + silu * (1.0 - sig))
    grad_up = grad_act * silu
    for i, (grad, val, a, w, right, fac, isq, ld, mag, z, nr_acc, m_acc) in enumerate((
        (grad_gate, gv, ag_ref, wg_ref, rg_ref, fg_ref, ig_ref, dg_ref, mg_ref, zg, ng, sg),
        (grad_up, uv, au_ref, wu_ref, ru_ref, fu_ref, iu_ref, du_ref, mu_ref, zu, nu, su),
    )):
        s = col_sum(grad * val)
        vec[pl.ds(j, 1), i * 256 : (i + 1) * 256] = s / mag[...]
        ncoef = -s * isq[...]
        gp = (grad * fac[...]).astype(BF16)
        nr = (ncoef * right[...]).astype(BF16)
        both = dot_nt(jnp.concatenate([gp, nr], axis=0), w[...])
        accs[...] += both[:n]
        nr_acc[...] += both[n:]
        z[...] += dot_nt(gp, right[...])
        m_acc[...] += dot_nt(nr, right[...])
        loc_ref[:, pl.ds(pl.multiple_of(i * f + j * 256, 256), 256)] = (RATIO * (dot_tn(a[...], gp) + ld[...] * ncoef)).astype(BF16)

    @pl.when(j == pl.num_programs(0) - 1)
    def _():
        zgl, zul, ydl = zg[...].astype(BF16), zu[...].astype(BF16), yd[...].astype(BF16)
        sums = jnp.zeros((1, d), F32)
        for r in row_chunks(n):
            ps_ref[r, :] = (accs[r, :] + RATIO * (dot(zgl[r, :], lg_ref[...]) + dot(zul[r, :], lu_ref[...]))).astype(BF16)
            pd = (accd[r, :] + RATIO * dot(ydl[r, :], rd_ref[...])).astype(BF16)
            pd_ref[r, :] = pd
            sums = sums + col_sum(cot_ref[r, :].astype(F32) * pd.astype(F32))
        sd_ref[...] = sums * fd_ref[...]
        dd_ref[...] = accd[n:, :] + RATIO * dot(gd[...], rd_ref[...])
        td_ref[...] = dot_tn(ydl, gpd[...])
        loc_ref[:, 2 * f :] = vec[...].astype(BF16)
        mix_ref[:, :d] = (RATIO * (dot_tn(zgl, second_ref[...]) + ng[...] + RATIO * dot(sg[...], lg_ref[...]))).astype(BF16)
        mix_ref[:, d:] = (RATIO * (dot_tn(zul, second_ref[...]) + nu[...] + RATIO * dot(su[...], lu_ref[...]))).astype(BF16)


def ffn(raw, cot, vectors, right_d, second, als, lefts, weights, left_dt, vals, rights, facs, isqs, lds, firsts):
    n, d = cot.shape
    f = weights[0].shape[1]
    small = pltpu.VMEM((n, RANK), F32)
    square = pltpu.VMEM((RANK, RANK), F32)
    wide = pltpu.VMEM((RANK, d), F32)
    ins = [(raw, ANY), (cot, None), (vectors, one(1, d, 3))] + [(x, None) for x in (right_d, second, *als, *lefts)]
    ins += [(w, cols(d)) for w in weights] + [(left_dt, cols(RANK))] + [(x, cols(n)) for x in vals]
    ins += [(x, cols(RANK)) for x in rights] + [(x, cols(1)) for x in (*facs, *isqs)] + [(x, cols(RANK)) for x in lds]
    ins += [(vectors, cols(1, 256, first)) for first in firsts]
    outs = [(shape((n, d), BF16), None)] * 2 + [(shape((1, d)), None)] + [(shape((RANK, d)), None)] * 2 + [(shape((1, d)), None)] * 2
    outs += [(shape((RANK, 2 * f + 512), BF16), None), (shape((RANK, 2 * d), BF16), None)]
    outs += [(shape((f, d), BF16), rows_of(256, d)), (shape((RANK, f)), cols(RANK))]
    scratch = [
        pltpu.VMEM(raw.shape, BF16), pltpu.VMEM((f, d), BF16), pltpu.SemaphoreType.DMA((raw.shape[0] // 4,)),
        pltpu.VMEM((n, d), BF16), pltpu.VMEM((n, RANK), BF16), pltpu.VMEM((n + RANK, d), F32), pltpu.VMEM((n, d), F32),
        small, square, small, small, wide, wide, square, square, pltpu.VMEM((RANK, 512), F32),
    ]
    return call(ffn_kernel, f // 256, ins, outs, scratch, "ffn", 8 * n * d * f, 6 * d * f)


def down_kernel(s0_ref, s1_ref, isq_ref, mag_ref, rd_ref, dd_ref, td_ref, wd_ref, ldt_ref, tl_ref, loc_ref, mix_ref, nr, m):
    j = pl.program_id(0)
    f = loc_ref.shape[1] - 256
    width = ldt_ref.shape[1]

    @pl.when(j == 0)
    def _():
        s = s0_ref[...] + s1_ref[...]
        ncoef = -s * isq_ref[...]
        nr[...] = (ncoef * rd_ref[...]).astype(BF16)
        m[...] = dot_nt(nr[...], rd_ref[...])
        mix_ref[...] = (RATIO * (td_ref[...] + dd_ref[...] * ncoef)).astype(BF16)
        v = s / mag_ref[...]
        rows = [v[:, i * 256 : (i + 1) * 256] for i in range(v.shape[1] // 256)]
        rows += [jnp.zeros((RANK - len(rows), 256), F32)]
        loc_ref[:, f:] = jnp.concatenate(rows, axis=0).astype(BF16)

    out = RATIO * (tl_ref[...] + dot_nt(nr[...], wd_ref[...]) + RATIO * dot(m[...], ldt_ref[...]))
    loc_ref[:, pl.ds(pl.multiple_of(j * width, 128), width)] = out.astype(BF16)


def down_correction(s0, s1, isq, vectors, right_d, dd, td, w_down, left_dt, tl):
    f, d = w_down.shape
    ins = [(s0, None), (s1, None), (isq, None), (vectors, one(1, d, 3))] + [(x, None) for x in (right_d, dd, td)]
    ins += [(w_down, rows_of(1408, d)), (left_dt, cols(RANK, 1408)), (tl, cols(RANK, 1408))]
    outs = [(shape((RANK, f + 256), BF16), None), (shape((RANK, d), BF16), None)]
    scratch = [pltpu.VMEM((RANK, d), BF16), pltpu.VMEM((RANK, RANK), F32)]
    return call(down_kernel, f // 1408, ins, outs, scratch, "down_correction", 2 * RANK * d * f, 2 * d * f)


def back_kernel(
    own_ref, got_ref, own_o_ref, got_o_ref, x_ref, cot_ref, gain_ref, mo_ref, fo_ref, io_ref, ro_ref, do_ref, yo_ref, first_ref,
    aq_ref, ak_ref, av_ref, lq_ref, lk_ref, lv_ref, cos_ref, sin_ref,
    wq_ref, wk_ref, wv_ref, wo_ref, rq_ref, rk_ref, rv_ref, fq_ref, fk_ref, fv_ref, iq_ref, ik_ref, iv_ref,
    dq_ref, dk_ref, dv_ref, mq_ref, mk_ref, mv_ref, left_o_ref, q_ref, k_ref, v_ref, probs_ref, mix_ref,
    pf_ref, gh_ref, loc_ref, mixed_ref,
    gpo, zo, mo, acc, zq, zk, zv, nq, nk, nv, sq, sk, sv, vec,
):
    j = pl.program_id(0)
    n, d = x_ref.shape

    @pl.when(j == 0)
    def _():
        sums = jnp.zeros((1, d), F32)
        for r in row_chunks(n):
            value = (own_o_ref[r, :].astype(F32) + got_o_ref[r, :].astype(F32)) * fo_ref[...]
            hidden = x_ref[r, :].astype(F32) + value
            inverse = unit_rows(hidden)
            unit = hidden * inverse
            w2 = (own_ref[r, :].astype(F32) + got_ref[r, :].astype(F32)) * gain_ref[...]
            grad = cot_ref[r, :].astype(F32) + inverse * (w2 - unit * jnp.mean(w2 * unit, axis=-1, keepdims=True))
            gh_ref[r, :] = grad
            gpo[r, :] = (grad * fo_ref[...]).astype(BF16)
            sums = sums + col_sum(grad * value)
        vec[...] = jnp.zeros_like(vec)
        v = sums / mo_ref[...]
        for i in range(d // 256):
            vec[i : i + 1, 256:] = v[:, i * 256 : (i + 1) * 256]
        ncoef = -sums * io_ref[...]
        nr = (ncoef * ro_ref[...]).astype(BF16)
        gpo[n:, :] = nr
        mo[...] = dot_nt(nr, ro_ref[...])
        zo[...] = dot_nt(gpo[:n, :], ro_ref[...]).astype(BF16)
        mixed_ref[:, 3 * d :] = (RATIO * (dot_tn(yo_ref[...], gpo[:n, :]) + do_ref[...] * ncoef)).astype(BF16)
        for ref in (acc, zq, zk, zv, nq, nk, nv, sq, sk, sv):
            ref[...] = jnp.zeros_like(ref)

    span = (loc_ref.shape[1] - 1024) // 4

    def place(i):
        return pl.ds(pl.multiple_of(i * span + j * 256, 256), 256)

    left_o = left_o_ref[...].astype(BF16)
    both = dot_nt(gpo[...], wo_ref[...])
    grad_attn = (both[:n] + RATIO * dot(zo[...], left_o)).astype(BF16)
    loc_ref[:, place(3)] = (RATIO * (dot_tn(zo[...], mix_ref[...]) + both[n:] + RATIO * dot(mo[...], left_o))).astype(BF16)
    cosine, sine = cos_ref[...], -sin_ref[...]
    scale = HEAD_DIM**-0.5
    parts = ([], [], [])
    for h in range(2):
        lanes = slice(h * HEAD_DIM, (h + 1) * HEAD_DIM)
        ga, q, k, v, probs = grad_attn[:, lanes], q_ref[:, lanes], k_ref[:, lanes], v_ref[:, lanes], probs_ref[h]
        p = probs.astype(F32)
        gprobs = dot_nt(ga, v)
        gscores = (p * (gprobs - jnp.sum(p * gprobs, axis=-1, keepdims=True))).astype(BF16)
        gq = rotate(dot(gscores, k), cosine, sine) * scale
        gk = rotate(dot_tn(gscores, q), cosine, sine)
        gv = dot_tn(probs, ga)
        parts[0].append((gq, col_sum(gq * rotate(q.astype(F32), cosine, sine)) * (1.0 / scale)))
        parts[1].append((gk, col_sum(gk * rotate(k.astype(F32), cosine, sine))))
        parts[2].append((gv, col_sum(gv * v.astype(F32))))
    for i, (part, a, w, right, fac, isq, ld, mag, z, nr_acc, m_acc) in enumerate((
        (parts[0], aq_ref, wq_ref, rq_ref, fq_ref, iq_ref, dq_ref, mq_ref, zq, nq, sq),
        (parts[1], ak_ref, wk_ref, rk_ref, fk_ref, ik_ref, dk_ref, mk_ref, zk, nk, sk),
        (parts[2], av_ref, wv_ref, rv_ref, fv_ref, iv_ref, dv_ref, mv_ref, zv, nv, sv),
    )):
        grad = jnp.concatenate([p[0] for p in part], axis=1)
        s = jnp.concatenate([p[1] for p in part], axis=1)
        vec[pl.ds(4 * i + j, 1), :256] = s / mag[...]
        ncoef = -s * isq[...]
        gp = (grad * fac[...]).astype(BF16)
        nr = (ncoef * right[...]).astype(BF16)
        both = dot_nt(jnp.concatenate([gp, nr], axis=0), w[...])
        acc[...] += both[:n]
        nr_acc[...] += both[n:]
        z[...] += dot_nt(gp, right[...])
        m_acc[...] += dot_nt(nr, right[...])
        loc_ref[:, place(i)] = (RATIO * (dot_tn(a[...], gp) + ld[...] * ncoef)).astype(BF16)

    @pl.when(j == pl.num_programs(0) - 1)
    def _():
        zs = [z[...].astype(BF16) for z in (zq, zk, zv)]
        lefts = [lq_ref[...].astype(BF16), lk_ref[...].astype(BF16), lv_ref[...].astype(BF16)]
        for r in row_chunks(n):
            low = sum(dot(z[r, :], left) for z, left in zip(zs, lefts))
            pf_ref[r, :] = (acc[r, :] + RATIO * low).astype(BF16)
        for i, (z, nr_acc, m_acc, left) in enumerate(zip(zs, (nq, nk, nv), (sq, sk, sv), lefts)):
            out = RATIO * (dot_tn(z, first_ref[...]) + nr_acc[...] + RATIO * dot(m_acc[...], left))
            mixed_ref[:, i * d : (i + 1) * d] = out.astype(BF16)
        loc_ref[:, 4 * span :] = jnp.concatenate([vec[...], jnp.zeros((RANK, 512), F32)], axis=1).astype(BF16)


def back(
    own, got, own_o, got_o, tokens, cot, vectors, fac_o, isq_o, right_o, ld_o, yo, first, als, lefts, cosine, sine,
    weights, rights, facs, isqs, lds, firsts, left_o, qkv, probs, mix,
):
    n, d = tokens.shape
    h = weights[0].shape[1]
    wq, wk, wv, wo = weights
    small = pltpu.VMEM((n, RANK), F32)
    wide = pltpu.VMEM((RANK, d), F32)
    square = pltpu.VMEM((RANK, RANK), F32)
    ins = [(x, None) for x in (own, got, own_o, got_o, tokens, cot)] + [(vectors, one(1, d, 1)), (vectors, one(1, d, 2))]
    ins += [(x, None) for x in (fac_o, isq_o, right_o, ld_o, yo, first, *als, *lefts, cosine, sine)]
    ins += [(wq, cols(d)), (wk, cols(d)), (wv, cols(d)), (wo, rows_of(256, d))]
    ins += [(x, cols(RANK)) for x in rights] + [(x, cols(1)) for x in (*facs, *isqs)] + [(x, cols(RANK)) for x in lds]
    ins += [(vectors, cols(1, 256, i)) for i in firsts]
    ins += [(left_o, cols(RANK))] + [(x, cols(n)) for x in qkv] + [(probs, pl.BlockSpec((2, n, n), lambda j: (j, 0, 0))), (mix, cols(n))]
    outs = [(shape((n, d), BF16), None), (shape((n, d)), None), (shape((RANK, 4 * h + 1024), BF16), None), (shape((RANK, 4 * d), BF16), None)]
    scratch = [pltpu.VMEM((n + RANK, d), BF16), pltpu.VMEM((n, RANK), BF16), square, pltpu.VMEM((n, d), F32)]
    scratch += [small] * 3 + [wide] * 3 + [square] * 3 + [pltpu.VMEM((RANK, 512), F32)]
    return call(back_kernel, h // 256, ins, outs, scratch, "back", 8 * n * d * h, 8 * d * h)


def layer_kernel(x_ref, own_o_ref, got_o_ref, fo_ref, own_ref, got_ref, fd_ref, out_ref):
    hidden = x_ref[...].astype(F32) + (own_o_ref[...].astype(F32) + got_o_ref[...].astype(F32)) * fo_ref[...]
    out_ref[...] = (hidden + (own_ref[...].astype(F32) + got_ref[...].astype(F32)) * fd_ref[...]).astype(BF16)


def layer_end(tokens, own_o, got_o, fac_o, own, got, fac_d):
    n, d = tokens.shape
    block = rows_of(128, d)
    ins = [(tokens, block), (own_o, block), (got_o, block), (fac_o, None), (own, block), (got, block), (fac_d, None)]
    return call(layer_kernel, n // 128, ins, [(shape((n, d), BF16), block)], [], "layer_end", 6 * n * d, 12 * n * d)[0]


def token_kernel(x_ref, gh_ref, own_ref, got_ref, gain_ref, out_ref):
    x = x_ref[...].astype(F32)
    inverse = unit_rows(x)
    unit = x * inverse
    w1 = (own_ref[...].astype(F32) + got_ref[...].astype(F32)) * gain_ref[...]
    out_ref[...] = (gh_ref[...] + inverse * (w1 - unit * jnp.mean(w1 * unit, axis=-1, keepdims=True))).astype(BF16)


def token_end(tokens, grad_hidden, own, got, vectors):
    n, d = tokens.shape
    block = rows_of(128, d)
    ins = [(tokens, block), (grad_hidden, block), (own, block), (got, block), (vectors, one(1, d, 0))]
    return call(token_kernel, n // 128, ins, [(shape((n, d), BF16), block)], [], "token_end", 10 * n * d, 12 * n * d)[0]


def shard_kernel(w_ref, left_ref, right_ref, out_ref):
    left, right = left_ref[...], right_ref[...]
    lw = dot(left, w_ref[...])
    ld = lw + RATIO * dot(dot_nt(left, left), right)
    out_ref[...] = square_sum(w_ref) + RATIO * col_sum(right * (lw + ld))


def shard_stats(w, left, right):
    return call(shard_kernel, 1, [(w, None), (left, None), (right, None)], [(shape((1, w.shape[1])), None)], [], "shard_stats", w.size, w.size)[0]


def bundle_kernel(xh_ref, own_ref, far_ref, s0_ref, s1_ref, s2_ref, s3_ref, out_ref):
    rows, d = own_ref.shape
    total = (s0_ref[...] + s1_ref[...]) + (s2_ref[...] + s3_ref[...])
    high = total.astype(BF16).astype(F32)
    zero = jnp.zeros((1, d), F32)
    for side in range(2):
        @pl.when(xh_ref[0] == side)
        def _():
            for at, ref in ((side, own_ref), (1 - side, far_ref)):
                tail = [high, total - high, zero, zero] if at == 0 else [zero] * 4
                out_ref[at] = jnp.concatenate([ref[...].astype(F32)] + tail, axis=0).astype(BF16)


def bundle(xh, own, far, sums):
    rows, d = own.shape
    ins = [(xh, pl.BlockSpec(memory_space=pltpu.SMEM)), (own, None), (far, None)] + [(x, None) for x in sums]
    return call(bundle_kernel, 1, ins, [(shape((2, rows + 4, d), BF16), None)], [], "bundle", own.size, 4 * own.size)[0]


def halves_kernel(count, core_ref, *refs):
    ins, (keep_ref, send_ref) = refs[:count], refs[count:]
    at = 0
    for ref in ins:
        w = ref.shape[1] // 2
        for side in range(2):
            @pl.when(core_ref[0] == side)
            def _(at=at, w=w, ref=ref, side=side):
                keep_ref[:, at : at + w] = ref[:, side * w : (side + 1) * w]
                send_ref[:, at : at + w] = ref[:, (1 - side) * w : (2 - side) * w]
        at += w


def halves(core, arrays):
    width = sum(x.shape[1] for x in arrays) // 2
    ins = [(core, pl.BlockSpec(memory_space=pltpu.SMEM))] + [(x, None) for x in arrays]
    outs = [(shape((RANK, width), BF16), None)] * 2
    return call(functools.partial(halves_kernel, len(arrays)), 1, ins, outs, [], "halves", RANK * width, 8 * RANK * width)


def quarters_kernel(widths, z_ref, keep_ref, got_ref, *refs):
    outs, total = refs[:4], refs[4]
    total[...] = (keep_ref[...].astype(F32) + got_ref[...].astype(F32)).astype(BF16)
    at = to = 0
    for w in widths:
        q = w // 8
        for k in range(4):
            start = at + (z_ref[0] ^ k) * q
            outs[k][:, to : to + q] = total[:, pl.ds(pl.multiple_of(start, 128), q)]
        at += w // 2
        to += q


def quarters(z, keep, got, widths):
    width = sum(widths) // 8
    ins = [(z, pl.BlockSpec(memory_space=pltpu.SMEM)), (keep, None), (got, None)]
    outs = [(shape((RANK, width), BF16), None)] * 4
    return call(functools.partial(quarters_kernel, widths), 1, ins, outs, [pltpu.VMEM(keep.shape, BF16)], "quarters", RANK * width, 32 * RANK * width)


def joined_kernel(widths, z_ref, *refs):
    ins, out_ref = refs[:4], refs[4]
    at = to = 0
    for w in widths:
        q = w // 8
        for k in range(4):
            out_ref[:, pl.ds(pl.multiple_of(to + (z_ref[0] ^ k) * q, 128), q)] = ins[k][:, at : at + q]
        at += q
        to += w // 2


def joined(z, parts, widths):
    ins = [(z, pl.BlockSpec(memory_space=pltpu.SMEM))] + [(x, None) for x in parts]
    width = sum(widths) // 2
    return call(functools.partial(joined_kernel, widths), 1, ins, [(shape((RANK, width), BF16), None)], [], "joined", RANK * width, 4 * RANK * width)[0]


def unpack_kernel(widths, places, core_ref, half_ref, got_ref, *refs):
    whole, outs = refs[-1], refs[:-1]
    at = to = 0
    for w in widths:
        h = w // 2
        for side in range(2):
            @pl.when(core_ref[0] == side)
            def _(at=at, to=to, h=h, side=side):
                whole[:, to + side * h : to + (side + 1) * h] = half_ref[:, at : at + h].astype(F32)
                whole[:, to + (1 - side) * h : to + (2 - side) * h] = got_ref[:, at : at + h].astype(F32)
        at += h
        to += w
    for out, (start, count, row) in zip(outs, places):
        if row is None:
            out[...] = whole[:, start : start + count]
        else:
            for i in range(count // 256):
                out[:, i * 256 : (i + 1) * 256] = whole[row + i : row + i + 1, start : start + 256]


def unpack(core, half, got, widths, places):
    ins = [(core, pl.BlockSpec(memory_space=pltpu.SMEM)), (half, None), (got, None)]
    outs = [(shape((RANK if row is None else 1, count)), None) for _, count, row in places]
    total = sum(widths)
    return call(functools.partial(unpack_kernel, widths, places), 1, ins, outs, [pltpu.VMEM((RANK, total), F32)], "unpack", RANK * total, 8 * RANK * total)


def swap(x, axis_name, k):
    n = lax.axis_size(axis_name)
    return lax.ppermute(x, axis_name, [(i, i ^ k) for i in range(n)])


def tree(parts):
    while len(parts) > 1:
        parts = [parts[i] + parts[i + 1] for i in range(0, len(parts), 2)]
    return parts[0]


def scatter_sum(arrays, core, z):
    widths = [x.shape[1] for x in arrays]
    keep, send = halves(core, arrays)
    own, *sends = quarters(z, keep, swap(send, "core", 1), widths)
    part = tree([own.astype(F32)] + [swap(x, "z", k + 1).astype(F32) for k, x in enumerate(sends)]).astype(BF16)
    return tree([part.astype(F32)] + [swap(part, "y", k).astype(F32) for k in range(1, 4)]).astype(BF16)


def rope_tables(span):
    half = HEAD_DIM // 2
    frequency = 10000.0 ** (-(np.arange(half, dtype=np.float64) * 2.0) / HEAD_DIM)
    angles = np.arange(span, dtype=np.float64)[:, None] * frequency[None, :]
    cosine, sine = np.cos(angles), np.sin(angles)
    return np.concatenate([cosine, cosine], 1).astype(np.float32), np.concatenate([-sine, sine], 1).astype(np.float32)


def after(x, *others):
    return lax.optimization_barrier((x,) + others)[0]


def body(
    tokens, lengths, cotangent, gain_attn, gain_ffn,
    w_query, w_key, w_value, w_output, w_gate, w_up, w_down,
    left_query, right_query, mag_query,
    left_key, right_key, mag_key,
    left_value, right_value, mag_value,
    left_output, right_output, mag_output,
    left_gate, right_gate, mag_gate,
    left_up, right_up, mag_up,
    left_down, right_down, mag_down,
):
    n, d = tokens.shape
    h, f = w_query.shape[1], w_gate.shape[1]
    cosine, sine = (jnp.asarray(t) for t in rope_tables(n))
    core, z, xh = (lax.axis_index(a).astype(jnp.int32)[None] for a in ("core", "z", "xh"))
    lq, lk, lv, lo, lg, lu, ld = (
        x.T for x in (left_query, left_key, left_value, left_output, left_gate, left_up, left_down)
    )
    shard = w_down.shape[0]
    left_shard = lax.dynamic_slice_in_dim(left_down, lax.axis_index(DP) * shard, shard, 0).T
    far = swap(w_down, "xh", 1)
    sq_d = shard_stats(w_down, left_shard, right_down)
    sums = [sq_d] + [swap(sq_d, ("xh", "mp"), k) for k in range(1, 4)]
    raw = lax.all_gather(bundle(xh, w_down, far, sums), ("y", "z", "core"), axis=0, tiled=False)

    vectors = jnp.concatenate(
        [gain_attn, gain_ffn, mag_output, mag_down, mag_query, mag_key, mag_value, mag_gate, mag_up]
    )[None, :]
    at_q, at_k, at_v = (4 * d // 256 + i * (h // 256) for i in range(3))
    at_g = at_v + h // 256
    at_u = at_g + f // 256
    (fq, iq, dq), (fk, ik, dk), (fv, iv, dv), (sq_o, do) = stats(
        [(w_query, lq, right_query, vectors, at_q), (w_key, lk, right_key, vectors, at_k), (w_value, lv, right_value, vectors, at_v)],
        [(w_output, lo, right_output)], 4,
    )
    sq_o = sq_o + swap(sq_o, "mp", 1)
    fo, io = mag_output[None, :] * lax.rsqrt(sq_o), 1.0 / sq_o

    first, aq, ak, av, part_o, yo, q, k, v, probs, mix = attend(
        lengths, tokens, vectors, (lq, lk, lv), cosine, sine, right_output,
        (w_query, w_key, w_value, w_output), (right_query, right_key, right_value), (fq, fk, fv), lo,
    )
    got_o = swap(part_o, "mp", 1)
    (fg, ig, dg), (fu, iu, du) = stats(
        [(w_gate, lg, right_gate, vectors, at_g), (w_up, lu, after(right_up, part_o), vectors, at_u)], [], 11
    )
    second, ag, au, gv, uv = gate_up(
        tokens, part_o, got_o, fo, vectors, (lg, lu), (w_gate, w_up), (right_gate, right_up), (fg, fu)
    )
    part_d, part_s, s_d, dd, td, fd, idn, loc_e, mix_e, down, tl = ffn(
        raw, cotangent, vectors, right_down, second, (ag, au), (lg, lu), (w_gate, w_up), ld, (gv, uv),
        (right_gate, right_up), (fg, fu), (ig, iu), (dg, du), (at_g, at_u),
    )
    got_s = swap(part_s, "mp", 1)
    far_s = swap(s_d, "mp", 1)
    loc_d, mix_d = down_correction(s_d, far_s, idn, vectors, right_down, dd, td, down, ld, tl)
    early = scatter_sum([loc_e, mix_e], core, z)
    got_d = swap(after(part_d, got_s, far_s), "mp", 1)
    part_f, grad_hidden, loc_l, mix_l = back(
        part_s, got_s, part_o, got_o, tokens, after(cotangent, early), vectors, fo, io, right_output, do, yo, first,
        (aq, ak, av), (lq, lk, lv), cosine, sine,
        (w_query, w_key, w_value, w_output), (right_query, right_key, right_value), (fq, fk, fv), (iq, ik, iv),
        (dq, dk, dv), (at_q, at_k, at_v), lo, (q, k, v), probs, mix,
    )
    part_f, loc_l, got_d = lax.optimization_barrier((part_f, loc_l, got_d))
    got_f = swap(part_f, "mp", 1)
    layer_out = layer_end(tokens, part_o, got_o, fo, part_d, got_d, fd)
    grad_tokens = token_end(tokens, grad_hidden, part_f, got_f, vectors)
    late = scatter_sum([loc_l, loc_d, mix_l, mix_d], core, z)
    we, wl, wd = loc_e.shape[1], loc_l.shape[1], loc_d.shape[1]
    cut_e, cut_l = we // 8, (wl + wd) // 8
    part = jnp.concatenate([early[:, :cut_e], late[:, :cut_l], early[:, cut_e:], late[:, cut_l:]], axis=1)
    part = after(part, got_f)
    mixed = part[:, cut_e + cut_l :]
    far, near, across = swap(part, "xh", 1), swap(mixed, "mp", 1), swap(mixed, ("xh", "mp"), 3)
    total = part.astype(F32) + far.astype(F32)
    other = near.astype(F32) + across.astype(F32)
    part = jnp.concatenate([total[:, : cut_e + cut_l], total[:, cut_e + cut_l :] + other], axis=1).astype(BF16)
    widths = [we, wl, wd, mix_e.shape[1], mix_l.shape[1], mix_d.shape[1]]
    half = joined(z, [part] + [swap(part, "z", k) for k in range(1, 4)], widths)
    vec_e, at_l = 2 * f, we
    vec_l, at_d = at_l + 4 * h, at_l + wl
    at_me = at_d + wd
    at_ml = at_me + 2 * d
    at_md = at_ml + 4 * d
    places = [
        (at_ml, d, None), (at_l, h, None), (vec_l, h, 0),
        (at_ml + d, d, None), (at_l + h, h, None), (vec_l, h, 4),
        (at_ml + 2 * d, d, None), (at_l + 2 * h, h, None), (vec_l, h, 8),
        (at_l + 3 * h, h, None), (at_ml + 3 * d, d, None), (vec_l + 256, d, 0),
        (at_me, d, None), (0, f, None), (vec_e, f, 0),
        (at_me + d, d, None), (f, f, None), (vec_e + 256, f, 0),
        (at_d, f, None), (at_md, d, None), (at_d + f, d, 0),
    ]
    outs = unpack(core, half, swap(half, "core", 1), widths, places)
    outs = [x[0] if i % 3 == 2 else x.T if i % 3 == 0 else x for i, x in enumerate(outs)]
    return (layer_out, grad_tokens, *outs)


def solution(mesh):
    fine = Mesh(mesh.devices.reshape(4, 2, 4, 2, 2), ("y", "xh", "z", "core", "mp"))
    col, row, vec, rep = P(None, "mp"), P("mp", None), P("mp"), P()
    tok = P(DP, None)
    split, merged = (rep, col, vec), (row, rep, rep)
    return jax.shard_map(
        body,
        mesh=fine,
        in_specs=(tok, P(DP), tok, rep, rep, col, col, col, row, col, col, P(("mp",) + DP, None))
        + split * 3 + merged + split * 2 + merged,
        out_specs=(tok, tok) + split * 3 + merged + split * 2 + merged,
        check_vma=False,
    )
```

```python
import functools
import jax
import jax.numpy as jnp
import numpy as np
from jax import lax
from jax.experimental import pallas as pl
from jax.experimental.pallas import tpu as pltpu
from jax.sharding import Mesh, PartitionSpec as P

HEAD_DIM = 128
RANK = 16
RATIO = 2.0
EPSILON = 1e-05
STATS_WIDTH = 1536
PART = 160
F32 = jnp.float32
BF16 = jnp.bfloat16
DP = ("y", "xh", "z", "core")
ANY = pl.BlockSpec(memory_space=pl.ANY)
SMEM = pl.BlockSpec(memory_space=pltpu.SMEM)
MIB = 1024 * 1024


def dot(a, b, dims=((1,), (0,))):
    return lax.dot_general(a.astype(BF16), b.astype(BF16), (dims, ((), ())), preferred_element_type=F32)


def dot_nt(a, b):
    return dot(a, b, ((1,), (1,)))


def dot_tn(a, b):
    return dot(a, b, ((0,), (0,)))


def col_sum(v):
    return jnp.sum(v, axis=0, keepdims=True)


def chunks(n, size):
    return [slice(r, min(r + size, n)) for r in range(0, n, size)]


def shape(dims, dtype=F32):
    return jax.ShapeDtypeStruct(dims, dtype)


def row_of(ref, lanes):
    return jnp.concatenate([ref[i : i + 1, :] for i in range(lanes.start // 128, lanes.stop // 128)], axis=1)


def rows_of(height, width):
    return pl.BlockSpec((height, width), lambda j: (j, 0))


def full(x):
    return pl.BlockSpec(x.shape, lambda j, r=len(x.shape): (0,) * r, pipeline_mode=pl.Buffered(1))


def call(kernel, ins, outs, scratch, name, work, traffic, grid=1, mib=60):
    return pl.pallas_call(
        kernel,
        grid=(grid,),
        in_specs=[full(x) if block is None else block for x, block in ins],
        out_specs=[full(x) if block is None else block for x, block in outs],
        out_shape=[x for x, _ in outs],
        scratch_shapes=scratch,
        compiler_params=pltpu.CompilerParams(vmem_limit_bytes=mib * MIB),
        cost_estimate=pl.CostEstimate(flops=int(work), bytes_accessed=int(traffic), transcendentals=0),
        name=name,
    )(*[x for x, _ in ins])


class Copies:
    def __init__(self, sems):
        self.sems, self.used, self.waiting = sems, 0, {}

    def start(self, key, src, dst):
        copy = pltpu.make_async_copy(src, dst, self.sems.at[self.used])
        self.used += 1
        copy.start()
        self.waiting.setdefault(key, []).append(copy)

    def wait(self, key):
        for copy in self.waiting.pop(key, []):
            copy.wait()

    def finish(self):
        for key in list(self.waiting):
            self.wait(key)


def sems(n):
    return pltpu.SemaphoreType.DMA((n,))


def square_sum(w_ref, lanes):
    depth = w_ref.shape[0]
    width = lanes.stop - lanes.start
    if depth % 128:
        v = w_ref[:, lanes].astype(F32)
        return col_sum(v * v)
    parts = []
    for c in chunks(width, 256):
        to = slice(lanes.start + c.start, lanes.start + c.stop)
        squares = jnp.zeros((8, c.stop - c.start), F32)
        for r in chunks(depth, 64):
            chunk = w_ref[r, to].astype(F32)
            squares = squares + jnp.sum((chunk * chunk).reshape(8, 8, c.stop - c.start), axis=0)
        parts.append(col_sum(squares))
    return jnp.concatenate(parts, axis=1)


def stats_kernel(kinds, *refs):
    count = len(kinds)
    w_refs, rest = refs[:count], list(refs[count:])
    ins = [[rest.pop(0) for _ in range(3 if whole else 2)] for whole in kinds]
    outs = [[rest.pop(0) for _ in range(3 if whole else 2)] for whole in kinds]
    bufs, sem = rest[:count], rest[count]
    copies = Copies(sem)
    todo = sorted((lanes.start, i, lanes) for i, w in enumerate(w_refs) for lanes in chunks(w.shape[1], STATS_WIDTH))
    for start, i, lanes in todo:
        copies.start((i, start), w_refs[i].at[:, lanes], bufs[i].at[:, lanes])
    lefts = [x[0][...].astype(BF16) for x in ins]
    grams = [dot_nt(left, left) for left in lefts]
    for start, i, lanes in todo:
        copies.wait((i, start))
        right = ins[i][1][:, lanes]
        lw = dot(lefts[i], bufs[i][:, lanes])
        ld = lw + RATIO * dot(grams[i], right)
        total = square_sum(bufs[i], lanes) + RATIO * col_sum(right * (lw + ld))
        if kinds[i]:
            fac_ref, isq_ref, ld_ref = outs[i]
            isq_ref[:, lanes] = 1.0 / total
            fac_ref[:, lanes] = row_of(ins[i][2], lanes) * lax.rsqrt(total)
        else:
            total_ref, ld_ref = outs[i]
            total_ref[:, lanes] = total
        ld_ref[:, lanes] = ld


def stats(projections):
    kinds = [p[3] is not None for p in projections]
    ins = [(p[0], ANY) for p in projections]
    outs = []
    for (w, left, right, mag), whole in zip(projections, kinds):
        ins += [(left, None), (right, None)] + ([(mag, None)] if whole else [])
        outs += [(shape((1, w.shape[1])), None)] * (2 if whole else 1) + [(shape((RANK, w.shape[1])), None)]
    size = sum(p[0].size for p in projections)
    scratch = [pltpu.VMEM(p[0].shape, BF16) for p in projections] + [sems(16)]
    flat = call(functools.partial(stats_kernel, kinds), ins, outs, scratch, "stats", 2 * RANK * size, 2 * size)
    given = []
    for whole in kinds:
        n = 3 if whole else 2
        given.append(flat[:n])
        flat = flat[n:]
    return given


def unit_rows(v):
    return lax.rsqrt(jnp.mean(v * v, axis=-1, keepdims=True) + EPSILON)


def rotate(v, cosine, sine):
    return v * cosine + pltpu.roll(v, HEAD_DIM // 2, 1) * sine


def attend_kernel(
    length_ref, x_ref, gain_ref, lq_ref, lk_ref, lv_ref, cos_ref, sin_ref, ro_ref, rq_ref, rk_ref, rv_ref, fq_ref, fk_ref, fv_ref, lo_ref,
    wq_ref, wk_ref, wv_ref, wo_ref,
    part_ref, aq_ref, ak_ref, av_ref, yo_ref, first_out, q_out, k_out, v_out, probs_out, mix_out,
    wq, wk, wv, wo, first, q, k, v, probs, mix, sem,
):
    n, d = x_ref.shape
    copies = Copies(sem)
    groups = chunks(wq_ref.shape[1], 256)
    head, rest = groups[0], slice(groups[1].start, groups[-1].stop)
    for key, lanes in (("head", head), ("rest", rest)):
        for w, src in ((wq, wq_ref), (wk, wk_ref), (wv, wv_ref)):
            copies.start(key, src.at[:, lanes], w.at[:, lanes])
    copies.start("rest", wo_ref, wo)
    everything = slice(0, d)
    gain = row_of(gain_ref, everything)
    for r in chunks(n, 16):
        x = x_ref[r, :].astype(F32)
        first[r, :] = (x * unit_rows(x) * gain).astype(BF16)
    for left, out in ((lq_ref, aq_ref), (lk_ref, ak_ref), (lv_ref, av_ref)):
        out[...] = dot_nt(first[...], left[...]).astype(BF16)
    cosine, sine = cos_ref[...], sin_ref[...]
    row = lax.broadcasted_iota(jnp.int32, (n, n), 0)
    col = lax.broadcasted_iota(jnp.int32, (n, n), 1)
    allowed = (col <= row) & (col < length_ref[0])

    def project(lanes):
        def one(w, a, right, fac):
            return (dot(first[...], w[:, lanes]) + RATIO * dot(a[...], right[:, lanes])) * fac[:, lanes]

        vq, vk = one(wq, aq_ref, rq_ref, fq_ref), one(wk, ak_ref, rk_ref, fk_ref)
        v[:, lanes] = one(wv, av_ref, rv_ref, fv_ref).astype(BF16)
        for h in chunks(256, HEAD_DIM):
            to = slice(lanes.start + h.start, lanes.start + h.stop)
            q[:, to] = (rotate(vq[:, h], cosine, sine) * HEAD_DIM**-0.5).astype(BF16)
            k[:, to] = rotate(vk[:, h], cosine, sine).astype(BF16)

    def attention(lanes):
        for h in chunks(256, HEAD_DIM):
            at = slice(lanes.start + h.start, lanes.start + h.stop)
            i = at.start // HEAD_DIM
            scores = jnp.where(allowed, dot_nt(q[:, at], k[:, at]), -1e30)
            e = jnp.exp(scores - jnp.max(scores, axis=-1, keepdims=True))
            probs[i] = (e * (1.0 / jnp.sum(e, axis=-1, keepdims=True))).astype(BF16)
            mix[:, at] = dot(probs[i], v[:, at]).astype(BF16)

    copies.wait("head")
    project(head)
    copies.wait("rest")
    for i, lanes in enumerate(groups):
        if i + 1 < len(groups):
            project(groups[i + 1])
        attention(lanes)
    for src, dst in ((first, first_out), (q, q_out), (k, k_out), (v, v_out), (probs, probs_out), (mix, mix_out)):
        copies.start("end", src, dst)
    yo_ref[...] = dot_nt(mix[...], lo_ref[...]).astype(BF16)
    for lanes in chunks(d, 512):
        part_ref[:, lanes] = (dot(mix[...], wo[:, lanes]) + RATIO * dot(yo_ref[...], ro_ref[:, lanes])).astype(BF16)
    copies.finish()


def attend(length, tokens, gain, lefts, cosine, sine, right_o, rights, facs, left_o, weights):
    n, d = tokens.shape
    h = weights[0].shape[1]
    heads = h // HEAD_DIM
    ins = [(length, SMEM)] + [(x, None) for x in (tokens, gain, *lefts, cosine, sine, right_o, *rights, *facs, left_o)]
    ins += [(w, ANY) for w in weights]
    outs = [(shape((n, d), BF16), None)] + [(shape((n, RANK), BF16), None)] * 4 + [(shape((n, d), BF16), ANY)]
    outs += [(shape((n, h), BF16), ANY)] * 3 + [(shape((heads, n, n), BF16), ANY), (shape((n, h), BF16), ANY)]
    scratch = [pltpu.VMEM(w.shape, BF16) for w in weights] + [pltpu.VMEM((n, d), BF16)] + [pltpu.VMEM((n, h), BF16)] * 3
    scratch += [pltpu.VMEM((heads, n, n), BF16), pltpu.VMEM((n, h), BF16), sems(64)]
    return call(attend_kernel, ins, outs, scratch, "attend", 8 * n * d * h, 8 * d * h)


def mlp_kernel(
    x_ref, own_ref, got_ref, fo_ref, gain_ref, cot_ref, fd_ref, rd_ref, lg_ref, lu_ref, ldt_ref,
    rg_ref, ru_ref, fg_ref, fu_ref, ig_ref, iu_ref, dg_ref, du_ref, mg_ref, mu_ref, raw_ref, wg_ref, wu_ref,
    ps_ref, zd_ref, loc_ref, mix_ref, act_out, wd_out,
    raw, act, wd, wg, wu, second, gpd, gpg, gpu, cg, cu, sem,
):
    n, d = cot_ref.shape
    f = wd.shape[0]
    slots, each = raw.shape[0], raw.shape[1]
    pieces, _, height = raw_ref.shape[:3]
    per = slots // 2
    rounds = pieces // (each * per)
    copies = Copies(sem)
    groups = chunks(f, 256)
    bounds = [(i * f // rounds) // 256 for i in range(rounds)] + [len(groups)]

    def fetch(i):
        for c in range(per * i, per * (i + 1)):
            copies.start(("raw", i), raw_ref.at[each * c : each * (c + 1)], raw.at[c % slots])
        lanes = slice(bounds[i] * 256, bounds[i + 1] * 256)
        copies.start(("w", i), wg_ref.at[:, lanes], wg.at[:, lanes])
        copies.start(("w", i), wu_ref.at[:, lanes], wu.at[:, lanes])

    fetch(0)
    fetch(1)
    gain, fo, fd = row_of(gain_ref, slice(0, d)), fo_ref[...], fd_ref[...]
    for r in chunks(n, 16):
        hidden = x_ref[r, :].astype(F32) + (own_ref[r, :].astype(F32) + got_ref[r, :].astype(F32)) * fo
        second[r, :] = (hidden * unit_rows(hidden) * gain).astype(BF16)
        gpd[r, :] = (cot_ref[r, :].astype(F32) * fd).astype(BF16)
    ag = dot_nt(second[...], lg_ref[...]).astype(BF16)
    au = dot_nt(second[...], lu_ref[...]).astype(BF16)
    zd_ref[...] = dot_nt(gpd[...], rd_ref[...]).astype(BF16)

    def compact(c):
        y, half = c // 2, c % 2
        for side in range(2):
            at = (y * 16 + side * 8 + half * 4) * height
            wd[at : at + 4 * height, :] = jnp.concatenate([raw[c % slots, i, side] for i in range(each)], axis=0)

    def gates(lanes):
        grad_act = dot_nt(gpd[...], wd[lanes, :]) + RATIO * dot(zd_ref[...], ldt_ref[:, lanes])
        g = (dot(second[...], wg[:, lanes]) + RATIO * dot(ag, rg_ref[:, lanes])) * fg_ref[:, lanes]
        u = (dot(second[...], wu[:, lanes]) + RATIO * dot(au, ru_ref[:, lanes])) * fu_ref[:, lanes]
        sig = 1.0 / (1.0 + jnp.exp(-g))
        silu = g * sig
        act[:, lanes] = (silu * u).astype(BF16)
        for grad, val, right, fac, isq, gp, nc in (
            (grad_act * u * (sig + silu * (1.0 - sig)), g, rg_ref, fg_ref, ig_ref, gpg, cg),
            (grad_act * silu, u, ru_ref, fu_ref, iu_ref, gpu, cu),
        ):
            s = col_sum(grad * val)
            nc[:, lanes] = s
            gp[:n, lanes] = (grad * fac[:, lanes]).astype(BF16)
            gp[n:, lanes] = (-s * isq[:, lanes] * right[:, lanes]).astype(BF16)

    for i in range(rounds):
        copies.wait(("raw", i))
        copies.wait(("w", i))
        for c in range(per * i, per * (i + 1)):
            compact(c)
        if i + 2 < rounds:
            fetch(i + 2)
        for lanes in groups[bounds[i] : bounds[i + 1]]:
            gates(lanes)
    copies.start("end", wd, wd_out)
    copies.start("end", act, act_out)
    sides = ((gpg, rg_ref, lg_ref, wg), (gpu, ru_ref, lu_ref, wu))
    zs = [dot_nt(gp[...], right[...]).astype(BF16) for gp, right, _, _ in sides]
    for lanes in chunks(d, 512):
        both = [dot_nt(gp[...], w[lanes, :]) for gp, _, _, w in sides]
        low = sum(dot(z, left[:, lanes]) for z, (_, _, left, _) in zip(zs, sides))
        ps_ref[:, lanes] = (both[0][:n] + both[1][:n] + RATIO * low[:n]).astype(BF16)
        for i, (part, z, (_, _, left, _)) in enumerate(zip(both, zs, sides)):
            out = dot_tn(z[:n], second[:, lanes]) + part[n:] + RATIO * dot(z[n:], left[:, lanes])
            mix_ref[:, i * d + lanes.start : i * d + lanes.stop] = (RATIO * out).astype(BF16)
    for i, (a, gp, isq, ld, mag, nc) in enumerate(((ag, gpg, ig_ref, dg_ref, mg_ref, cg), (au, gpu, iu_ref, du_ref, mu_ref, cu))):
        s = nc[...]
        loc_ref[:, i * f : (i + 1) * f] = (RATIO * (dot_tn(a, gp[:n, :]) - ld[...] * (s * isq[...]))).astype(BF16)
        v = s / row_of(mag, slice(0, f))
        rows = [v[:, lanes] for lanes in groups] + [jnp.zeros((RANK - len(groups), 256), F32)]
        loc_ref[:, 2 * f + 256 * i : 2 * f + 256 * (i + 1)] = jnp.concatenate(rows, axis=0).astype(BF16)
    copies.finish()


def mlp(tokens, own, got, fac_o, gain, cot, fac_d, right_d, lefts, left_dt, rights, facs, isqs, lds, mags, raw, weights):
    n, d = cot.shape
    f = weights[0].shape[1]
    ins = [(x, None) for x in (tokens, own, got, fac_o, gain, cot, fac_d, right_d, *lefts, left_dt, *rights, *facs, *isqs, *lds, *mags)]
    ins += [(x, ANY) for x in (raw, *weights)]
    outs = [(shape((n, d), BF16), None), (shape((n, RANK), BF16), None)]
    outs += [(shape((RANK, 2 * f + 512), BF16), None), (shape((RANK, 2 * d), BF16), None)]
    outs += [(shape((n, f), BF16), ANY), (shape((f, d), BF16), ANY)]
    scratch = [
        pltpu.VMEM((4, 4, *raw.shape[1:]), BF16), pltpu.VMEM((n, f), BF16), pltpu.VMEM((f, d), BF16), pltpu.VMEM((d, f), BF16), pltpu.VMEM((d, f), BF16),
        pltpu.VMEM((n, d), BF16), pltpu.VMEM((n, d), BF16), pltpu.VMEM((n + RANK, f), BF16), pltpu.VMEM((n + RANK, f), BF16),
        pltpu.VMEM((1, f), F32), pltpu.VMEM((1, f), F32), sems(32),
    ]
    return call(mlp_kernel, ins, outs, scratch, "mlp", 10 * n * d * f, 6 * d * f, mib=62)


def down_kernel(ldt_ref, fd_ref, rd_ref, zd_ref, act_ref, cot_ref, wd_ref, pd_ref, sd_ref, dd_ref, td_ref, tl_ref, wd, lhs, cot_buf, sem):
    n, f = act_ref.shape
    d = cot_ref.shape[1]
    copies = Copies(sem)
    groups = chunks(d, 512)
    copies.start("act", act_ref, lhs.at[:n, :])
    for lanes in groups:
        copies.start(lanes.start, wd_ref.at[:, lanes], wd.at[:, lanes])
        copies.start(lanes.start, cot_ref.at[:, lanes], cot_buf.at[:, lanes])
    lhs[n:, :] = ldt_ref[...].astype(BF16)
    copies.wait("act")
    low = dot_nt(lhs[...], ldt_ref[...]).astype(BF16)
    tl_ref[...] = dot_tn(zd_ref[...], lhs[:n, :])
    for lanes in groups:
        copies.wait(lanes.start)
        out = dot(lhs[...], wd[:, lanes]) + RATIO * dot(low, rd_ref[:, lanes])
        pd = out[:n].astype(BF16)
        pd_ref[:, lanes] = pd
        dd_ref[:, lanes] = out[n:]
        cot = cot_buf[:, lanes].astype(F32)
        sd_ref[:, lanes] = col_sum(cot * pd.astype(F32)) * fd_ref[:, lanes]
        td_ref[:, lanes] = dot_tn(low[:n], cot * fd_ref[:, lanes])


def down_forward(act, left_dt, cot, fac_d, right_d, zd, w_down):
    n, f = act.shape
    d = cot.shape[1]
    ins = [(x, None) for x in (left_dt, fac_d, right_d, zd)] + [(x, ANY) for x in (act, cot, w_down)]
    outs = [(shape((n, d), BF16), None), (shape((1, d)), None), (shape((RANK, d)), None), (shape((RANK, d)), None), (shape((RANK, f)), None)]
    scratch = [pltpu.VMEM((f, d), BF16), pltpu.VMEM((n + RANK, f), BF16), pltpu.VMEM((n, d), BF16), sems(16)]
    return call(down_kernel, ins, outs, scratch, "down_forward", 2 * n * d * f, 2 * d * f)


def back_kernel(
    gain_ref, mo_ref, fo_ref, io_ref, ro_ref, do_ref, yo_ref,
    aq_ref, ak_ref, av_ref, lq_ref, lk_ref, lv_ref, cos_ref, sin_ref, rq_ref, rk_ref, rv_ref, fq_ref, fk_ref, fv_ref,
    iq_ref, ik_ref, iv_ref, dq_ref, dk_ref, dv_ref, mq_ref, mk_ref, mv_ref, lo_ref,
    s0_ref, s1_ref, id_ref, md_ref, rd_ref, dd_ref, td_ref, ldt_ref, tl_ref,
    own_hbm, got_hbm, own_o_hbm, got_o_hbm, x_hbm, cot_hbm, q_ref, k_ref, v_ref, probs_ref, mix_ref, first_ref, wq_ref, wk_ref, wv_ref, wo_ref, wd_ref,
    pf0_ref, pf1_ref, loc_ref, mixed_ref, locd_ref, mixd_ref, gh_out,
    own_ref, got_ref, own_o_ref, got_o_ref, x_ref, cot_ref, q, k, v, probs, mix, first, wq, wk, wv, wo, wd, gh, gpo, gpq, gpk, gpv, sq, sk, sv, sem,
):
    n, d = x_ref.shape
    span = wq_ref.shape[1]
    copies = Copies(sem)
    groups = chunks(span, 256)
    for src, dst in ((own_o_hbm, own_o_ref), (got_o_hbm, got_o_ref), (x_hbm, x_ref), (own_hbm, own_ref), (got_hbm, got_ref), (cot_hbm, cot_ref)):
        copies.start("first", src, dst)
    copies.start("heads", wo_ref, wo)
    for src, dst in ((q_ref, q), (k_ref, k), (v_ref, v), (probs_ref, probs)):
        copies.start("heads", src, dst)
    for src, dst in ((wq_ref, wq), (wk_ref, wk), (wv_ref, wv)):
        copies.start("late", src, dst)
    copies.start("late", mix_ref, mix)
    copies.start("late", first_ref, first)
    copies.start("down", wd_ref, wd)
    gain, fo = row_of(gain_ref, slice(0, d)), fo_ref[...]
    sums = jnp.zeros((8, d), F32)
    copies.wait("first")
    for r in chunks(n, 16):
        value = (own_o_ref[r, :].astype(F32) + got_o_ref[r, :].astype(F32)) * fo
        hidden = x_ref[r, :].astype(F32) + value
        inverse = unit_rows(hidden)
        unit = hidden * inverse
        w2 = (own_ref[r, :].astype(F32) + got_ref[r, :].astype(F32)) * gain
        grad = cot_ref[r, :].astype(F32) + inverse * (w2 - unit * jnp.mean(w2 * unit, axis=-1, keepdims=True))
        gh[r, :] = grad
        gpo[r, :] = (grad * fo).astype(BF16)
        both = grad * value
        sums = sums + both[:8] + both[8:]
    copies.start("end", gh, gh_out)
    so = col_sum(sums)
    ncoef = -so * io_ref[...]
    gpo[n:, :] = (ncoef * ro_ref[...]).astype(BF16)
    zo = dot_nt(gpo[...], ro_ref[...]).astype(BF16)
    mixed_ref[:, 3 * d :] = (RATIO * (dot_tn(yo_ref[...], gpo[:n, :]) + do_ref[...] * ncoef)).astype(BF16)
    cosine, sine = cos_ref[...], -sin_ref[...]
    scale = HEAD_DIM**-0.5
    parts_o = []
    copies.wait("heads")
    for lanes in groups:
        both = dot_nt(gpo[...], wo[lanes, :]) + RATIO * dot(zo, lo_ref[:, lanes])
        grad_attn = both[:n].astype(BF16)
        parts_o.append(both[n:])
        for h in chunks(256, HEAD_DIM):
            at = slice(lanes.start + h.start, lanes.start + h.stop)
            ga, p_low = grad_attn[:, h], probs[at.start // HEAD_DIM]
            p = p_low.astype(F32)
            gprobs = dot_nt(ga, v[:, at])
            gscores = (p * (gprobs - jnp.sum(p * gprobs, axis=-1, keepdims=True))).astype(BF16)
            gq = rotate(dot(gscores, k[:, at]), cosine, sine) * scale
            gk = rotate(dot_tn(gscores, q[:, at]), cosine, sine)
            gv = dot_tn(p_low, ga)
            vq = rotate(q[:, at].astype(F32), cosine, sine) * (1.0 / scale)
            vk = rotate(k[:, at].astype(F32), cosine, sine)
            for grad, val, fac, isq, right, gp, s_ref in (
                (gq, vq, fq_ref, iq_ref, rq_ref, gpq, sq),
                (gk, vk, fk_ref, ik_ref, rk_ref, gpk, sk),
                (gv, v[:, at].astype(F32), fv_ref, iv_ref, rv_ref, gpv, sv),
            ):
                s = col_sum(grad * val)
                s_ref[:, at] = s
                gp[:n, at] = (grad * fac[:, at]).astype(BF16)
                gp[n:, at] = (-s * isq[:, at] * right[:, at]).astype(BF16)
    sides = ((gpq, rq_ref, lq_ref, wq), (gpk, rk_ref, lk_ref, wk), (gpv, rv_ref, lv_ref, wv))
    zs = [dot_nt(gp[...], right[...]).astype(BF16) for gp, right, _, _ in sides]
    copies.wait("late")
    for lanes in chunks(d, 512):
        both = [dot_nt(gp[...], w[lanes, :]) for gp, _, _, w in sides]
        low = sum(dot(z, left[:, lanes]) for z, (_, _, left, _) in zip(zs, sides))
        pf = (both[0][:n] + both[1][:n] + both[2][:n] + RATIO * low[:n]).astype(BF16)
        pf0_ref[:, lanes] = pf[: pf0_ref.shape[0]]
        pf1_ref[:, lanes] = pf[pf0_ref.shape[0] :]
        for i, (part, z, (_, _, left, _)) in enumerate(zip(both, zs, sides)):
            out = dot_tn(z[:n], first[:, lanes]) + part[n:] + RATIO * dot(z[n:], left[:, lanes])
            mixed_ref[:, i * d + lanes.start : i * d + lanes.stop] = (RATIO * out).astype(BF16)
    rows = []
    for i, (a, gp, isq, ld, mag, s_ref) in enumerate((
        (aq_ref, gpq, iq_ref, dq_ref, mq_ref, sq), (ak_ref, gpk, ik_ref, dk_ref, mk_ref, sk), (av_ref, gpv, iv_ref, dv_ref, mv_ref, sv),
    )):
        s = s_ref[...]
        loc_ref[:, i * span : (i + 1) * span] = (RATIO * (dot_tn(a[...], gp[:n, :]) - ld[...] * (s * isq[...]))).astype(BF16)
        v_row = s / row_of(mag, slice(0, span))
        rows += [v_row[:, lanes] for lanes in groups]
    out = dot_tn(zo[:n], mix[...]) + jnp.concatenate(parts_o, axis=1)
    loc_ref[:, 3 * span : 4 * span] = (RATIO * out).astype(BF16)
    v_row = so / row_of(mo_ref, slice(0, d))
    more = [v_row[:, lanes] for lanes in chunks(d, 256)]
    tiles = []
    for some in (rows, more):
        tiles.append(jnp.concatenate(some + [jnp.zeros((RANK - len(some), 256), F32)], axis=0))
    loc_ref[:, 4 * span :] = jnp.concatenate(tiles + [jnp.zeros((RANK, 512), F32)], axis=1).astype(BF16)
    f = wd.shape[0]
    s = s0_ref[...] + s1_ref[...]
    ncoef = -s * id_ref[...]
    nr = (ncoef * rd_ref[...]).astype(BF16)
    m = dot_nt(nr, rd_ref[...])
    mixd_ref[...] = (RATIO * (td_ref[...] + dd_ref[...] * ncoef)).astype(BF16)
    v_row = s / row_of(md_ref, slice(0, d))
    rows = [v_row[:, lanes] for lanes in chunks(d, 256)]
    locd_ref[:, f:] = jnp.concatenate(rows + [jnp.zeros((RANK - len(rows), 256), F32)], axis=0).astype(BF16)
    copies.wait("down")
    out = tl_ref[...] + dot_nt(nr, wd[...]) + RATIO * dot(m, ldt_ref[...])
    locd_ref[:, :f] = (RATIO * out).astype(BF16)
    copies.finish()


def back(
    own, got, own_o, got_o, tokens, cot, gain, mag_o, fac_o, isq_o, right_o, ld_o, yo, als, lefts, cosine, sine,
    rights, facs, isqs, lds, mags, left_o, downs, qkv, probs, mix, first, weights,
):
    n, d = tokens.shape
    h = weights[0].shape[1]
    f = weights[4].shape[0]
    ins = [(x, None) for x in (gain, mag_o, fac_o, isq_o, right_o, ld_o, yo)]
    ins += [(x, None) for x in (*als, *lefts, cosine, sine, *rights, *facs, *isqs, *lds, *mags, left_o, *downs)]
    ins += [(x, ANY) for x in (own, got, own_o, got_o, tokens, cot, *qkv, probs, mix, first, *weights)]
    outs = [(shape((PART, d), BF16), None), (shape((n - PART, d), BF16), None), (shape((RANK, 4 * h + 1024), BF16), None), (shape((RANK, 4 * d), BF16), None)]
    outs += [(shape((RANK, f + 256), BF16), None), (shape((RANK, d), BF16), None), (shape((n, d)), ANY)]
    head = pltpu.VMEM((n, h), BF16)
    scratch = [pltpu.VMEM((n, d), BF16)] * 6 + [head] * 3 + [pltpu.VMEM(probs.shape, BF16), head, pltpu.VMEM((n, d), BF16)] + [pltpu.VMEM(w.shape, BF16) for w in weights]
    scratch += [pltpu.VMEM((n, d), F32), pltpu.VMEM((n + RANK, d), BF16)] + [pltpu.VMEM((n + RANK, h), BF16)] * 3
    scratch += [pltpu.VMEM((1, h), F32)] * 3 + [sems(40)]
    return call(back_kernel, ins, outs, scratch, "back", 8 * n * d * h, 8 * d * h)


def layer_kernel(x_ref, own_o_ref, got_o_ref, fo_ref, own_ref, got_ref, fd_ref, out_ref):
    for r in chunks(x_ref.shape[0], 16):
        hidden = x_ref[r, :].astype(F32) + (own_o_ref[r, :].astype(F32) + got_o_ref[r, :].astype(F32)) * fo_ref[...]
        out_ref[r, :] = (hidden + (own_ref[r, :].astype(F32) + got_ref[r, :].astype(F32)) * fd_ref[...]).astype(BF16)


def layer_end(tokens, own_o, got_o, fac_o, own, got, fac_d):
    n, d = tokens.shape
    block = rows_of(128, d)
    ins = [(tokens, block), (own_o, block), (got_o, block), (fac_o, None), (own, block), (got, block), (fac_d, None)]
    return call(layer_kernel, ins, [(shape((n, d), BF16), block)], [], "layer_end", 6 * n * d, 12 * n * d, n // 128)[0]


def token_kernel(x_ref, gh_ref, own0_ref, own1_ref, got0_ref, got1_ref, gain_ref, out_ref):
    gain = row_of(gain_ref, slice(0, x_ref.shape[1]))
    half = got0_ref.shape[0]
    for r in chunks(x_ref.shape[0], 16):
        x = x_ref[r, :].astype(F32)
        inverse = unit_rows(x)
        unit = x * inverse
        own, got, at = (own0_ref, got0_ref, r) if r.start < half else (own1_ref, got1_ref, slice(r.start - half, r.stop - half))
        w1 = (own[at, :].astype(F32) + got[at, :].astype(F32)) * gain
        out_ref[r, :] = (gh_ref[r, :] + inverse * (w1 - unit * jnp.mean(w1 * unit, axis=-1, keepdims=True))).astype(BF16)


def token_end(tokens, grad_hidden, own, got, gain):
    n, d = tokens.shape
    ins = [(x, None) for x in (tokens, grad_hidden, *own, *got, gain)]
    return call(token_kernel, ins, [(shape((n, d), BF16), None)], [], "token_end", 10 * n * d, 12 * n * d)[0]


def shard_kernel(w_ref, left_ref, right_ref, out_ref):
    left, right = left_ref[...], right_ref[...]
    lw = dot(left, w_ref[...])
    ld = lw + RATIO * dot(dot_nt(left, left), right)
    out_ref[...] = square_sum(w_ref, slice(0, w_ref.shape[1])) + RATIO * col_sum(right * (lw + ld))


def shard_stats(w, left, right):
    return call(shard_kernel, [(w, None), (left, None), (right, None)], [(shape((1, w.shape[1])), None)], [], "shard_stats", w.size, w.size)[0]


def halves_kernel(count, core_ref, *refs):
    ins, (keep_ref, send_ref) = refs[:count], refs[count:]
    for side in range(2):
        @pl.when(core_ref[0] == side)
        def _():
            at = 0
            for ref in ins:
                w = ref.shape[1] // 2
                keep_ref[:, at : at + w] = ref[:, side * w : (side + 1) * w]
                send_ref[:, at : at + w] = ref[:, (1 - side) * w : (2 - side) * w]
                at += w


def halves(core, arrays):
    width = sum(x.shape[1] for x in arrays) // 2
    outs = [(shape((RANK, width), BF16), None)] * 2
    return call(functools.partial(halves_kernel, len(arrays)), [(core, SMEM)] + [(x, None) for x in arrays], outs, [], "halves", 0, width)


def quarters_kernel(widths, z_ref, keep_ref, got_ref, *refs):
    outs, total = refs[:4], refs[4]
    total[...] = (keep_ref[...].astype(F32) + got_ref[...].astype(F32)).astype(BF16)
    at = to = 0
    for w in widths:
        q = w // 8
        for k in range(4):
            start = at + (z_ref[0] ^ k) * q
            outs[k][:, to : to + q] = total[:, pl.ds(pl.multiple_of(start, 128), q)]
        at += w // 2
        to += q


def quarters(z, keep, got, widths):
    width = sum(widths) // 8
    outs = [(shape((RANK, width), BF16), None)] * 4
    ins = [(z, SMEM), (keep, None), (got, None)]
    return call(functools.partial(quarters_kernel, widths), ins, outs, [pltpu.VMEM(keep.shape, BF16)], "quarters", 0, width)


def joined_kernel(widths, z_ref, *refs):
    ins, out_ref = refs[:4], refs[4]
    at = to = 0
    for w in widths:
        q = w // 8
        for k in range(4):
            out_ref[:, pl.ds(pl.multiple_of(to + (z_ref[0] ^ k) * q, 128), q)] = ins[k][:, at : at + q]
        at += q
        to += w // 2


def joined(z, parts, widths):
    width = sum(widths) // 2
    ins = [(z, SMEM)] + [(x, None) for x in parts]
    return call(functools.partial(joined_kernel, widths), ins, [(shape((RANK, width), BF16), None)], [], "joined", 0, width)[0]


def unpack_kernel(widths, places, core_ref, half_ref, got_ref, *refs):
    whole, outs = refs[-1], refs[:-1]
    for side in range(2):
        @pl.when(core_ref[0] == side)
        def _():
            at = to = 0
            for w in widths:
                h = w // 2
                whole[:, to + side * h : to + (side + 1) * h] = half_ref[:, at : at + h].astype(F32)
                whole[:, to + (1 - side) * h : to + (2 - side) * h] = got_ref[:, at : at + h].astype(F32)
                at += h
                to += w
    for out, (start, count, row) in zip(outs, places):
        if row is None:
            out[...] = whole[:, start : start + count]
        else:
            for i in range(count // 128):
                at = start + i % 2 * 128
                out[i : i + 1, :] = whole[row + i // 2 : row + i // 2 + 1, at : at + 128]


def unpack(core, half, got, widths, places):
    outs = [(shape((RANK, count) if row is None else (count // 128, 128)), None) for _, count, row in places]
    total = sum(widths)
    ins = [(core, SMEM), (half, None), (got, None)]
    return call(functools.partial(unpack_kernel, widths, places), ins, outs, [pltpu.VMEM((RANK, total), F32)], "unpack", 0, total)


def swap(x, axis_name, k):
    n = lax.axis_size(axis_name)
    return lax.ppermute(x, axis_name, [(i, i ^ k) for i in range(n)])


def tree(parts):
    while len(parts) > 1:
        parts = [parts[i] + parts[i + 1] for i in range(0, len(parts), 2)]
    return parts[0]


def xor_sum(x, axis_name):
    n = lax.axis_size(axis_name)
    return tree([x] + [swap(x, axis_name, k) for k in range(1, n)])


def after(x, *others):
    return lax.optimization_barrier((x,) + others)[0]


def scatter_sum(arrays, core, z, *ahead):
    widths = [x.shape[1] for x in arrays]
    keep, send = halves(core, arrays)
    own, *sends = quarters(z, keep, swap(send, "core", 1), widths)
    got = [swap(x, "z", k + 1) for k, x in enumerate(sends)]
    own = after(own, *ahead)
    return tree([own.astype(F32)] + [x.astype(F32) for x in got]).astype(BF16)


def rope_tables(span):
    half = HEAD_DIM // 2
    frequency = 10000.0 ** (-(np.arange(half, dtype=np.float64) * 2.0) / HEAD_DIM)
    angles = np.arange(span, dtype=np.float64)[:, None] * frequency[None, :]
    cosine, sine = np.cos(angles), np.sin(angles)
    return np.concatenate([cosine, cosine], 1).astype(np.float32), np.concatenate([-sine, sine], 1).astype(np.float32)


def body(
    tokens, lengths, cotangent, gain_attn, gain_ffn,
    w_query, w_key, w_value, w_output, w_gate, w_up, w_down,
    left_query, right_query, mag_query,
    left_key, right_key, mag_key,
    left_value, right_value, mag_value,
    left_output, right_output, mag_output,
    left_gate, right_gate, mag_gate,
    left_up, right_up, mag_up,
    left_down, right_down, mag_down,
):
    n, d = tokens.shape
    h, f = w_query.shape[1], w_gate.shape[1]
    cosine, sine = (jnp.asarray(t) for t in rope_tables(n))
    core, z = (lax.axis_index(a).astype(jnp.int32)[None] for a in ("core", "z"))
    lq, lk, lv, lo, lg, lu, ld = (
        x.T for x in (left_query, left_key, left_value, left_output, left_gate, left_up, left_down)
    )
    gain1, gain2, mag_q, mag_k, mag_v, mag_o, mag_g, mag_u, mag_d = (
        x.reshape(-1, 128) for x in (gain_attn, gain_ffn, mag_query, mag_key, mag_value, mag_output, mag_gate, mag_up, mag_down)
    )
    shard = w_down.shape[0]
    left_shard = lax.dynamic_slice_in_dim(left_down, lax.axis_index(DP) * shard, shard, 0).T
    far = swap(w_down, "xh", 1)
    first_side = lax.axis_index("xh") == 0
    rows = jnp.stack([jnp.where(first_side, w_down, far), jnp.where(first_side, far, w_down)])
    raw = lax.all_gather(rows, ("y", "z", "core"), axis=0, tiled=False)
    sq_d = shard_stats(w_down, left_shard, right_down)
    sq_d = xor_sum(sq_d, ("xh", "mp"))

    (fq, iq, dq), (fk, ik, dk), (fv, iv, dv), (sq_o, do) = stats([
        (w_query, lq, right_query, mag_q), (w_key, lk, right_key, mag_k), (w_value, lv, right_value, mag_v),
        (w_output, lo, right_output, None),
    ])
    sq_d = after(sq_d, sq_o)
    sq_d = sq_d + swap(sq_d, "core", 1)
    sq_d = xor_sum(sq_d, "z")
    sq_o = sq_o + swap(sq_o, "mp", 1)
    fo, io = mag_output[None, :] * lax.rsqrt(sq_o), 1.0 / sq_o

    part_o, aq, ak, av, yo, first, q, k, v, probs, mix = attend(
        lengths, tokens, gain1, (lq, lk, lv), cosine, sine, right_output,
        (right_query, right_key, right_value), (fq, fk, fv), lo, (w_query, w_key, w_value, w_output),
    )
    got_o = swap(part_o, "mp", 1)
    sq_d = xor_sum(after(sq_d, part_o), "y")
    (fg, ig, dg), (fu, iu, du) = stats([(w_gate, lg, right_gate, mag_g), (w_up, lu, after(right_up, part_o), mag_u)])
    fd, idn = mag_down[None, :] * lax.rsqrt(sq_d), 1.0 / sq_d
    part_s, zd, loc_e, mix_e, act, down = mlp(
        tokens, part_o, got_o, fo, gain2, cotangent, fd, right_down, (lg, lu), ld, (right_gate, right_up),
        (fg, fu), (ig, iu), (dg, du), (mag_g, mag_u), raw, (w_gate, w_up),
    )
    got_s = swap(part_s, "mp", 1)
    part_d, s_d, dd, td, tl = down_forward(act, ld, cotangent, fd, right_down, zd, down)
    far_s = swap(s_d, "mp", 1)
    early = scatter_sum([loc_e, mix_e], core, z)
    got_d = swap(after(part_d, got_s, far_s, early), "mp", 1)
    part_f0, part_f1, loc_l, mix_l, loc_d, mix_d, grad_hidden = back(
        part_s, got_s, part_o, got_o, tokens, cotangent, gain2, mag_o, fo, io, right_output, do, yo,
        (aq, ak, av), (lq, lk, lv), cosine, sine, (right_query, right_key, right_value), (fq, fk, fv), (iq, ik, iv),
        (dq, dk, dv), (mag_q, mag_k, mag_v), lo, (s_d, far_s, idn, mag_d, right_down, dd, td, ld, tl),
        (q, k, v), probs, mix, first, (w_query, w_key, w_value, w_output, down),
    )
    part_f0, part_f1, loc_l, got_d, early = lax.optimization_barrier((part_f0, part_f1, loc_l, got_d, early))
    got_f0, got_f1 = swap(part_f0, "mp", 1), swap(part_f1, "mp", 1)
    layer_out = layer_end(tokens, part_o, got_o, fo, part_d, got_d, fd)
    grad_tokens = token_end(tokens, grad_hidden, (part_f0, part_f1), (got_f0, got_f1), gain1)
    late = scatter_sum([loc_l, loc_d, mix_l, mix_d], core, z, got_f0, layer_out)
    we, wl, wd = loc_e.shape[1], loc_l.shape[1], loc_d.shape[1]
    cut_e, cut_l = we // 8, (wl + wd) // 8
    part = jnp.concatenate([early[:, :cut_e], late[:, :cut_l], early[:, cut_e:], late[:, cut_l:]], axis=1)
    part = tree([part.astype(F32)] + [swap(part, "y", k).astype(F32) for k in range(1, 4)]).astype(BF16)
    mixed = part[:, cut_e + cut_l :]
    far, near, across = swap(part, "xh", 1), swap(mixed, "mp", 1), swap(mixed, ("xh", "mp"), 3)
    total = part.astype(F32) + far.astype(F32)
    other = near.astype(F32) + across.astype(F32)
    part = jnp.concatenate([total[:, : cut_e + cut_l], total[:, cut_e + cut_l :] + other], axis=1).astype(BF16)
    widths = [we, wl, wd, mix_e.shape[1], mix_l.shape[1], mix_d.shape[1]]
    half = joined(z, [after(part, got_f1)] + [swap(part, "z", k) for k in range(1, 4)], widths)
    vec_e, at_l = 2 * f, we
    vec_l, at_d = at_l + 4 * h, at_l + wl
    at_me = at_d + wd
    at_ml = at_me + 2 * d
    at_md = at_ml + 4 * d
    places = [
        (at_ml, d, None), (at_l, h, None), (vec_l, h, 0),
        (at_ml + d, d, None), (at_l + h, h, None), (vec_l, h, 4),
        (at_ml + 2 * d, d, None), (at_l + 2 * h, h, None), (vec_l, h, 8),
        (at_l + 3 * h, h, None), (at_ml + 3 * d, d, None), (vec_l + 256, d, 0),
        (at_me, d, None), (0, f, None), (vec_e, f, 0),
        (at_me + d, d, None), (f, f, None), (vec_e + 256, f, 0),
        (at_d, f, None), (at_md, d, None), (at_d + f, d, 0),
    ]
    outs = unpack(core, half, swap(half, "core", 1), widths, places)
    outs = [x.reshape(-1) if i % 3 == 2 else x.T if i % 3 == 0 else x for i, x in enumerate(outs)]
    return (layer_out, grad_tokens, *outs)


def solution(mesh):
    fine = Mesh(mesh.devices.reshape(4, 2, 4, 2, 2), ("y", "xh", "z", "core", "mp"))
    col, row, vec, rep = P(None, "mp"), P("mp", None), P("mp"), P()
    tok = P(DP, None)
    split, merged = (rep, col, vec), (row, rep, rep)
    return jax.shard_map(
        body,
        mesh=fine,
        in_specs=(tok, P(DP), tok, rep, rep, col, col, col, row, col, col, P(("mp",) + DP, None))
        + split * 3 + merged + split * 2 + merged,
        out_specs=(tok, tok) + split * 3 + merged + split * 2 + merged,
        check_vma=False,
    )
```

```python
import functools
import jax
import jax.numpy as jnp
import numpy as np
from jax import lax
from jax.experimental import pallas as pl
from jax.experimental.pallas import tpu as pltpu
from jax.sharding import Mesh, PartitionSpec as P

HEAD_DIM = 128
RANK = 16
RATIO = 2.0
EPSILON = 1e-05
STATS_WIDTH = 1536
PARTS = (112, 80, 64)
F32 = jnp.float32
BF16 = jnp.bfloat16
DP = ("y", "xh", "z", "core")
ANY = pl.BlockSpec(memory_space=pl.ANY)
SMEM = pl.BlockSpec(memory_space=pltpu.SMEM)
VMEM = pl.BlockSpec(memory_space=pltpu.VMEM)
MIB = 1024 * 1024


def dot(a, b, dims=((1,), (0,))):
    return lax.dot_general(a.astype(BF16), b.astype(BF16), (dims, ((), ())), preferred_element_type=F32)


def dot_nt(a, b):
    return dot(a, b, ((1,), (1,)))


def dot_tn(a, b):
    return dot(a, b, ((0,), (0,)))


def col_sum(v):
    return jnp.sum(v, axis=0, keepdims=True)


def chunks(n, size):
    return [slice(r, min(r + size, n)) for r in range(0, n, size)]


def shape(dims, dtype=F32):
    return jax.ShapeDtypeStruct(dims, dtype)


def row_of(ref, lanes):
    return jnp.concatenate([ref[i : i + 1, :] for i in range(lanes.start // 128, lanes.stop // 128)], axis=1)


def rows_of(height, width):
    return pl.BlockSpec((height, width), lambda j: (j, 0))


def full(x):
    return pl.BlockSpec(x.shape, lambda j, r=len(x.shape): (0,) * r, pipeline_mode=pl.Buffered(1))


def call(kernel, ins, outs, scratch, name, work, traffic, grid=1, mib=60):
    return pl.pallas_call(
        kernel,
        grid=(grid,),
        in_specs=[full(x) if block is None else block for x, block in ins],
        out_specs=[full(x) if block is None else block for x, block in outs],
        out_shape=[x for x, _ in outs],
        scratch_shapes=scratch,
        compiler_params=pltpu.CompilerParams(vmem_limit_bytes=mib * MIB),
        cost_estimate=pl.CostEstimate(flops=int(work), bytes_accessed=int(traffic), transcendentals=0),
        name=name,
    )(*[x for x, _ in ins])


class Copies:
    def __init__(self, sems):
        self.sems, self.used, self.waiting = sems, 0, {}

    def start(self, key, src, dst):
        copy = pltpu.make_async_copy(src, dst, self.sems.at[self.used])
        self.used += 1
        copy.start()
        self.waiting.setdefault(key, []).append(copy)

    def wait(self, key):
        for copy in self.waiting.pop(key, []):
            copy.wait()

    def finish(self):
        for key in list(self.waiting):
            self.wait(key)


def deal(core_ref, arrays, keep_ref, send_ref):
    for side in range(2):
        @pl.when(core_ref[0] == side)
        def _():
            at = 0
            for ref in arrays:
                w = ref.shape[1] // 2
                keep_ref[:, at : at + w] = ref[:, side * w : (side + 1) * w]
                send_ref[:, at : at + w] = ref[:, (1 - side) * w : (2 - side) * w]
                at += w


def sems(n):
    return pltpu.SemaphoreType.DMA((n,))


def square_sum(w_ref, lanes):
    depth = w_ref.shape[0]
    width = lanes.stop - lanes.start
    if depth % 128:
        v = w_ref[:, lanes].astype(F32)
        return col_sum(v * v)
    parts = []
    for c in chunks(width, 256):
        to = slice(lanes.start + c.start, lanes.start + c.stop)
        squares = jnp.zeros((8, c.stop - c.start), F32)
        for r in chunks(depth, 64):
            chunk = w_ref[r, to].astype(F32)
            squares = squares + jnp.sum((chunk * chunk).reshape(8, 8, c.stop - c.start), axis=0)
        parts.append(col_sum(squares))
    return jnp.concatenate(parts, axis=1)


def stats_kernel(kinds, *refs):
    count = len(kinds)
    w_refs, rest = refs[:count], list(refs[count:])
    ins = [[rest.pop(0) for _ in range(3 if whole else 2)] for whole in kinds]
    outs = [[rest.pop(0) for _ in range(3 if whole else 2)] for whole in kinds]
    bufs, sem = rest[:count], rest[count]
    copies = Copies(sem)
    todo = sorted((lanes.start, i, lanes) for i, w in enumerate(w_refs) for lanes in chunks(w.shape[1], STATS_WIDTH))
    for start, i, lanes in todo:
        copies.start((i, start), w_refs[i].at[:, lanes], bufs[i].at[:, lanes])
    lefts = [x[0][...].astype(BF16) for x in ins]
    grams = [dot_nt(left, left) for left in lefts]
    for start, i, lanes in todo:
        copies.wait((i, start))
        right = ins[i][1][:, lanes]
        lw = dot(lefts[i], bufs[i][:, lanes])
        ld = lw + RATIO * dot(grams[i], right)
        total = square_sum(bufs[i], lanes) + RATIO * col_sum(right * (lw + ld))
        if kinds[i]:
            fac_ref, isq_ref, ld_ref = outs[i]
            isq_ref[:, lanes] = 1.0 / total
            fac_ref[:, lanes] = row_of(ins[i][2], lanes) * lax.rsqrt(total)
        else:
            total_ref, ld_ref = outs[i]
            total_ref[:, lanes] = total
        ld_ref[:, lanes] = ld


def stats(projections):
    kinds = [p[3] is not None for p in projections]
    ins = [(p[0], ANY) for p in projections]
    outs = []
    for (w, left, right, mag), whole in zip(projections, kinds):
        ins += [(left, None), (right, None)] + ([(mag, None)] if whole else [])
        outs += [(shape((1, w.shape[1])), None)] * (2 if whole else 1) + [(shape((RANK, w.shape[1])), None)]
    size = sum(p[0].size for p in projections)
    scratch = [pltpu.VMEM(p[0].shape, BF16) for p in projections] + [sems(16)]
    flat = call(functools.partial(stats_kernel, kinds), ins, outs, scratch, "stats", 2 * RANK * size, 2 * size)
    given = []
    for whole in kinds:
        n = 3 if whole else 2
        given.append(flat[:n])
        flat = flat[n:]
    return given


def unit_rows(v):
    return lax.rsqrt(jnp.mean(v * v, axis=-1, keepdims=True) + EPSILON)


def rotate(v, cosine, sine):
    return v * cosine + pltpu.roll(v, HEAD_DIM // 2, 1) * sine


def attend_kernel(
    length_ref, x_ref, gain_ref, lq_ref, lk_ref, lv_ref, cos_ref, sin_ref, ro_ref, rq_ref, rk_ref, rv_ref, fq_ref, fk_ref, fv_ref, lo_ref,
    wq_ref, wk_ref, wv_ref, wo_ref,
    part_ref, aq_ref, ak_ref, av_ref, yo_ref, first_out, q_out, k_out, v_out, probs_out, mix_out,
    wq, wk, wv, wo, first, q, k, v, probs, mix, sem,
):
    n, d = x_ref.shape
    copies = Copies(sem)
    groups = chunks(wq_ref.shape[1], 256)
    head, rest = groups[0], slice(groups[1].start, groups[-1].stop)
    for key, lanes in (("head", head), ("rest", rest)):
        for w, src in ((wq, wq_ref), (wk, wk_ref), (wv, wv_ref)):
            copies.start(key, src.at[:, lanes], w.at[:, lanes])
    copies.start("rest", wo_ref, wo)
    everything = slice(0, d)
    gain = row_of(gain_ref, everything)
    for r in chunks(n, 16):
        x = x_ref[r, :].astype(F32)
        first[r, :] = (x * unit_rows(x) * gain).astype(BF16)
    for left, out in ((lq_ref, aq_ref), (lk_ref, ak_ref), (lv_ref, av_ref)):
        out[...] = dot_nt(first[...], left[...]).astype(BF16)
    cosine, sine = cos_ref[...], sin_ref[...]
    row = lax.broadcasted_iota(jnp.int32, (n, n), 0)
    col = lax.broadcasted_iota(jnp.int32, (n, n), 1)
    allowed = (col <= row) & (col < length_ref[0])

    def project(lanes):
        def one(w, a, right, fac):
            return (dot(first[...], w[:, lanes]) + RATIO * dot(a[...], right[:, lanes])) * fac[:, lanes]

        vq, vk = one(wq, aq_ref, rq_ref, fq_ref), one(wk, ak_ref, rk_ref, fk_ref)
        v[:, lanes] = one(wv, av_ref, rv_ref, fv_ref).astype(BF16)
        for h in chunks(256, HEAD_DIM):
            to = slice(lanes.start + h.start, lanes.start + h.stop)
            q[:, to] = (rotate(vq[:, h], cosine, sine) * HEAD_DIM**-0.5).astype(BF16)
            k[:, to] = rotate(vk[:, h], cosine, sine).astype(BF16)

    def attention(lanes):
        for h in chunks(256, HEAD_DIM):
            at = slice(lanes.start + h.start, lanes.start + h.stop)
            i = at.start // HEAD_DIM
            scores = jnp.where(allowed, dot_nt(q[:, at], k[:, at]), -1e30)
            e = jnp.exp(scores - jnp.max(scores, axis=-1, keepdims=True))
            probs[i] = (e * (1.0 / jnp.sum(e, axis=-1, keepdims=True))).astype(BF16)
            mix[:, at] = dot(probs[i], v[:, at]).astype(BF16)

    copies.wait("head")
    project(head)
    copies.wait("rest")
    for i, lanes in enumerate(groups):
        if i + 1 < len(groups):
            project(groups[i + 1])
        attention(lanes)
    for src, dst in ((first, first_out), (q, q_out), (k, k_out), (v, v_out), (probs, probs_out), (mix, mix_out)):
        copies.start("end", src, dst)
    yo_ref[...] = dot_nt(mix[...], lo_ref[...]).astype(BF16)
    for lanes in chunks(d, 512):
        part_ref[:, lanes] = (dot(mix[...], wo[:, lanes]) + RATIO * dot(yo_ref[...], ro_ref[:, lanes])).astype(BF16)
    copies.finish()


def attend(length, tokens, gain, lefts, cosine, sine, right_o, rights, facs, left_o, weights):
    n, d = tokens.shape
    h = weights[0].shape[1]
    heads = h // HEAD_DIM
    ins = [(length, SMEM)] + [(x, None) for x in (tokens, gain, *lefts, cosine, sine, right_o, *rights, *facs, left_o)]
    ins += [(w, ANY) for w in weights]
    outs = [(shape((n, d), BF16), None)] + [(shape((n, RANK), BF16), None)] * 4 + [(shape((n, d), BF16), ANY)]
    outs += [(shape((n, h), BF16), ANY)] * 3 + [(shape((heads, n, n), BF16), ANY), (shape((n, h), BF16), ANY)]
    scratch = [pltpu.VMEM(w.shape, BF16) for w in weights] + [pltpu.VMEM((n, d), BF16)] + [pltpu.VMEM((n, h), BF16)] * 3
    scratch += [pltpu.VMEM((heads, n, n), BF16), pltpu.VMEM((n, h), BF16), sems(64)]
    return call(attend_kernel, ins, outs, scratch, "attend", 8 * n * d * h, 8 * d * h)


def mlp_kernel(core_ref, xh_ref, *refs):
    ins, refs = refs[:21], refs[21:]
    raw_ref, wg_ref, wu_ref, ps_ref, zd_ref, keep_ref, send_ref, act_out, wd_out, *refs = refs
    bufs, refs = refs[:21], refs[21:]
    raw, act, wd, wg, wu, second, gpd, gpg, gpu, cg, cu, loc_ref, mix_ref, sem = refs
    (
        x_ref, own_ref, got_ref, fo_ref, gain_ref, cot_ref, fd_ref, rd_ref, lg_ref, lu_ref, ldt_ref,
        rg_ref, ru_ref, fg_ref, fu_ref, ig_ref, iu_ref, dg_ref, du_ref, mg_ref, mu_ref,
    ) = bufs
    n, d = cot_ref.shape
    f = wd.shape[0]
    slots, each = raw.shape[0], raw.shape[1]
    pieces, height = raw_ref.shape[0], raw_ref.shape[1] // 2
    per = slots // 2
    rounds = pieces // (each * per)
    copies = Copies(sem)
    groups = chunks(f, 256)
    bounds = [(i * f // rounds) // 256 for i in range(rounds)] + [len(groups)]

    def fetch(i):
        for c in range(per * i, per * (i + 1)):
            copies.start(("raw", i), raw_ref.at[each * c : each * (c + 1)], raw.at[c % slots])
        lanes = slice(bounds[i] * 256, bounds[i + 1] * 256)
        copies.start(("w", i), wg_ref.at[:, lanes], wg.at[:, lanes])
        copies.start(("w", i), wu_ref.at[:, lanes], wu.at[:, lanes])

    for src, dst in zip(ins, bufs):
        copies.start("in", src, dst)
    fetch(0)
    fetch(1)
    copies.wait("in")
    gain, fo, fd = row_of(gain_ref, slice(0, d)), fo_ref[...], fd_ref[...]
    for r in chunks(n, 16):
        hidden = x_ref[r, :].astype(F32) + (own_ref[r, :].astype(F32) + got_ref[r, :].astype(F32)) * fo
        second[r, :] = (hidden * unit_rows(hidden) * gain).astype(BF16)
        gpd[r, :] = (cot_ref[r, :].astype(F32) * fd).astype(BF16)
    ag = dot_nt(second[...], lg_ref[...]).astype(BF16)
    au = dot_nt(second[...], lu_ref[...]).astype(BF16)
    zd_ref[...] = dot_nt(gpd[...], rd_ref[...]).astype(BF16)

    def compact(c):
        y, half = c // 2, c % 2
        for side in range(2):
            at = (y * 16 + half * 4) * height + (xh_ref[0] ^ side) * (8 * height)
            block = jnp.concatenate([raw[c % slots, i, side * height : (side + 1) * height] for i in range(each)], axis=0)
            wd[pl.ds(pl.multiple_of(at, 16), 4 * height), :] = block

    def gates(lanes):
        grad_act = dot_nt(gpd[...], wd[lanes, :]) + RATIO * dot(zd_ref[...], ldt_ref[:, lanes])
        g = (dot(second[...], wg[:, lanes]) + RATIO * dot(ag, rg_ref[:, lanes])) * fg_ref[:, lanes]
        u = (dot(second[...], wu[:, lanes]) + RATIO * dot(au, ru_ref[:, lanes])) * fu_ref[:, lanes]
        sig = 1.0 / (1.0 + jnp.exp(-g))
        silu = g * sig
        act[:, lanes] = (silu * u).astype(BF16)
        for grad, val, right, fac, isq, gp, nc in (
            (grad_act * u * (sig + silu * (1.0 - sig)), g, rg_ref, fg_ref, ig_ref, gpg, cg),
            (grad_act * silu, u, ru_ref, fu_ref, iu_ref, gpu, cu),
        ):
            s = col_sum(grad * val)
            nc[:, lanes] = s
            gp[:n, lanes] = (grad * fac[:, lanes]).astype(BF16)
            gp[n:, lanes] = (-s * isq[:, lanes] * right[:, lanes]).astype(BF16)

    for i in range(rounds):
        copies.wait(("raw", i))
        copies.wait(("w", i))
        for c in range(per * i, per * (i + 1)):
            compact(c)
        if i + 2 < rounds:
            fetch(i + 2)
        for lanes in groups[bounds[i] : bounds[i + 1]]:
            gates(lanes)
    copies.start("end", wd, wd_out)
    copies.start("end", act, act_out)
    for i, (a, gp, isq, ld, mag, nc) in enumerate(((ag, gpg, ig_ref, dg_ref, mg_ref, cg), (au, gpu, iu_ref, du_ref, mu_ref, cu))):
        s = nc[...]
        loc_ref[:, i * f : (i + 1) * f] = (RATIO * (dot_tn(a, gp[:n, :]) - ld[...] * (s * isq[...]))).astype(BF16)
        v = s / row_of(mag, slice(0, f))
        rows = [v[:, lanes] for lanes in groups] + [jnp.zeros((RANK - len(groups), 256), F32)]
        loc_ref[:, 2 * f + 256 * i : 2 * f + 256 * (i + 1)] = jnp.concatenate(rows, axis=0).astype(BF16)
    sides = ((gpg, rg_ref, lg_ref, wg), (gpu, ru_ref, lu_ref, wu))
    zs = [dot_nt(gp[...], right[...]).astype(BF16) for gp, right, _, _ in sides]
    for lanes in chunks(d, 512):
        both = [dot_nt(gp[...], w[lanes, :]) for gp, _, _, w in sides]
        low = sum(dot(z, left[:, lanes]) for z, (_, _, left, _) in zip(zs, sides))
        ps_ref[:, lanes] = (both[0][:n] + both[1][:n] + RATIO * low[:n]).astype(BF16)
        for i, (part, z, (_, _, left, _)) in enumerate(zip(both, zs, sides)):
            out = dot_tn(z[:n], second[:, lanes]) + part[n:] + RATIO * dot(z[n:], left[:, lanes])
            mix_ref[:, i * d + lanes.start : i * d + lanes.stop] = (RATIO * out).astype(BF16)
    deal(core_ref, (loc_ref, mix_ref), keep_ref, send_ref)
    copies.finish()


def mlp(core, xh, tokens, own, got, fac_o, gain, cot, fac_d, right_d, lefts, left_dt, rights, facs, isqs, lds, mags, raw, weights):
    n, d = cot.shape
    f = weights[0].shape[1]
    given = (tokens, own, got, fac_o, gain, cot, fac_d, right_d, *lefts, left_dt, *rights, *facs, *isqs, *lds, *mags)
    ins = [(core, SMEM), (xh, SMEM)] + [(x, ANY) for x in (*given, raw, *weights)]
    wide = 2 * f + 512
    outs = [(shape((n, d), BF16), None), (shape((n, RANK), BF16), None)] + [(shape((RANK, wide // 2 + d), BF16), None)] * 2
    outs += [(shape((n, f), BF16), ANY), (shape((f, d), BF16), ANY)]
    scratch = [pltpu.VMEM(x.shape, x.dtype) for x in given] + [
        pltpu.VMEM((4, 4, *raw.shape[1:]), BF16), pltpu.VMEM((n, f), BF16), pltpu.VMEM((f, d), BF16),
        pltpu.VMEM((d, f), BF16), pltpu.VMEM((d, f), BF16),
        pltpu.VMEM((n, d), BF16), pltpu.VMEM((n, d), BF16), pltpu.VMEM((n + RANK, f), BF16), pltpu.VMEM((n + RANK, f), BF16),
        pltpu.VMEM((1, f), F32), pltpu.VMEM((1, f), F32), pltpu.VMEM((RANK, wide), BF16), pltpu.VMEM((RANK, 2 * d), BF16), sems(48),
    ]
    return call(mlp_kernel, ins, outs, scratch, "mlp", 10 * n * d * f, 6 * d * f, mib=62)


def down_kernel(ldt_ref, fd_ref, rd_ref, zd_ref, act_ref, cot_ref, wd_ref, pd_ref, sd_ref, dd_ref, td_ref, tl_ref, wd, lhs, cot_buf, sem):
    n, f = act_ref.shape
    d = cot_ref.shape[1]
    copies = Copies(sem)
    groups = chunks(d, 512)
    copies.start("act", act_ref, lhs.at[:n, :])
    for lanes in groups:
        copies.start(lanes.start, wd_ref.at[:, lanes], wd.at[:, lanes])
        copies.start(lanes.start, cot_ref.at[:, lanes], cot_buf.at[:, lanes])
    lhs[n:, :] = ldt_ref[...].astype(BF16)
    copies.wait("act")
    low = dot_nt(lhs[...], ldt_ref[...]).astype(BF16)
    tl_ref[...] = dot_tn(zd_ref[...], lhs[:n, :])
    for lanes in groups:
        copies.wait(lanes.start)
        out = dot(lhs[...], wd[:, lanes]) + RATIO * dot(low, rd_ref[:, lanes])
        pd = out[:n].astype(BF16)
        pd_ref[:, lanes] = pd
        dd_ref[:, lanes] = out[n:]
        cot = cot_buf[:, lanes].astype(F32)
        sd_ref[:, lanes] = col_sum(cot * pd.astype(F32)) * fd_ref[:, lanes]
        td_ref[:, lanes] = dot_tn(low[:n], cot * fd_ref[:, lanes])


def down_forward(act, left_dt, cot, fac_d, right_d, zd, w_down):
    n, f = act.shape
    d = cot.shape[1]
    ins = [(x, None) for x in (left_dt, fac_d, right_d, zd)] + [(x, ANY) for x in (act, cot, w_down)]
    outs = [(shape((n, d), BF16), None), (shape((1, d)), None), (shape((RANK, d)), None), (shape((RANK, d)), None), (shape((RANK, f)), None)]
    scratch = [pltpu.VMEM((f, d), BF16), pltpu.VMEM((n + RANK, f), BF16), pltpu.VMEM((n, d), BF16), sems(16)]
    return call(down_kernel, ins, outs, scratch, "down_forward", 2 * n * d * f, 2 * d * f)


def back_kernel(
    core_ref, gain_ref, mo_ref, fo_ref, io_ref, ro_ref, do_ref, yo_ref,
    aq_ref, ak_ref, av_ref, lq_ref, lk_ref, lv_ref, cos_ref, sin_ref, rq_ref, rk_ref, rv_ref, fq_ref, fk_ref, fv_ref,
    iq_ref, ik_ref, iv_ref, dq_ref, dk_ref, dv_ref, mq_ref, mk_ref, mv_ref, lo_ref,
    s0_ref, s1_ref, id_ref, md_ref, rd_ref, dd_ref, td_ref, ldt_ref, tl_ref,
    own_hbm, got_hbm, own_o_hbm, got_o_hbm, x_hbm, cot_hbm, q_ref, k_ref, v_ref, probs_ref, mix_ref, first_ref, wq_ref, wk_ref, wv_ref, wo_ref, wd_ref,
    pf0_ref, pf1_ref, pf2_ref, keep_ref, send_ref, gh_out,
    own_ref, got_ref, own_o_ref, got_o_ref, x_ref, cot_ref, q, k, v, probs, mix, first, wq, wk, wv, wo, wd, gh, gpo, gpq, gpk, gpv, sq, sk, sv, loc_ref, mixed_ref, locd_ref, mixd_ref, sem,
):
    n, d = x_ref.shape
    span = wq_ref.shape[1]
    copies = Copies(sem)
    groups = chunks(span, 256)
    for src, dst in ((own_o_hbm, own_o_ref), (got_o_hbm, got_o_ref), (x_hbm, x_ref), (own_hbm, own_ref), (got_hbm, got_ref), (cot_hbm, cot_ref)):
        copies.start("first", src, dst)
    copies.start("heads", wo_ref, wo)
    for src, dst in ((q_ref, q), (k_ref, k), (v_ref, v), (probs_ref, probs)):
        copies.start("heads", src, dst)
    copies.start("down", wd_ref, wd)
    for src, dst in ((wq_ref, wq), (wk_ref, wk), (wv_ref, wv)):
        copies.start("late", src, dst)
    copies.start("late", mix_ref, mix)
    copies.start("late", first_ref, first)
    gain, fo = row_of(gain_ref, slice(0, d)), fo_ref[...]
    sums = jnp.zeros((8, d), F32)
    copies.wait("first")
    for r in chunks(n, 16):
        value = (own_o_ref[r, :].astype(F32) + got_o_ref[r, :].astype(F32)) * fo
        hidden = x_ref[r, :].astype(F32) + value
        inverse = unit_rows(hidden)
        unit = hidden * inverse
        w2 = (own_ref[r, :].astype(F32) + got_ref[r, :].astype(F32)) * gain
        grad = cot_ref[r, :].astype(F32) + inverse * (w2 - unit * jnp.mean(w2 * unit, axis=-1, keepdims=True))
        gh[r, :] = grad
        gpo[r, :] = (grad * fo).astype(BF16)
        both = grad * value
        sums = sums + both[:8] + both[8:]
    copies.start("end", gh, gh_out)
    so = col_sum(sums)
    ncoef = -so * io_ref[...]
    gpo[n:, :] = (ncoef * ro_ref[...]).astype(BF16)
    zo = dot_nt(gpo[...], ro_ref[...]).astype(BF16)
    mixed_ref[:, 3 * d :] = (RATIO * (dot_tn(yo_ref[...], gpo[:n, :]) + do_ref[...] * ncoef)).astype(BF16)
    cosine, sine = cos_ref[...], -sin_ref[...]
    scale = HEAD_DIM**-0.5
    parts_o = []
    f = wd.shape[0]
    s = s0_ref[...] + s1_ref[...]
    ncoef = -s * id_ref[...]
    nr = (ncoef * rd_ref[...]).astype(BF16)
    m = dot_nt(nr, rd_ref[...])
    mixd_ref[...] = (RATIO * (td_ref[...] + dd_ref[...] * ncoef)).astype(BF16)
    v_row = s / row_of(md_ref, slice(0, d))
    rows = [v_row[:, lanes] for lanes in chunks(d, 256)]
    locd_ref[:, f:] = jnp.concatenate(rows + [jnp.zeros((RANK - len(rows), 256), F32)], axis=0).astype(BF16)
    copies.wait("heads")
    for i, lanes in enumerate(groups):
        if i == len(groups) // 2:
            copies.wait("down")
        if i >= len(groups) // 2:
            half = chunks(f, f // 2)[i - len(groups) // 2]
            out = tl_ref[:, half] + dot_nt(nr, wd[half, :]) + RATIO * dot(m, ldt_ref[:, half])
            locd_ref[:, half] = (RATIO * out).astype(BF16)
        both = dot_nt(gpo[...], wo[lanes, :]) + RATIO * dot(zo, lo_ref[:, lanes])
        grad_attn = both[:n].astype(BF16)
        parts_o.append(both[n:])
        for h in chunks(256, HEAD_DIM):
            at = slice(lanes.start + h.start, lanes.start + h.stop)
            ga, p_low = grad_attn[:, h], probs[at.start // HEAD_DIM]
            p = p_low.astype(F32)
            gprobs = dot_nt(ga, v[:, at])
            gscores = (p * (gprobs - jnp.sum(p * gprobs, axis=-1, keepdims=True))).astype(BF16)
            gq = rotate(dot(gscores, k[:, at]), cosine, sine) * scale
            gk = rotate(dot_tn(gscores, q[:, at]), cosine, sine)
            gv = dot_tn(p_low, ga)
            vq = rotate(q[:, at].astype(F32), cosine, sine) * (1.0 / scale)
            vk = rotate(k[:, at].astype(F32), cosine, sine)
            for grad, val, fac, isq, right, gp, s_ref in (
                (gq, vq, fq_ref, iq_ref, rq_ref, gpq, sq),
                (gk, vk, fk_ref, ik_ref, rk_ref, gpk, sk),
                (gv, v[:, at].astype(F32), fv_ref, iv_ref, rv_ref, gpv, sv),
            ):
                s = col_sum(grad * val)
                s_ref[:, at] = s
                gp[:n, at] = (grad * fac[:, at]).astype(BF16)
                gp[n:, at] = (-s * isq[:, at] * right[:, at]).astype(BF16)
    sides = ((gpq, rq_ref, lq_ref, wq), (gpk, rk_ref, lk_ref, wk), (gpv, rv_ref, lv_ref, wv))
    zs = [dot_nt(gp[...], right[...]).astype(BF16) for gp, right, _, _ in sides]
    copies.wait("late")
    for lanes in chunks(d, 512):
        both = [dot_nt(gp[...], w[lanes, :]) for gp, _, _, w in sides]
        low = sum(dot(z, left[:, lanes]) for z, (_, _, left, _) in zip(zs, sides))
        pf = (both[0][:n] + both[1][:n] + both[2][:n] + RATIO * low[:n]).astype(BF16)
        at = 0
        for ref in (pf0_ref, pf1_ref, pf2_ref):
            ref[:, lanes] = pf[at : at + ref.shape[0]]
            at += ref.shape[0]
        for i, (part, z, (_, _, left, _)) in enumerate(zip(both, zs, sides)):
            out = dot_tn(z[:n], first[:, lanes]) + part[n:] + RATIO * dot(z[n:], left[:, lanes])
            mixed_ref[:, i * d + lanes.start : i * d + lanes.stop] = (RATIO * out).astype(BF16)
    rows = []
    for i, (a, gp, isq, ld, mag, s_ref) in enumerate((
        (aq_ref, gpq, iq_ref, dq_ref, mq_ref, sq), (ak_ref, gpk, ik_ref, dk_ref, mk_ref, sk), (av_ref, gpv, iv_ref, dv_ref, mv_ref, sv),
    )):
        s = s_ref[...]
        loc_ref[:, i * span : (i + 1) * span] = (RATIO * (dot_tn(a[...], gp[:n, :]) - ld[...] * (s * isq[...]))).astype(BF16)
        v_row = s / row_of(mag, slice(0, span))
        rows += [v_row[:, lanes] for lanes in groups]
    out = dot_tn(zo[:n], mix[...]) + jnp.concatenate(parts_o, axis=1)
    loc_ref[:, 3 * span : 4 * span] = (RATIO * out).astype(BF16)
    v_row = so / row_of(mo_ref, slice(0, d))
    more = [v_row[:, lanes] for lanes in chunks(d, 256)]
    tiles = []
    for some in (rows, more):
        tiles.append(jnp.concatenate(some + [jnp.zeros((RANK - len(some), 256), F32)], axis=0))
    loc_ref[:, 4 * span :] = jnp.concatenate(tiles + [jnp.zeros((RANK, 512), F32)], axis=1).astype(BF16)
    deal(core_ref, (loc_ref, locd_ref, mixed_ref, mixd_ref), keep_ref, send_ref)
    copies.finish()


def back(
    core, own, got, own_o, got_o, tokens, cot, gain, mag_o, fac_o, isq_o, right_o, ld_o, yo, als, lefts, cosine, sine,
    rights, facs, isqs, lds, mags, left_o, downs, qkv, probs, mix, first, weights,
):
    n, d = tokens.shape
    h = weights[0].shape[1]
    f = weights[4].shape[0]
    ins = [(core, SMEM)] + [(x, None) for x in (gain, mag_o, fac_o, isq_o, right_o, ld_o, yo)]
    ins += [(x, None) for x in (*als, *lefts, cosine, sine, *rights, *facs, *isqs, *lds, *mags, left_o, *downs)]
    ins += [(x, ANY) for x in (own, got, own_o, got_o, tokens, cot, *qkv, probs, mix, first, *weights)]
    wides = (4 * h + 1024, 4 * d, f + 256, d)
    outs = [(shape((part, d), BF16), None) for part in PARTS]
    outs += [(shape((RANK, sum(wides) // 2), BF16), None)] * 2 + [(shape((n, d)), ANY)]
    head = pltpu.VMEM((n, h), BF16)
    scratch = [pltpu.VMEM((n, d), BF16)] * 6 + [head] * 3 + [pltpu.VMEM(probs.shape, BF16), head, pltpu.VMEM((n, d), BF16)] + [pltpu.VMEM(w.shape, BF16) for w in weights]
    scratch += [pltpu.VMEM((n, d), F32), pltpu.VMEM((n + RANK, d), BF16)] + [pltpu.VMEM((n + RANK, h), BF16)] * 3
    scratch += [pltpu.VMEM((1, h), F32)] * 3 + [pltpu.VMEM((RANK, w), BF16) for w in wides] + [sems(40)]
    return call(back_kernel, ins, outs, scratch, "back", 8 * n * d * h, 8 * d * h)


def layer_kernel(x_ref, own_o_ref, got_o_ref, fo_ref, own_ref, got_ref, fd_ref, out_ref):
    for r in chunks(x_ref.shape[0], 16):
        hidden = x_ref[r, :].astype(F32) + (own_o_ref[r, :].astype(F32) + got_o_ref[r, :].astype(F32)) * fo_ref[...]
        out_ref[r, :] = (hidden + (own_ref[r, :].astype(F32) + got_ref[r, :].astype(F32)) * fd_ref[...]).astype(BF16)


def layer_end(tokens, own_o, got_o, fac_o, own, got, fac_d):
    n, d = tokens.shape
    block = rows_of(128, d)
    ins = [(tokens, block), (own_o, block), (got_o, block), (fac_o, None), (own, block), (got, block), (fac_d, None)]
    return call(layer_kernel, ins, [(shape((n, d), BF16), block)], [], "layer_end", 6 * n * d, 12 * n * d, n // 128)[0]


def token_kernel(x_ref, gh_ref, own0_ref, own1_ref, own2_ref, got0_ref, got1_ref, got2_ref, gain_ref, out_ref):
    gain = row_of(gain_ref, slice(0, x_ref.shape[1]))
    places = []
    for own, got in ((own0_ref, got0_ref), (own1_ref, got1_ref), (own2_ref, got2_ref)):
        places += [(own, got, r) for r in chunks(own.shape[0], 16)]
    for r, (own, got, to) in zip(chunks(x_ref.shape[0], 16), places):
        x = x_ref[r, :].astype(F32)
        inverse = unit_rows(x)
        unit = x * inverse
        w1 = (own[to, :].astype(F32) + got[to, :].astype(F32)) * gain
        out_ref[r, :] = (gh_ref[r, :] + inverse * (w1 - unit * jnp.mean(w1 * unit, axis=-1, keepdims=True))).astype(BF16)


def token_end(tokens, grad_hidden, own, got, gain):
    n, d = tokens.shape
    ins = [(x, None) for x in (tokens, grad_hidden, *own, *got, gain)]
    return call(token_kernel, ins, [(shape((n, d), BF16), None)], [], "token_end", 10 * n * d, 12 * n * d)[0]


def shard_kernel(w_ref, left_ref, right_ref, out_ref):
    left, right = left_ref[...], right_ref[...]
    lw = dot(left, w_ref[...])
    ld = lw + RATIO * dot(dot_nt(left, left), right)
    out_ref[...] = square_sum(w_ref, slice(0, w_ref.shape[1])) + RATIO * col_sum(right * (lw + ld))


def shard_stats(w, left, right):
    return call(shard_kernel, [(w, None), (left, None), (right, None)], [(shape((1, w.shape[1])), None)], [], "shard_stats", w.size, w.size)[0]


def quarters_kernel(widths, z_ref, keep_ref, got_ref, *refs):
    outs, total = refs[:4], refs[4]
    total[...] = (keep_ref[...].astype(F32) + got_ref[...].astype(F32)).astype(BF16)
    at = to = 0
    for w in widths:
        q = w // 8
        for k in range(4):
            start = at + (z_ref[0] ^ k) * q
            outs[k][:, to : to + q] = total[:, pl.ds(pl.multiple_of(start, 128), q)]
        at += w // 2
        to += q


def quarters(z, keep, got, widths):
    width = sum(widths) // 8
    outs = [(shape((RANK, width), BF16), VMEM)] * 4
    ins = [(z, SMEM), (keep, None), (got, VMEM)]
    return call(functools.partial(quarters_kernel, widths), ins, outs, [pltpu.VMEM(keep.shape, BF16)], "quarters", 0, width, mib=16)


def joined_kernel(widths, z_ref, *refs):
    ins, out_ref = refs[:4], refs[4]
    at = to = 0
    for w in widths:
        q = w // 8
        for k in range(4):
            out_ref[:, pl.ds(pl.multiple_of(to + (z_ref[0] ^ k) * q, 128), q)] = ins[k][:, at : at + q]
        at += q
        to += w // 2


def joined(z, parts, widths):
    width = sum(widths) // 2
    ins = [(z, SMEM)] + [(x, VMEM) for x in parts]
    return call(functools.partial(joined_kernel, widths), ins, [(shape((RANK, width), BF16), VMEM)], [], "joined", 0, width, mib=16)[0]


def unpack_kernel(widths, places, core_ref, half_ref, got_ref, *refs):
    whole, outs = refs[-1], refs[:-1]
    for side in range(2):
        @pl.when(core_ref[0] == side)
        def _():
            at = to = 0
            for w in widths:
                h = w // 2
                whole[:, to + side * h : to + (side + 1) * h] = half_ref[:, at : at + h].astype(F32)
                whole[:, to + (1 - side) * h : to + (2 - side) * h] = got_ref[:, at : at + h].astype(F32)
                at += h
                to += w
    for out, (start, count, row) in zip(outs, places):
        if row is None:
            out[...] = whole[:, start : start + count]
        else:
            for i in range(count // 128):
                at = start + i % 2 * 128
                out[i : i + 1, :] = whole[row + i // 2 : row + i // 2 + 1, at : at + 128]


def unpack(core, half, got, widths, places):
    outs = [(shape((RANK, count) if row is None else (count // 128, 128)), None) for _, count, row in places]
    total = sum(widths)
    ins = [(core, SMEM), (half, VMEM), (got, VMEM)]
    return call(functools.partial(unpack_kernel, widths, places), ins, outs, [pltpu.VMEM((RANK, total), F32)], "unpack", 0, total, mib=32)


def swap(x, axis_name, k):
    n = lax.axis_size(axis_name)
    return lax.ppermute(x, axis_name, [(i, i ^ k) for i in range(n)])


def tree(parts):
    while len(parts) > 1:
        parts = [parts[i] + parts[i + 1] for i in range(0, len(parts), 2)]
    return parts[0]


def xor_sum(x, axis_name):
    n = lax.axis_size(axis_name)
    return tree([x] + [swap(x, axis_name, k) for k in range(1, n)])


def after(x, *others):
    return lax.optimization_barrier((x,) + others)[0]


def scatter_sum(keep, send, widths, z, *ahead):
    own, *sends = quarters(z, keep, swap(send, "core", 1), widths)
    got = [swap(x, "z", k + 1) for k, x in enumerate(sends)]
    own = after(own, *ahead)
    return tree([own.astype(F32)] + [x.astype(F32) for x in got]).astype(BF16)


def rope_tables(span):
    half = HEAD_DIM // 2
    frequency = 10000.0 ** (-(np.arange(half, dtype=np.float64) * 2.0) / HEAD_DIM)
    angles = np.arange(span, dtype=np.float64)[:, None] * frequency[None, :]
    cosine, sine = np.cos(angles), np.sin(angles)
    return np.concatenate([cosine, cosine], 1).astype(np.float32), np.concatenate([-sine, sine], 1).astype(np.float32)


def body(
    tokens, lengths, cotangent, gain_attn, gain_ffn,
    w_query, w_key, w_value, w_output, w_gate, w_up, w_down,
    left_query, right_query, mag_query,
    left_key, right_key, mag_key,
    left_value, right_value, mag_value,
    left_output, right_output, mag_output,
    left_gate, right_gate, mag_gate,
    left_up, right_up, mag_up,
    left_down, right_down, mag_down,
):
    n, d = tokens.shape
    h, f = w_query.shape[1], w_gate.shape[1]
    cosine, sine = (jnp.asarray(t) for t in rope_tables(n))
    core, z, xh = (lax.axis_index(a).astype(jnp.int32)[None] for a in ("core", "z", "xh"))
    lq, lk, lv, lo, lg, lu, ld = (
        x.T for x in (left_query, left_key, left_value, left_output, left_gate, left_up, left_down)
    )
    gain1, gain2, mag_q, mag_k, mag_v, mag_o, mag_g, mag_u, mag_d = (
        x.reshape(-1, 128) for x in (gain_attn, gain_ffn, mag_query, mag_key, mag_value, mag_output, mag_gate, mag_up, mag_down)
    )
    shard = w_down.shape[0]
    left_shard = lax.dynamic_slice_in_dim(left_down, lax.axis_index(DP) * shard, shard, 0).T
    far = swap(w_down, "xh", 1)
    raw = lax.all_gather(jnp.concatenate([w_down, far], axis=0), ("y", "z", "core"), axis=0, tiled=False)
    sq_d = shard_stats(w_down, left_shard, right_down)
    sq_d = xor_sum(sq_d, ("xh", "mp"))

    (fq, iq, dq), (fk, ik, dk), (fv, iv, dv), (sq_o, do) = stats([
        (w_query, lq, right_query, mag_q), (w_key, lk, right_key, mag_k), (w_value, lv, right_value, mag_v),
        (w_output, lo, right_output, None),
    ])
    sq_d = after(sq_d, sq_o)
    sq_d = sq_d + swap(sq_d, "core", 1)
    sq_d = xor_sum(sq_d, "z")
    sq_o = sq_o + swap(sq_o, "mp", 1)
    fo, io = mag_output[None, :] * lax.rsqrt(sq_o), 1.0 / sq_o

    part_o, aq, ak, av, yo, first, q, k, v, probs, mix = attend(
        lengths, tokens, gain1, (lq, lk, lv), cosine, sine, right_output,
        (right_query, right_key, right_value), (fq, fk, fv), lo, (w_query, w_key, w_value, w_output),
    )
    got_o = swap(part_o, "mp", 1)
    sq_d = xor_sum(after(sq_d, part_o), "y")
    (fg, ig, dg), (fu, iu, du) = stats([(w_gate, lg, right_gate, mag_g), (w_up, lu, after(right_up, part_o), mag_u)])
    fd, idn = mag_down[None, :] * lax.rsqrt(sq_d), 1.0 / sq_d
    part_s, zd, keep_e, send_e, act, down = mlp(
        core, xh, tokens, part_o, got_o, fo, gain2, cotangent, fd, right_down, (lg, lu), ld, (right_gate, right_up),
        (fg, fu), (ig, iu), (dg, du), (mag_g, mag_u), raw, (w_gate, w_up),
    )
    got_s = swap(part_s, "mp", 1)
    part_d, s_d, dd, td, tl = down_forward(act, ld, cotangent, fd, right_down, zd, down)
    far_s = swap(s_d, "mp", 1)
    we, wl, wd, me, ml, md = widths = [2 * f + 512, 4 * h + 1024, f + 256, 2 * d, 4 * d, d]
    early = scatter_sum(keep_e, send_e, [we, me], z)
    got_d = swap(after(part_d, got_s, far_s, early), "mp", 1)
    *part_f, keep_l, send_l, grad_hidden = back(
        core, part_s, got_s, part_o, got_o, tokens, cotangent, gain2, mag_o, fo, io, right_output, do, yo,
        (aq, ak, av), (lq, lk, lv), cosine, sine, (right_query, right_key, right_value), (fq, fk, fv), (iq, ik, iv),
        (dq, dk, dv), (mag_q, mag_k, mag_v), lo, (s_d, far_s, idn, mag_d, right_down, dd, td, ld, tl),
        (q, k, v), probs, mix, first, (w_query, w_key, w_value, w_output, down),
    )
    part_f[0], keep_l, send_l, got_d, early = lax.optimization_barrier((part_f[0], keep_l, send_l, got_d, early))
    got_f = [swap(part_f[0], "mp", 1)]
    layer_out = layer_end(tokens, part_o, got_o, fo, part_d, got_d, fd)
    late = scatter_sum(keep_l, send_l, [wl, wd, ml, md], z, got_f[0], layer_out)
    cut_e, cut_l = we // 8, (wl + wd) // 8
    part = jnp.concatenate([early[:, :cut_e], late[:, :cut_l], early[:, cut_e:], late[:, cut_l:]], axis=1)
    got = [swap(part, "y", k) for k in range(1, 4)]
    got_f.append(swap(after(part_f[1], got_f[0]), "mp", 1))
    part = after(part, got_f[1])
    part = tree([part.astype(F32)] + [x.astype(F32) for x in got]).astype(BF16)
    mixed = part[:, cut_e + cut_l :]
    far, near, across = swap(part, "xh", 1), swap(mixed, "mp", 1), swap(mixed, ("xh", "mp"), 3)
    got_f.append(swap(after(part_f[2], far, near, across), "mp", 1))
    grad_tokens = token_end(tokens, grad_hidden, part_f, got_f, gain1)
    total = part.astype(F32) + far.astype(F32)
    other = near.astype(F32) + across.astype(F32)
    part = jnp.concatenate([total[:, : cut_e + cut_l], total[:, cut_e + cut_l :] + other], axis=1).astype(BF16)
    half = joined(z, [after(part, got_f[2])] + [swap(part, "z", k) for k in range(1, 4)], widths)
    vec_e, at_l = 2 * f, we
    vec_l, at_d = at_l + 4 * h, at_l + wl
    at_me = at_d + wd
    at_ml = at_me + 2 * d
    at_md = at_ml + 4 * d
    places = [
        (at_ml, d, None), (at_l, h, None), (vec_l, h, 0),
        (at_ml + d, d, None), (at_l + h, h, None), (vec_l, h, 4),
        (at_ml + 2 * d, d, None), (at_l + 2 * h, h, None), (vec_l, h, 8),
        (at_l + 3 * h, h, None), (at_ml + 3 * d, d, None), (vec_l + 256, d, 0),
        (at_me, d, None), (0, f, None), (vec_e, f, 0),
        (at_me + d, d, None), (f, f, None), (vec_e + 256, f, 0),
        (at_d, f, None), (at_md, d, None), (at_d + f, d, 0),
    ]
    outs = unpack(core, half, swap(half, "core", 1), widths, places)
    outs = [x.reshape(-1) if i % 3 == 2 else x.T if i % 3 == 0 else x for i, x in enumerate(outs)]
    return (layer_out, grad_tokens, *outs)


def solution(mesh):
    fine = Mesh(mesh.devices.reshape(4, 2, 4, 2, 2), ("y", "xh", "z", "core", "mp"))
    col, row, vec, rep = P(None, "mp"), P("mp", None), P("mp"), P()
    tok = P(DP, None)
    split, merged = (rep, col, vec), (row, rep, rep)
    return jax.shard_map(
        body,
        mesh=fine,
        in_specs=(tok, P(DP), tok, rep, rep, col, col, col, row, col, col, P(("mp",) + DP, None))
        + split * 3 + merged + split * 2 + merged,
        out_specs=(tok, tok) + split * 3 + merged + split * 2 + merged,
        check_vma=False,
    )
```

```python
import functools
import jax
import jax.numpy as jnp
import numpy as np
from jax import lax
from jax.experimental import pallas as pl
from jax.experimental.pallas import tpu as pltpu
from jax.sharding import Mesh, PartitionSpec as P

HEAD_DIM = 128
RANK = 16
RATIO = 2.0
EPSILON = 1e-05
STATS_WIDTH = 1536
PARTS = (96, 96, 64)
F32 = jnp.float32
BF16 = jnp.bfloat16
DP = ("y", "xh", "z", "core")
ANY = pl.BlockSpec(memory_space=pl.ANY)
SMEM = pl.BlockSpec(memory_space=pltpu.SMEM)
VMEM = pl.BlockSpec(memory_space=pltpu.VMEM)
MIB = 1024 * 1024


def dot(a, b, dims=((1,), (0,))):
    return lax.dot_general(a.astype(BF16), b.astype(BF16), (dims, ((), ())), preferred_element_type=F32)


def dot_nt(a, b):
    return dot(a, b, ((1,), (1,)))


def dot_tn(a, b):
    return dot(a, b, ((0,), (0,)))


def col_sum(v):
    return jnp.sum(v, axis=0, keepdims=True)


def chunks(n, size):
    return [slice(r, min(r + size, n)) for r in range(0, n, size)]


def shape(dims, dtype=F32):
    return jax.ShapeDtypeStruct(dims, dtype)


def row_of(ref, lanes):
    return jnp.concatenate([ref[i : i + 1, :] for i in range(lanes.start // 128, lanes.stop // 128)], axis=1)


def rows_of(height, width):
    return pl.BlockSpec((height, width), lambda j: (j, 0))


def full(x):
    return pl.BlockSpec(x.shape, lambda j, r=len(x.shape): (0,) * r, pipeline_mode=pl.Buffered(1))


def call(kernel, ins, outs, scratch, name, work, traffic, grid=1, mib=60, alias=None):
    return pl.pallas_call(
        kernel,
        grid=(grid,),
        in_specs=[full(x) if block is None else block for x, block in ins],
        out_specs=[full(x) if block is None else block for x, block in outs],
        out_shape=[x for x, _ in outs],
        scratch_shapes=scratch,
        input_output_aliases=alias or {},
        compiler_params=pltpu.CompilerParams(vmem_limit_bytes=mib * MIB),
        cost_estimate=pl.CostEstimate(flops=int(work), bytes_accessed=int(traffic), transcendentals=0),
        name=name,
    )(*[x for x, _ in ins])


class Copies:
    def __init__(self, sems):
        self.sems, self.used, self.waiting = sems, 0, {}

    def start(self, key, src, dst):
        copy = pltpu.make_async_copy(src, dst, self.sems.at[self.used])
        self.used += 1
        copy.start()
        self.waiting.setdefault(key, []).append(copy)

    def wait(self, key):
        for copy in self.waiting.pop(key, []):
            copy.wait()

    def finish(self):
        for key in list(self.waiting):
            self.wait(key)


def deal(core_ref, arrays, keep_ref, send_ref):
    for side in range(2):
        @pl.when(core_ref[0] == side)
        def _():
            at = 0
            for ref in arrays:
                w = ref.shape[1] // 2
                keep_ref[:, at : at + w] = ref[:, side * w : (side + 1) * w]
                send_ref[:, at : at + w] = ref[:, (1 - side) * w : (2 - side) * w]
                at += w


def sems(n):
    return pltpu.SemaphoreType.DMA((n,))


def square_sum(w_ref, lanes):
    depth = w_ref.shape[0]
    width = lanes.stop - lanes.start
    if depth % 128:
        v = w_ref[:, lanes].astype(F32)
        return col_sum(v * v)
    parts = []
    for c in chunks(width, 256):
        to = slice(lanes.start + c.start, lanes.start + c.stop)
        squares = jnp.zeros((8, c.stop - c.start), F32)
        for r in chunks(depth, 64):
            chunk = w_ref[r, to].astype(F32)
            squares = squares + jnp.sum((chunk * chunk).reshape(8, 8, c.stop - c.start), axis=0)
        parts.append(col_sum(squares))
    return jnp.concatenate(parts, axis=1)


def stats_kernel(kinds, *refs):
    count = len(kinds)
    w_refs, rest = refs[:count], list(refs[count:])
    ins = [[rest.pop(0) for _ in range(3 if whole else 2)] for whole in kinds]
    outs = [[rest.pop(0) for _ in range(3 if whole else 2)] for whole in kinds]
    bufs, sem = rest[:count], rest[count]
    copies = Copies(sem)
    todo = sorted((lanes.start, i, lanes) for i, w in enumerate(w_refs) for lanes in chunks(w.shape[1], STATS_WIDTH))
    for start, i, lanes in todo:
        copies.start((i, start), w_refs[i].at[:, lanes], bufs[i].at[:, lanes])
    lefts = [x[0][...].astype(BF16) for x in ins]
    grams = [dot_nt(left, left) for left in lefts]
    for start, i, lanes in todo:
        copies.wait((i, start))
        right = ins[i][1][:, lanes]
        lw = dot(lefts[i], bufs[i][:, lanes])
        ld = lw + RATIO * dot(grams[i], right)
        total = square_sum(bufs[i], lanes) + RATIO * col_sum(right * (lw + ld))
        if kinds[i]:
            fac_ref, isq_ref, ld_ref = outs[i]
            isq_ref[:, lanes] = 1.0 / total
            fac_ref[:, lanes] = row_of(ins[i][2], lanes) * lax.rsqrt(total)
        else:
            total_ref, ld_ref = outs[i]
            total_ref[:, lanes] = total
        ld_ref[:, lanes] = ld


def stats(projections):
    kinds = [p[3] is not None for p in projections]
    ins = [(p[0], ANY) for p in projections]
    outs = []
    for (w, left, right, mag), whole in zip(projections, kinds):
        ins += [(left, None), (right, None)] + ([(mag, None)] if whole else [])
        outs += [(shape((1, w.shape[1])), None)] * (2 if whole else 1) + [(shape((RANK, w.shape[1])), None)]
    size = sum(p[0].size for p in projections)
    scratch = [pltpu.VMEM(p[0].shape, BF16) for p in projections] + [sems(16)]
    flat = call(functools.partial(stats_kernel, kinds), ins, outs, scratch, "stats", 2 * RANK * size, 2 * size)
    given = []
    for whole in kinds:
        n = 3 if whole else 2
        given.append(flat[:n])
        flat = flat[n:]
    return given


def unit_rows(v):
    return lax.rsqrt(jnp.mean(v * v, axis=-1, keepdims=True) + EPSILON)


def rotate(v, cosine, sine):
    return v * cosine + pltpu.roll(v, HEAD_DIM // 2, 1) * sine


def attend_kernel(
    length_ref, x_ref, gain_ref, lq_ref, lk_ref, lv_ref, cos_ref, sin_ref, ro_ref, rq_ref, rk_ref, rv_ref, fq_ref, fk_ref, fv_ref, lo_ref,
    wq_ref, wk_ref, wv_ref, wo_ref,
    part_ref, aq_ref, ak_ref, av_ref, yo_ref, first_out, q_out, k_out, v_out, probs_out, mix_out,
    wq, wk, wv, wo, first, q, k, v, probs, mix, sem,
):
    n, d = x_ref.shape
    copies = Copies(sem)
    groups = chunks(wq_ref.shape[1], 256)
    head, rest = groups[0], slice(groups[1].start, groups[-1].stop)
    for key, lanes in (("head", head), ("rest", rest)):
        for w, src in ((wq, wq_ref), (wk, wk_ref), (wv, wv_ref)):
            copies.start(key, src.at[:, lanes], w.at[:, lanes])
    copies.start("rest", wo_ref, wo)
    everything = slice(0, d)
    gain = row_of(gain_ref, everything)
    for r in chunks(n, 16):
        x = x_ref[r, :].astype(F32)
        first[r, :] = (x * unit_rows(x) * gain).astype(BF16)
    for left, out in ((lq_ref, aq_ref), (lk_ref, ak_ref), (lv_ref, av_ref)):
        out[...] = dot_nt(first[...], left[...]).astype(BF16)
    cosine, sine = cos_ref[...], sin_ref[...]
    row = lax.broadcasted_iota(jnp.int32, (n, n), 0)
    col = lax.broadcasted_iota(jnp.int32, (n, n), 1)
    allowed = (col <= row) & (col < length_ref[0])

    def project(lanes):
        def one(w, a, right, fac):
            return (dot(first[...], w[:, lanes]) + RATIO * dot(a[...], right[:, lanes])) * fac[:, lanes]

        vq, vk = one(wq, aq_ref, rq_ref, fq_ref), one(wk, ak_ref, rk_ref, fk_ref)
        v[:, lanes] = one(wv, av_ref, rv_ref, fv_ref).astype(BF16)
        for h in chunks(256, HEAD_DIM):
            to = slice(lanes.start + h.start, lanes.start + h.stop)
            q[:, to] = (rotate(vq[:, h], cosine, sine) * HEAD_DIM**-0.5).astype(BF16)
            k[:, to] = rotate(vk[:, h], cosine, sine).astype(BF16)

    def attention(lanes):
        for h in chunks(256, HEAD_DIM):
            at = slice(lanes.start + h.start, lanes.start + h.stop)
            i = at.start // HEAD_DIM
            scores = jnp.where(allowed, dot_nt(q[:, at], k[:, at]), -1e30)
            e = jnp.exp(scores - jnp.max(scores, axis=-1, keepdims=True))
            probs[i] = (e * (1.0 / jnp.sum(e, axis=-1, keepdims=True))).astype(BF16)
            mix[:, at] = dot(probs[i], v[:, at]).astype(BF16)

    copies.wait("head")
    project(head)
    copies.wait("rest")
    for i, lanes in enumerate(groups):
        if i + 1 < len(groups):
            project(groups[i + 1])
        attention(lanes)
    for src, dst in ((first, first_out), (q, q_out), (k, k_out), (v, v_out), (probs, probs_out), (mix, mix_out)):
        copies.start("end", src, dst)
    yo_ref[...] = dot_nt(mix[...], lo_ref[...]).astype(BF16)
    for lanes in chunks(d, 512):
        part_ref[:, lanes] = (dot(mix[...], wo[:, lanes]) + RATIO * dot(yo_ref[...], ro_ref[:, lanes])).astype(BF16)
    copies.finish()


def attend(length, tokens, gain, lefts, cosine, sine, right_o, rights, facs, left_o, weights):
    n, d = tokens.shape
    h = weights[0].shape[1]
    heads = h // HEAD_DIM
    ins = [(length, SMEM)] + [(x, None) for x in (tokens, gain, *lefts, cosine, sine, right_o, *rights, *facs, left_o)]
    ins += [(w, ANY) for w in weights]
    outs = [(shape((n, d), BF16), None)] + [(shape((n, RANK), BF16), None)] * 4 + [(shape((n, d), BF16), ANY)]
    outs += [(shape((n, h), BF16), ANY)] * 3 + [(shape((heads, n, n), BF16), ANY), (shape((n, h), BF16), ANY)]
    scratch = [pltpu.VMEM(w.shape, BF16) for w in weights] + [pltpu.VMEM((n, d), BF16)] + [pltpu.VMEM((n, h), BF16)] * 3
    scratch += [pltpu.VMEM((heads, n, n), BF16), pltpu.VMEM((n, h), BF16), sems(64)]
    return call(attend_kernel, ins, outs, scratch, "attend", 8 * n * d * h, 8 * d * h)


def mlp_kernel(core_ref, xh_ref, *refs):
    ins, refs = refs[:21], refs[21:]
    raw_ref, wg_ref, wu_ref, ps_ref, zd_ref, keep_ref, send_ref, act_out, wd_out, *refs = refs
    bufs, refs = refs[:21], refs[21:]
    raw, act, wd, wg, wu, gv, uv, av, second, gpd, gpg, gpu, cg, cu, loc_ref, mix_ref, sem = refs
    (
        x_ref, own_ref, got_ref, fo_ref, gain_ref, cot_ref, fd_ref, rd_ref, lg_ref, lu_ref, ldt_ref,
        rg_ref, ru_ref, fg_ref, fu_ref, ig_ref, iu_ref, dg_ref, du_ref, mg_ref, mu_ref,
    ) = bufs
    n, d = cot_ref.shape
    f = wd.shape[0]
    slots, each = raw.shape[0], raw.shape[1]
    pieces, height = raw_ref.shape[0], raw_ref.shape[1] // 2
    per = slots // 2
    rounds = pieces // (each * per)
    copies = Copies(sem)
    groups = chunks(f, 256)
    bounds = [(i * f // rounds) // 256 for i in range(rounds)] + [len(groups)]

    def fetch_weights(i):
        lanes = slice(bounds[i] * 256, bounds[i + 1] * 256)
        copies.start(("w", i), wg_ref.at[:, lanes], wg.at[:, lanes])
        copies.start(("w", i), wu_ref.at[:, lanes], wu.at[:, lanes])

    def fetch(i):
        for c in range(per * i, per * (i + 1)):
            copies.start(("raw", i), raw_ref.at[each * c : each * (c + 1)], raw.at[c % slots])
        if i:
            fetch_weights(i)

    ahead = (0, 1, 2, 3, 4, 8, 9, 11, 12)
    for i in ahead:
        copies.start("ahead", ins[i], bufs[i])
    fetch_weights(0)
    for i in range(len(ins)):
        if i not in ahead:
            copies.start("in", ins[i], bufs[i])
    fetch(0)
    fetch(1)
    copies.wait("ahead")
    gain, fo = row_of(gain_ref, slice(0, d)), fo_ref[...]
    for r in chunks(n, 16):
        hidden = x_ref[r, :].astype(F32) + (own_ref[r, :].astype(F32) + got_ref[r, :].astype(F32)) * fo
        second[r, :] = (hidden * unit_rows(hidden) * gain).astype(BF16)
    ag = dot_nt(second[...], lg_ref[...]).astype(BF16)
    au = dot_nt(second[...], lu_ref[...]).astype(BF16)
    ag2, au2 = ag * RATIO, au * RATIO

    def forward(j):
        lanes, slot = groups[j], j % 2
        gv[slot] = dot(second[...], wg[:, lanes]) + dot(ag2, rg_ref[:, lanes])
        uv[slot] = dot(second[...], wu[:, lanes]) + dot(au2, ru_ref[:, lanes])

    copies.wait(("w", 0))
    for j in range(bounds[1]):
        forward(j)
    copies.wait("in")
    fd = fd_ref[...]
    for r in chunks(n, 16):
        gpd[r, :] = (cot_ref[r, :].astype(F32) * fd).astype(BF16)
    zd = dot_nt(gpd[...], rd_ref[...]).astype(BF16)
    zd_ref[...] = zd
    zd2 = zd * RATIO

    def compact(c):
        y, half = c // 2, c % 2
        for side in range(2):
            at = (y * 16 + half * 4) * height + (xh_ref[0] ^ side) * (8 * height)
            block = jnp.concatenate([raw[c % slots, i, side * height : (side + 1) * height] for i in range(each)], axis=0)
            wd[pl.ds(pl.multiple_of(at, 16), 4 * height), :] = block

    def products(j):
        lanes, slot = groups[j], j % 2
        if j >= bounds[1]:
            forward(j)
        av[slot] = dot_nt(gpd[...], wd[lanes, :]) + dot(zd2, ldt_ref[:, lanes])

    def gates(j):
        lanes, slot = groups[j], j % 2
        fg, fu = fg_ref[:, lanes], fu_ref[:, lanes]
        sum_g, sum_u = jnp.zeros((8, 256), F32), jnp.zeros((8, 256), F32)
        for r in chunks(n, 16):
            g, u, grad_act = gv[slot, r, :] * fg, uv[slot, r, :] * fu, av[slot, r, :]
            sig = 1.0 / (1.0 + jnp.exp(-g))
            silu = g * sig
            act[r, lanes] = (silu * u).astype(BF16)
            grad_gate = grad_act * u * (sig + silu * (1.0 - sig))
            grad_up = grad_act * silu
            gpg[r, lanes] = (grad_gate * fg).astype(BF16)
            gpu[r, lanes] = (grad_up * fu).astype(BF16)
            prod_g, prod_u = grad_gate * g, grad_up * u
            sum_g = sum_g + prod_g[:8] + prod_g[8:]
            sum_u = sum_u + prod_u[:8] + prod_u[8:]
        for total, right, isq, gp, nc in ((sum_g, rg_ref, ig_ref, gpg, cg), (sum_u, ru_ref, iu_ref, gpu, cu)):
            s = col_sum(total)
            nc[:, lanes] = s
            gp[n:, lanes] = (-s * isq[:, lanes] * right[:, lanes]).astype(BF16)

    for i in range(rounds):
        copies.wait(("raw", i))
        copies.wait(("w", i))
        for c in range(per * i, per * (i + 1)):
            compact(c)
        if i + 2 < rounds:
            fetch(i + 2)
        for j in range(bounds[i], bounds[i + 1]):
            products(j)
            if j > bounds[i]:
                gates(j - 1)
        gates(bounds[i + 1] - 1)
    copies.start("end", wd, wd_out)
    copies.start("end", act, act_out)
    for i, (a, gp, isq, ld, mag, nc) in enumerate(((ag, gpg, ig_ref, dg_ref, mg_ref, cg), (au, gpu, iu_ref, du_ref, mu_ref, cu))):
        s = nc[...]
        loc_ref[:, i * f : (i + 1) * f] = (RATIO * (dot_tn(a, gp[:n, :]) - ld[...] * (s * isq[...]))).astype(BF16)
        v = s / row_of(mag, slice(0, f))
        rows = [v[:, lanes] for lanes in groups] + [jnp.zeros((RANK - len(groups), 256), F32)]
        loc_ref[:, 2 * f + 256 * i : 2 * f + 256 * (i + 1)] = jnp.concatenate(rows, axis=0).astype(BF16)
    sides = ((gpg, rg_ref, lg_ref, wg), (gpu, ru_ref, lu_ref, wu))
    zs = [dot_nt(gp[...], right[...]).astype(BF16) for gp, right, _, _ in sides]
    for lanes in chunks(d, 512):
        both = [dot_nt(gp[...], w[lanes, :]) for gp, _, _, w in sides]
        low = sum(dot(z, left[:, lanes]) for z, (_, _, left, _) in zip(zs, sides))
        ps_ref[:, lanes] = (both[0][:n] + both[1][:n] + RATIO * low[:n]).astype(BF16)
        for i, (part, z, (_, _, left, _)) in enumerate(zip(both, zs, sides)):
            out = dot_tn(z[:n], second[:, lanes]) + part[n:] + RATIO * dot(z[n:], left[:, lanes])
            mix_ref[:, i * d + lanes.start : i * d + lanes.stop] = (RATIO * out).astype(BF16)
    deal(core_ref, (loc_ref, mix_ref), keep_ref, send_ref)
    copies.finish()


def mlp(core, xh, tokens, own, got, fac_o, gain, cot, fac_d, right_d, lefts, left_dt, rights, facs, isqs, lds, mags, raw, weights):
    n, d = cot.shape
    f = weights[0].shape[1]
    given = (tokens, own, got, fac_o, gain, cot, fac_d, right_d, *lefts, left_dt, *rights, *facs, *isqs, *lds, *mags)
    ins = [(core, SMEM), (xh, SMEM)] + [(x, ANY) for x in (*given, raw, *weights)]
    wide = 2 * f + 512
    outs = [(shape((n, d), BF16), None), (shape((n, RANK), BF16), None)] + [(shape((RANK, wide // 2 + d), BF16), VMEM)] * 2
    outs += [(shape((n, f), BF16), ANY), (shape((f, d), BF16), ANY)]
    scratch = [pltpu.VMEM(x.shape, x.dtype) for x in given] + [
        pltpu.VMEM((4, 4, *raw.shape[1:]), BF16), pltpu.VMEM((n, f), BF16), pltpu.VMEM((f, d), BF16),
        pltpu.VMEM((d, f), BF16), pltpu.VMEM((d, f), BF16), *[pltpu.VMEM((2, n, 256), F32)] * 3,
        pltpu.VMEM((n, d), BF16), pltpu.VMEM((n, d), BF16), pltpu.VMEM((n + RANK, f), BF16), pltpu.VMEM((n + RANK, f), BF16),
        pltpu.VMEM((1, f), F32), pltpu.VMEM((1, f), F32), pltpu.VMEM((RANK, wide), BF16), pltpu.VMEM((RANK, 2 * d), BF16), sems(48),
    ]
    return call(mlp_kernel, ins, outs, scratch, "mlp", 10 * n * d * f, 6 * d * f, mib=62)


def down_kernel(ldt_ref, fd_ref, rd_ref, zd_ref, act_ref, cot_ref, wd_ref, pd_ref, sd_ref, dd_ref, td_ref, tl_ref, wd, lhs, cot_buf, sem):
    n, f = act_ref.shape
    d = cot_ref.shape[1]
    copies = Copies(sem)
    groups = chunks(d, 512)
    copies.start("act", act_ref, lhs.at[:n, :])
    for lanes in groups:
        copies.start(lanes.start, wd_ref.at[:, lanes], wd.at[:, lanes])
        copies.start(lanes.start, cot_ref.at[:, lanes], cot_buf.at[:, lanes])
    lhs[n:, :] = ldt_ref[...].astype(BF16)
    copies.wait("act")
    low = dot_nt(lhs[...], ldt_ref[...]).astype(BF16)
    tl_ref[...] = dot_tn(zd_ref[...], lhs[:n, :])
    for lanes in groups:
        copies.wait(lanes.start)
        out = dot(lhs[...], wd[:, lanes]) + RATIO * dot(low, rd_ref[:, lanes])
        pd = out[:n].astype(BF16)
        pd_ref[:, lanes] = pd
        dd_ref[:, lanes] = out[n:]
        cot = cot_buf[:, lanes].astype(F32)
        sd_ref[:, lanes] = col_sum(cot * pd.astype(F32)) * fd_ref[:, lanes]
        td_ref[:, lanes] = dot_tn(low[:n], cot * fd_ref[:, lanes])


def down_forward(act, left_dt, cot, fac_d, right_d, zd, w_down):
    n, f = act.shape
    d = cot.shape[1]
    ins = [(x, None) for x in (left_dt, fac_d, right_d, zd)] + [(x, ANY) for x in (act, cot, w_down)]
    outs = [(shape((n, d), BF16), None), (shape((1, d)), None), (shape((RANK, d)), None), (shape((RANK, d)), None), (shape((RANK, f)), None)]
    scratch = [pltpu.VMEM((f, d), BF16), pltpu.VMEM((n + RANK, f), BF16), pltpu.VMEM((n, d), BF16), sems(16)]
    return call(down_kernel, ins, outs, scratch, "down_forward", 2 * n * d * f, 2 * d * f)


def correct_kernel(s0_ref, s1_ref, isq_ref, mag_ref, rd_ref, dd_ref, td_ref, ldt_ref, tl_ref, wd_ref, loc_ref, mix_ref, wd, sem):
    f, d = wd.shape
    copies = Copies(sem)
    groups = chunks(f, 1024)
    for rows in groups:
        copies.start(rows.start, wd_ref.at[rows, :], wd.at[rows, :])
    s = s0_ref[...] + s1_ref[...]
    ncoef = -s * isq_ref[...]
    nr = (ncoef * rd_ref[...]).astype(BF16)
    m = dot_nt(nr, rd_ref[...])
    mix_ref[:, :d] = (RATIO * (td_ref[...] + dd_ref[...] * ncoef)).astype(BF16)
    v = 0.5 * s / row_of(mag_ref, slice(0, d))
    rows = [v[:, lanes] for lanes in chunks(d, 256)]
    mix_ref[:, d : d + 256] = jnp.concatenate(rows + [jnp.zeros((RANK - len(rows), 256), F32)], axis=0).astype(BF16)
    mix_ref[:, d + 256 :] = jnp.zeros((RANK, mix_ref.shape[1] - d - 256), BF16)
    loc_ref[:, f:] = jnp.zeros((RANK, loc_ref.shape[1] - f), BF16)
    for rows in groups:
        copies.wait(rows.start)
        out = tl_ref[:, rows] + dot_nt(nr, wd[rows, :]) + RATIO * dot(m, ldt_ref[:, rows])
        loc_ref[:, rows] = (RATIO * out).astype(BF16)


def down_correction(s0, s1, isq, mag, right_d, dd, td, left_dt, tl, w_down):
    f, d = w_down.shape
    ins = [(x, None) for x in (s0, s1, isq, mag, right_d, dd, td, left_dt, tl)] + [(w_down, ANY)]
    outs = [(shape((RANK, f + 256), BF16), None), (shape((RANK, d + 1024), BF16), None)]
    scratch = [pltpu.VMEM((f, d), BF16), sems(4)]
    return call(correct_kernel, ins, outs, scratch, "down_correction", 2 * RANK * d * f, 2 * d * f)


def back_kernel(
    core_ref, gain_ref, mo_ref, fo_ref, io_ref, ro_ref, do_ref, yo_ref,
    aq_ref, ak_ref, av_ref, lq_ref, lk_ref, lv_ref, cos_ref, sin_ref, rq_ref, rk_ref, rv_ref, fq_ref, fk_ref, fv_ref,
    iq_ref, ik_ref, iv_ref, dq_ref, dk_ref, dv_ref, mq_ref, mk_ref, mv_ref, lo_ref,
    locd_ref, mixd_ref,
    own_hbm, got_hbm, own_o_hbm, got_o_hbm, x_hbm, cot_hbm, q_ref, k_ref, v_ref, probs_ref, mix_ref, first_ref, wq_ref, wk_ref, wv_ref, wo_ref,
    pf0_ref, pf1_ref, pf2_ref, keep_ref, send_ref, gh_out,
    own_ref, got_ref, own_o_ref, got_o_ref, x_ref, cot_ref, q, k, v, probs, mix, first, wq, wk, wv, wo, gh, gpo, gpq, gpk, gpv, sq, sk, sv, loc_ref, mixed_ref, sem,
):
    n, d = x_ref.shape
    span = wq_ref.shape[1]
    copies = Copies(sem)
    groups = chunks(span, 256)
    for src, dst in ((own_o_hbm, own_o_ref), (got_o_hbm, got_o_ref), (x_hbm, x_ref), (own_hbm, own_ref), (got_hbm, got_ref), (cot_hbm, cot_ref)):
        copies.start(0, src.at[: n // 2, :], dst.at[: n // 2, :])
    for src, dst in ((own_o_hbm, own_o_ref), (got_o_hbm, got_o_ref), (x_hbm, x_ref), (own_hbm, own_ref), (got_hbm, got_ref), (cot_hbm, cot_ref)):
        copies.start(n // 2, src.at[n // 2 :, :], dst.at[n // 2 :, :])
    copies.start("heads", wo_ref, wo)
    for src, dst in ((q_ref, q), (k_ref, k), (v_ref, v), (probs_ref, probs)):
        copies.start("heads", src, dst)
    for src, dst in ((wq_ref, wq), (wk_ref, wk), (wv_ref, wv)):
        copies.start("late", src, dst)
    copies.start("late", mix_ref, mix)
    copies.start("late", first_ref, first)
    gain, fo = row_of(gain_ref, slice(0, d)), fo_ref[...]
    sums = jnp.zeros((8, d), F32)
    for r in chunks(n, 16):
        copies.wait(r.start)
        value = (own_o_ref[r, :].astype(F32) + got_o_ref[r, :].astype(F32)) * fo
        hidden = x_ref[r, :].astype(F32) + value
        inverse = unit_rows(hidden)
        unit = hidden * inverse
        w2 = (own_ref[r, :].astype(F32) + got_ref[r, :].astype(F32)) * gain
        grad = cot_ref[r, :].astype(F32) + inverse * (w2 - unit * jnp.mean(w2 * unit, axis=-1, keepdims=True))
        gh[r, :] = grad
        gpo[r, :] = (grad * fo).astype(BF16)
        both = grad * value
        sums = sums + both[:8] + both[8:]
    copies.start("end", gh, gh_out)
    so = col_sum(sums)
    ncoef = -so * io_ref[...]
    gpo[n:, :] = (ncoef * ro_ref[...]).astype(BF16)
    zo = dot_nt(gpo[...], ro_ref[...]).astype(BF16)
    mixed_ref[:, 3 * d :] = (RATIO * (dot_tn(yo_ref[...], gpo[:n, :]) + do_ref[...] * ncoef)).astype(BF16)
    cosine, sine = cos_ref[...], -sin_ref[...]
    scale = HEAD_DIM**-0.5
    parts_o = []
    copies.wait("heads")
    for lanes in groups:
        both = dot_nt(gpo[...], wo[lanes, :]) + RATIO * dot(zo, lo_ref[:, lanes])
        grad_attn = both[:n].astype(BF16)
        parts_o.append(both[n:])
        for h in chunks(256, HEAD_DIM):
            at = slice(lanes.start + h.start, lanes.start + h.stop)
            ga, p_low = grad_attn[:, h], probs[at.start // HEAD_DIM]
            p = p_low.astype(F32)
            gprobs = dot_nt(ga, v[:, at])
            gscores = (p * (gprobs - jnp.sum(p * gprobs, axis=-1, keepdims=True))).astype(BF16)
            gq = rotate(dot(gscores, k[:, at]), cosine, sine) * scale
            gk = rotate(dot_tn(gscores, q[:, at]), cosine, sine)
            gv = dot_tn(p_low, ga)
            vq = rotate(q[:, at].astype(F32), cosine, sine) * (1.0 / scale)
            vk = rotate(k[:, at].astype(F32), cosine, sine)
            for grad, val, fac, isq, right, gp, s_ref in (
                (gq, vq, fq_ref, iq_ref, rq_ref, gpq, sq),
                (gk, vk, fk_ref, ik_ref, rk_ref, gpk, sk),
                (gv, v[:, at].astype(F32), fv_ref, iv_ref, rv_ref, gpv, sv),
            ):
                s = col_sum(grad * val)
                s_ref[:, at] = s
                gp[:n, at] = (grad * fac[:, at]).astype(BF16)
                gp[n:, at] = (-s * isq[:, at] * right[:, at]).astype(BF16)
    sides = ((gpq, rq_ref, lq_ref, wq), (gpk, rk_ref, lk_ref, wk), (gpv, rv_ref, lv_ref, wv))
    zs = [dot_nt(gp[...], right[...]).astype(BF16) for gp, right, _, _ in sides]
    copies.wait("late")
    for lanes in chunks(d, 512):
        both = [dot_nt(gp[...], w[lanes, :]) for gp, _, _, w in sides]
        low = sum(dot(z, left[:, lanes]) for z, (_, _, left, _) in zip(zs, sides))
        pf = (both[0][:n] + both[1][:n] + both[2][:n] + RATIO * low[:n]).astype(BF16)
        at = 0
        for ref in (pf0_ref, pf1_ref, pf2_ref):
            ref[:, lanes] = pf[at : at + ref.shape[0]]
            at += ref.shape[0]
        for i, (part, z, (_, _, left, _)) in enumerate(zip(both, zs, sides)):
            out = dot_tn(z[:n], first[:, lanes]) + part[n:] + RATIO * dot(z[n:], left[:, lanes])
            mixed_ref[:, i * d + lanes.start : i * d + lanes.stop] = (RATIO * out).astype(BF16)
    rows = []
    for i, (a, gp, isq, ld, mag, s_ref) in enumerate((
        (aq_ref, gpq, iq_ref, dq_ref, mq_ref, sq), (ak_ref, gpk, ik_ref, dk_ref, mk_ref, sk), (av_ref, gpv, iv_ref, dv_ref, mv_ref, sv),
    )):
        s = s_ref[...]
        loc_ref[:, i * span : (i + 1) * span] = (RATIO * (dot_tn(a[...], gp[:n, :]) - ld[...] * (s * isq[...]))).astype(BF16)
        v_row = s / row_of(mag, slice(0, span))
        rows += [v_row[:, lanes] for lanes in groups]
    out = dot_tn(zo[:n], mix[...]) + jnp.concatenate(parts_o, axis=1)
    loc_ref[:, 3 * span : 4 * span] = (RATIO * out).astype(BF16)
    v_row = so / row_of(mo_ref, slice(0, d))
    more = [v_row[:, lanes] for lanes in chunks(d, 256)]
    tiles = []
    for some in (rows, more):
        tiles.append(jnp.concatenate(some + [jnp.zeros((RANK - len(some), 256), F32)], axis=0))
    loc_ref[:, 4 * span :] = jnp.concatenate(tiles + [jnp.zeros((RANK, 512), F32)], axis=1).astype(BF16)
    deal(core_ref, (loc_ref, locd_ref, mixed_ref, mixd_ref), keep_ref, send_ref)
    copies.finish()


def back(
    core, own, got, own_o, got_o, tokens, cot, gain, mag_o, fac_o, isq_o, right_o, ld_o, yo, als, lefts, cosine, sine,
    rights, facs, isqs, lds, mags, left_o, downs, qkv, probs, mix, first, weights,
):
    n, d = tokens.shape
    h = weights[0].shape[1]
    ins = [(core, SMEM)] + [(x, None) for x in (gain, mag_o, fac_o, isq_o, right_o, ld_o, yo)]
    ins += [(x, None) for x in (*als, *lefts, cosine, sine, *rights, *facs, *isqs, *lds, *mags, left_o, *downs)]
    ins += [(x, ANY) for x in (own, got, own_o, got_o, tokens, cot, *qkv, probs, mix, first, *weights)]
    wides = (4 * h + 1024, 4 * d)
    outs = [(shape((part, d), BF16), None) for part in PARTS]
    outs += [(shape((RANK, (sum(wides) + sum(x.shape[1] for x in downs)) // 2), BF16), VMEM)] * 2 + [(shape((n, d)), ANY)]
    head = pltpu.VMEM((n, h), BF16)
    scratch = [pltpu.VMEM((n, d), BF16)] * 6 + [head] * 3 + [pltpu.VMEM(probs.shape, BF16), head, pltpu.VMEM((n, d), BF16)] + [pltpu.VMEM(w.shape, BF16) for w in weights]
    scratch += [pltpu.VMEM((n, d), F32), pltpu.VMEM((n + RANK, d), BF16)] + [pltpu.VMEM((n + RANK, h), BF16)] * 3
    scratch += [pltpu.VMEM((1, h), F32)] * 3 + [pltpu.VMEM((RANK, w), BF16) for w in wides] + [sems(40)]
    return call(back_kernel, ins, outs, scratch, "back", 8 * n * d * h, 8 * d * h)


def layer_kernel(x_ref, own_o_ref, got_o_ref, fo_ref, own_ref, got_ref, fd_ref, out_ref):
    for r in chunks(x_ref.shape[0], 16):
        hidden = x_ref[r, :].astype(F32) + (own_o_ref[r, :].astype(F32) + got_o_ref[r, :].astype(F32)) * fo_ref[...]
        out_ref[r, :] = (hidden + (own_ref[r, :].astype(F32) + got_ref[r, :].astype(F32)) * fd_ref[...]).astype(BF16)


def layer_end(tokens, own_o, got_o, fac_o, own, got, fac_d):
    n, d = tokens.shape
    block = rows_of(128, d)
    ins = [(tokens, block), (own_o, block), (got_o, block), (fac_o, None), (own, block), (got, block), (fac_d, None)]
    return call(layer_kernel, ins, [(shape((n, d), BF16), block)], [], "layer_end", 6 * n * d, 12 * n * d, n // 128)[0]


def token_kernel(first, count, *refs):
    x_hbm, gh_hbm, gain_ref, *refs = refs
    owns, gots, refs = refs[:count], refs[count : 2 * count], refs[2 * count :]
    out_hbm, x_buf, gh_buf, out_buf, sem = refs[-5:]
    rows = slice(first, first + x_buf.shape[0])
    copies = Copies(sem)
    copies.start("in", x_hbm.at[rows, :], x_buf)
    copies.start("in", gh_hbm.at[rows, :], gh_buf)
    gain = row_of(gain_ref, slice(0, x_buf.shape[1]))
    places = [(own, got, r) for own, got in zip(owns, gots) for r in chunks(own.shape[0], 16)]
    copies.wait("in")
    for r, (own, got, to) in zip(chunks(x_buf.shape[0], 16), places):
        x = x_buf[r, :].astype(F32)
        inverse = unit_rows(x)
        unit = x * inverse
        w1 = (own[to, :].astype(F32) + got[to, :].astype(F32)) * gain
        out_buf[r, :] = (gh_buf[r, :] + inverse * (w1 - unit * jnp.mean(w1 * unit, axis=-1, keepdims=True))).astype(BF16)
    copies.start("out", out_buf, out_hbm.at[rows, :])
    copies.finish()


def token_end(tokens, grad_hidden, gain, own, got, first, before=None):
    n, d = tokens.shape
    count = sum(x.shape[0] for x in own)
    ins = [(tokens, ANY), (grad_hidden, ANY), (gain, None)] + [(x, None) for x in (*own, *got)] + ([] if before is None else [(before, ANY)])
    scratch = [pltpu.VMEM((count, d), BF16), pltpu.VMEM((count, d), F32), pltpu.VMEM((count, d), BF16), sems(3)]
    alias = {} if before is None else {len(ins) - 1: 0}
    kernel = functools.partial(token_kernel, first, len(own))
    return call(kernel, ins, [(shape((n, d), BF16), ANY)], scratch, "token_end", 10 * count * d, 12 * count * d, alias=alias)[0]


def shard_kernel(w_ref, left_ref, right_ref, out_ref):
    left, right = left_ref[...], right_ref[...]
    lw = dot(left, w_ref[...])
    ld = lw + RATIO * dot(dot_nt(left, left), right)
    out_ref[...] = square_sum(w_ref, slice(0, w_ref.shape[1])) + RATIO * col_sum(right * (lw + ld))


def shard_stats(w, left, right):
    return call(shard_kernel, [(w, None), (left, None), (right, None)], [(shape((1, w.shape[1])), None)], [], "shard_stats", w.size, w.size)[0]


def quarters_kernel(pieces, z_ref, keep0_ref, got0_ref, keep1_ref, got1_ref, *refs):
    outs, totals = refs[:4], refs[4:]
    for total, keep_ref, got_ref in zip(totals, (keep0_ref, keep1_ref), (got0_ref, got1_ref)):
        total[...] = (keep_ref[...].astype(F32) + got_ref[...].astype(F32)).astype(BF16)
    to = 0
    for which, at, w in pieces:
        q = w // 8
        for k in range(4):
            start = at + (z_ref[0] ^ k) * q
            outs[k][:, to : to + q] = totals[which][:, pl.ds(pl.multiple_of(start, 128), q)]
        to += q


def quarters(z, keeps, gots, pieces):
    width = sum(w for _, _, w in pieces) // 8
    outs = [(shape((RANK, width), BF16), VMEM)] * 4
    ins = [(z, SMEM), (keeps[0], VMEM), (gots[0], VMEM), (keeps[1], VMEM), (gots[1], VMEM)]
    scratch = [pltpu.VMEM(x.shape, BF16) for x in keeps]
    return call(functools.partial(quarters_kernel, pieces), ins, outs, scratch, "quarters", 0, width, mib=16)


def joined_kernel(widths, z_ref, *refs):
    ins, out_ref = refs[:4], refs[4]
    at = to = 0
    for w in widths:
        q = w // 8
        for k in range(4):
            out_ref[:, pl.ds(pl.multiple_of(to + (z_ref[0] ^ k) * q, 128), q)] = ins[k][:, at : at + q]
        at += q
        to += w // 2


def joined(z, parts, widths):
    width = sum(widths) // 2
    ins = [(z, SMEM)] + [(x, VMEM) for x in parts]
    return call(functools.partial(joined_kernel, widths), ins, [(shape((RANK, width), BF16), VMEM)], [], "joined", 0, width, mib=16)[0]


def unpack_kernel(widths, places, core_ref, half_ref, got_ref, *refs):
    whole, outs = refs[-1], refs[:-1]
    for side in range(2):
        @pl.when(core_ref[0] == side)
        def _():
            at = to = 0
            for w in widths:
                h = w // 2
                whole[:, to + side * h : to + (side + 1) * h] = half_ref[:, at : at + h].astype(F32)
                whole[:, to + (1 - side) * h : to + (2 - side) * h] = got_ref[:, at : at + h].astype(F32)
                at += h
                to += w
    for out, (start, count, row) in zip(outs, places):
        if row is None:
            out[...] = whole[:, start : start + count]
        else:
            for i in range(count // 128):
                at = start + i % 2 * 128
                out[i : i + 1, :] = whole[row + i // 2 : row + i // 2 + 1, at : at + 128]


def unpack(core, half, got, widths, places):
    outs = [(shape((RANK, count) if row is None else (count // 128, 128)), None) for _, count, row in places]
    total = sum(widths)
    ins = [(core, SMEM), (half, VMEM), (got, VMEM)]
    return call(functools.partial(unpack_kernel, widths, places), ins, outs, [pltpu.VMEM((RANK, total), F32)], "unpack", 0, total, mib=32)


def swap(x, axis_name, k):
    n = lax.axis_size(axis_name)
    return lax.ppermute(x, axis_name, [(i, i ^ k) for i in range(n)])


def tree(parts):
    while len(parts) > 1:
        parts = [parts[i] + parts[i + 1] for i in range(0, len(parts), 2)]
    return parts[0]


def xor_sum(x, axis_name):
    n = lax.axis_size(axis_name)
    return tree([x] + [swap(x, axis_name, k) for k in range(1, n)])


def after(x, *others):
    return lax.optimization_barrier((x,) + others)[0]


def rope_tables(span):
    half = HEAD_DIM // 2
    frequency = 10000.0 ** (-(np.arange(half, dtype=np.float64) * 2.0) / HEAD_DIM)
    angles = np.arange(span, dtype=np.float64)[:, None] * frequency[None, :]
    cosine, sine = np.cos(angles), np.sin(angles)
    return np.concatenate([cosine, cosine], 1).astype(np.float32), np.concatenate([-sine, sine], 1).astype(np.float32)


def body(
    tokens, lengths, cotangent, gain_attn, gain_ffn,
    w_query, w_key, w_value, w_output, w_gate, w_up, w_down,
    left_query, right_query, mag_query,
    left_key, right_key, mag_key,
    left_value, right_value, mag_value,
    left_output, right_output, mag_output,
    left_gate, right_gate, mag_gate,
    left_up, right_up, mag_up,
    left_down, right_down, mag_down,
):
    n, d = tokens.shape
    h, f = w_query.shape[1], w_gate.shape[1]
    cosine, sine = (jnp.asarray(t) for t in rope_tables(n))
    core, z, xh = (lax.axis_index(a).astype(jnp.int32)[None] for a in ("core", "z", "xh"))
    lq, lk, lv, lo, lg, lu, ld = (
        x.T for x in (left_query, left_key, left_value, left_output, left_gate, left_up, left_down)
    )
    gain1, gain2, mag_q, mag_k, mag_v, mag_o, mag_g, mag_u, mag_d = (
        x.reshape(-1, 128) for x in (gain_attn, gain_ffn, mag_query, mag_key, mag_value, mag_output, mag_gate, mag_up, mag_down)
    )
    shard = w_down.shape[0]
    left_shard = lax.dynamic_slice_in_dim(left_down, lax.axis_index(DP) * shard, shard, 0).T
    far = swap(w_down, "xh", 1)
    raw = lax.all_gather(jnp.concatenate([w_down, far], axis=0), ("y", "z", "core"), axis=0, tiled=False)
    sq_d = shard_stats(w_down, left_shard, right_down)
    sq_d = xor_sum(sq_d, ("xh", "mp"))

    (fq, iq, dq), (fk, ik, dk), (fv, iv, dv), (sq_o, do) = stats([
        (w_query, lq, right_query, mag_q), (w_key, lk, right_key, mag_k), (w_value, lv, right_value, mag_v),
        (w_output, lo, right_output, None),
    ])
    sq_d = after(sq_d, sq_o)
    sq_d = sq_d + swap(sq_d, "core", 1)
    sq_d = xor_sum(sq_d, "z")
    sq_o = sq_o + swap(sq_o, "mp", 1)
    fo, io = mag_output[None, :] * lax.rsqrt(sq_o), 1.0 / sq_o

    part_o, aq, ak, av, yo, first, q, k, v, probs, mix = attend(
        lengths, tokens, gain1, (lq, lk, lv), cosine, sine, right_output,
        (right_query, right_key, right_value), (fq, fk, fv), lo, (w_query, w_key, w_value, w_output),
    )
    got_o = swap(part_o, "mp", 1)
    sq_d = xor_sum(after(sq_d, part_o), "y")
    (fg, ig, dg), (fu, iu, du) = stats([(w_gate, lg, right_gate, mag_g), (w_up, lu, after(right_up, part_o), mag_u)])
    fd, idn = mag_down[None, :] * lax.rsqrt(sq_d), 1.0 / sq_d
    part_s, zd, keep_e, send_e, act, down = mlp(
        core, xh, tokens, part_o, got_o, fo, gain2, cotangent, fd, right_down, (lg, lu), ld, (right_gate, right_up),
        (fg, fu), (ig, iu), (dg, du), (mag_g, mag_u), raw, (w_gate, w_up),
    )
    got_s = swap(part_s, "mp", 1)
    part_d, s_d, dd, td, tl = down_forward(act, ld, cotangent, fd, right_down, zd, down)
    far_s = swap(s_d, ("xh", "mp"), 3)
    far_s, got_e = lax.optimization_barrier((far_s, swap(send_e, "core", 1)))
    loc_d, mix_d = down_correction(s_d, far_s, idn, mag_d, right_down, dd, td, ld, tl, down)
    we, wl, wd, me, ml, md = widths = [2 * f + 512, 4 * h + 1024, f + 256, 2 * d, 4 * d, d + 1024]
    got_d = swap(after(part_d, loc_d), "mp", 1)
    *part_f, keep_l, send_l, grad_hidden = back(
        core, part_s, got_s, part_o, got_o, tokens, cotangent, gain2, mag_o, fo, io, right_output, do, yo,
        (aq, ak, av), (lq, lk, lv), cosine, sine, (right_query, right_key, right_value), (fq, fk, fv), (iq, ik, iv),
        (dq, dk, dv), (mag_q, mag_k, mag_v), lo, (loc_d, mix_d),
        (q, k, v), probs, mix, first, (w_query, w_key, w_value, w_output),
    )
    pieces = [(0, 0, we), (1, 0, wl), (1, wl // 2, wd), (0, we // 2, me), (1, (wl + wd) // 2, ml), (1, (wl + wd + ml) // 2, md)]
    own, *sends = quarters(z, (keep_e, keep_l), (got_e, swap(send_l, "core", 1)), pieces)
    *sends, part_f[0], got_d = lax.optimization_barrier((*sends, part_f[0], got_d))
    got_f = [swap(part_f[0], "mp", 1)]
    layer_out = layer_end(tokens, part_o, got_o, fo, part_d, got_d, fd)
    got = [swap(x, "z", k + 1) for k, x in enumerate(sends)]
    own, layer_out, got_f[0] = lax.optimization_barrier((own, layer_out, got_f[0]))
    part = tree([own.astype(F32)] + [x.astype(F32) for x in got]).astype(BF16)
    cut = (we + wl + wd) // 8
    got = [swap(part, "y", k) for k in range(1, 4)]
    got_f.append(swap(after(part_f[1], got_f[0]), "mp", 1))
    some_tokens = token_end(tokens, grad_hidden, gain1, part_f[:1], got_f[:1], 0)
    part, some_tokens, got_f[1] = lax.optimization_barrier((part, some_tokens, got_f[1]))
    part = tree([part.astype(F32)] + [x.astype(F32) for x in got]).astype(BF16)
    mixed = part[:, cut :]
    far, near, across = swap(part, "xh", 1), swap(mixed, "mp", 1), swap(mixed, ("xh", "mp"), 3)
    got_f.append(swap(after(part_f[2], far, near, across), "mp", 1))
    grad_tokens = token_end(tokens, grad_hidden, gain1, part_f[1:], got_f[1:], part_f[0].shape[0], some_tokens)
    total = part.astype(F32) + far.astype(F32)
    other = near.astype(F32) + across.astype(F32)
    part = jnp.concatenate([total[:, : cut], total[:, cut :] + other], axis=1).astype(BF16)
    got = [swap(part, "z", k) for k in range(1, 4)]
    part, grad_tokens = lax.optimization_barrier((part, grad_tokens))
    half = joined(z, [part] + got, widths)
    vec_e, at_l = 2 * f, we
    vec_l, at_d = at_l + 4 * h, at_l + wl
    at_me = at_d + wd
    at_ml = at_me + 2 * d
    at_md = at_ml + 4 * d
    places = [
        (at_ml, d, None), (at_l, h, None), (vec_l, h, 0),
        (at_ml + d, d, None), (at_l + h, h, None), (vec_l, h, 4),
        (at_ml + 2 * d, d, None), (at_l + 2 * h, h, None), (vec_l, h, 8),
        (at_l + 3 * h, h, None), (at_ml + 3 * d, d, None), (vec_l + 256, d, 0),
        (at_me, d, None), (0, f, None), (vec_e, f, 0),
        (at_me + d, d, None), (f, f, None), (vec_e + 256, f, 0),
        (at_d, f, None), (at_md, d, None), (at_md + d, d, 0),
    ]
    outs = unpack(core, half, swap(half, "core", 1), widths, places)
    outs = [x.reshape(-1) if i % 3 == 2 else x.T if i % 3 == 0 else x for i, x in enumerate(outs)]
    return (layer_out, grad_tokens, *outs)


def solution(mesh):
    fine = Mesh(mesh.devices.reshape(4, 2, 4, 2, 2), ("y", "xh", "z", "core", "mp"))
    col, row, vec, rep = P(None, "mp"), P("mp", None), P("mp"), P()
    tok = P(DP, None)
    split, merged = (rep, col, vec), (row, rep, rep)
    return jax.shard_map(
        body,
        mesh=fine,
        in_specs=(tok, P(DP), tok, rep, rep, col, col, col, row, col, col, P(("mp",) + DP, None))
        + split * 3 + merged + split * 2 + merged,
        out_specs=(tok, tok) + split * 3 + merged + split * 2 + merged,
        check_vma=False,
    )
```

```python
import functools
import jax
import jax.numpy as jnp
import numpy as np
from jax import lax
from jax.experimental import pallas as pl
from jax.experimental.pallas import tpu as pltpu
from jax.sharding import Mesh, PartitionSpec as P

HEAD_DIM = 128
RANK = 16
RATIO = 2.0
EPSILON = 1e-05
STATS_WIDTH = 1536
PARTS = (96, 96, 64)
F32 = jnp.float32
BF16 = jnp.bfloat16
DP = ("y", "xh", "z", "core")
ANY = pl.BlockSpec(memory_space=pl.ANY)
SMEM = pl.BlockSpec(memory_space=pltpu.SMEM)
VMEM = pl.BlockSpec(memory_space=pltpu.VMEM)
MIB = 1024 * 1024


def dot(a, b, dims=((1,), (0,))):
    return lax.dot_general(a.astype(BF16), b.astype(BF16), (dims, ((), ())), preferred_element_type=F32)


def dot_nt(a, b):
    return dot(a, b, ((1,), (1,)))


def dot_tn(a, b):
    return dot(a, b, ((0,), (0,)))


def col_sum(v):
    return jnp.sum(v, axis=0, keepdims=True)


def chunks(n, size):
    return [slice(r, min(r + size, n)) for r in range(0, n, size)]


def shape(dims, dtype=F32):
    return jax.ShapeDtypeStruct(dims, dtype)


def row_of(ref, lanes):
    return jnp.concatenate([ref[i : i + 1, :] for i in range(lanes.start // 128, lanes.stop // 128)], axis=1)


def rows_of(height, width):
    return pl.BlockSpec((height, width), lambda j: (j, 0))


def full(x):
    return pl.BlockSpec(x.shape, lambda j, r=len(x.shape): (0,) * r, pipeline_mode=pl.Buffered(1))


def call(kernel, ins, outs, scratch, name, work, traffic, grid=1, mib=60, alias=None):
    return pl.pallas_call(
        kernel,
        grid=(grid,),
        in_specs=[full(x) if block is None else block for x, block in ins],
        out_specs=[full(x) if block is None else block for x, block in outs],
        out_shape=[x for x, _ in outs],
        scratch_shapes=scratch,
        input_output_aliases=alias or {},
        compiler_params=pltpu.CompilerParams(vmem_limit_bytes=mib * MIB),
        cost_estimate=pl.CostEstimate(flops=int(work), bytes_accessed=int(traffic), transcendentals=0),
        name=name,
    )(*[x for x, _ in ins])


class Copies:
    def __init__(self, sems):
        self.sems, self.used, self.waiting = sems, 0, {}

    def start(self, key, src, dst):
        copy = pltpu.make_async_copy(src, dst, self.sems.at[self.used])
        self.used += 1
        copy.start()
        self.waiting.setdefault(key, []).append(copy)

    def wait(self, key):
        for copy in self.waiting.pop(key, []):
            copy.wait()

    def finish(self):
        for key in list(self.waiting):
            self.wait(key)


def tile_of(rows):
    return jnp.concatenate(rows + [jnp.zeros((RANK - len(rows), 256), F32)], axis=0).astype(BF16)


def deal(core_ref, arrays, keep_ref, send_ref):
    for side in range(2):
        @pl.when(core_ref[0] == side)
        def _():
            at = 0
            for ref in arrays:
                w = ref.shape[1] // 2
                keep_ref[:, at : at + w] = ref[:, side * w : (side + 1) * w]
                send_ref[:, at : at + w] = ref[:, (1 - side) * w : (2 - side) * w]
                at += w


def sems(n):
    return pltpu.SemaphoreType.DMA((n,))


def square_sum(w_ref, lanes):
    depth = w_ref.shape[0]
    width = lanes.stop - lanes.start
    if depth % 128:
        v = w_ref[:, lanes].astype(F32)
        return col_sum(v * v)
    parts = []
    for c in chunks(width, 256):
        to = slice(lanes.start + c.start, lanes.start + c.stop)
        squares = jnp.zeros((8, c.stop - c.start), F32)
        for r in chunks(depth, 64):
            chunk = w_ref[r, to].astype(F32)
            squares = squares + jnp.sum((chunk * chunk).reshape(8, 8, c.stop - c.start), axis=0)
        parts.append(col_sum(squares))
    return jnp.concatenate(parts, axis=1)


def stats_kernel(kinds, *refs):
    count = len(kinds)
    w_refs, rest = refs[:count], list(refs[count:])
    ins = [[rest.pop(0) for _ in range(3 if whole else 2)] for whole in kinds]
    outs = [[rest.pop(0) for _ in range(3 if whole else 2)] for whole in kinds]
    bufs, sem = rest[:count], rest[count]
    copies = Copies(sem)
    todo = sorted((lanes.start, i, lanes) for i, w in enumerate(w_refs) for lanes in chunks(w.shape[1], STATS_WIDTH))
    for start, i, lanes in todo:
        copies.start((i, start), w_refs[i].at[:, lanes], bufs[i].at[:, lanes])
    lefts = [x[0][...].astype(BF16) for x in ins]
    grams = [dot_nt(left, left) for left in lefts]
    for start, i, lanes in todo:
        copies.wait((i, start))
        right = ins[i][1][:, lanes]
        lw = dot(lefts[i], bufs[i][:, lanes])
        ld = lw + RATIO * dot(grams[i], right)
        total = square_sum(bufs[i], lanes) + RATIO * col_sum(right * (lw + ld))
        if kinds[i]:
            fac_ref, isq_ref, ld_ref = outs[i]
            isq_ref[:, lanes] = 1.0 / total
            fac_ref[:, lanes] = row_of(ins[i][2], lanes) * lax.rsqrt(total)
        else:
            total_ref, ld_ref = outs[i]
            total_ref[:, lanes] = total
        ld_ref[:, lanes] = ld


def stats(projections):
    kinds = [p[3] is not None for p in projections]
    ins = [(p[0], ANY) for p in projections]
    outs = []
    for (w, left, right, mag), whole in zip(projections, kinds):
        ins += [(left, None), (right, None)] + ([(mag, None)] if whole else [])
        outs += [(shape((1, w.shape[1])), None)] * (2 if whole else 1) + [(shape((RANK, w.shape[1])), None)]
    size = sum(p[0].size for p in projections)
    scratch = [pltpu.VMEM(p[0].shape, BF16) for p in projections] + [sems(16)]
    flat = call(functools.partial(stats_kernel, kinds), ins, outs, scratch, "stats", 2 * RANK * size, 2 * size)
    given = []
    for whole in kinds:
        n = 3 if whole else 2
        given.append(flat[:n])
        flat = flat[n:]
    return given


def unit_rows(v):
    return lax.rsqrt(jnp.mean(v * v, axis=-1, keepdims=True) + EPSILON)


def rotate(v, cosine, sine):
    return v * cosine + pltpu.roll(v, HEAD_DIM // 2, 1) * sine


def attend_kernel(
    length_ref, x_ref, gain_ref, lq_ref, lk_ref, lv_ref, cos_ref, sin_ref, ro_ref, rq_ref, rk_ref, rv_ref, fq_ref, fk_ref, fv_ref, lo_ref,
    wq_ref, wk_ref, wv_ref, wo_ref,
    part_ref, aq_ref, ak_ref, av_ref, yo_ref, first_out, q_out, k_out, v_out, probs_out, mix_out,
    wq, wk, wv, wo, first, q, k, v, probs, mix, sem,
):
    n, d = x_ref.shape
    copies = Copies(sem)
    groups = chunks(wq_ref.shape[1], 256)
    head, rest = groups[0], slice(groups[1].start, groups[-1].stop)
    for key, lanes in (("head", head), ("rest", rest)):
        for w, src in ((wq, wq_ref), (wk, wk_ref), (wv, wv_ref)):
            copies.start(key, src.at[:, lanes], w.at[:, lanes])
    copies.start("rest", wo_ref, wo)
    everything = slice(0, d)
    gain = row_of(gain_ref, everything)
    for r in chunks(n, 16):
        x = x_ref[r, :].astype(F32)
        first[r, :] = (x * unit_rows(x) * gain).astype(BF16)
    for left, out in ((lq_ref, aq_ref), (lk_ref, ak_ref), (lv_ref, av_ref)):
        out[...] = dot_nt(first[...], left[...]).astype(BF16)
    cosine, sine = cos_ref[...], sin_ref[...]
    row = lax.broadcasted_iota(jnp.int32, (n, n), 0)
    col = lax.broadcasted_iota(jnp.int32, (n, n), 1)
    allowed = (col <= row) & (col < length_ref[0])

    def project(lanes):
        def one(w, a, right, fac):
            return (dot(first[...], w[:, lanes]) + RATIO * dot(a[...], right[:, lanes])) * fac[:, lanes]

        vq, vk = one(wq, aq_ref, rq_ref, fq_ref), one(wk, ak_ref, rk_ref, fk_ref)
        v[:, lanes] = one(wv, av_ref, rv_ref, fv_ref).astype(BF16)
        for h in chunks(256, HEAD_DIM):
            to = slice(lanes.start + h.start, lanes.start + h.stop)
            q[:, to] = (rotate(vq[:, h], cosine, sine) * HEAD_DIM**-0.5).astype(BF16)
            k[:, to] = rotate(vk[:, h], cosine, sine).astype(BF16)

    def attention(lanes):
        for h in chunks(256, HEAD_DIM):
            at = slice(lanes.start + h.start, lanes.start + h.stop)
            i = at.start // HEAD_DIM
            scores = jnp.where(allowed, dot_nt(q[:, at], k[:, at]), -1e30)
            e = jnp.exp(scores - jnp.max(scores, axis=-1, keepdims=True))
            probs[i] = (e * (1.0 / jnp.sum(e, axis=-1, keepdims=True))).astype(BF16)
            mix[:, at] = dot(probs[i], v[:, at]).astype(BF16)

    copies.wait("head")
    project(head)
    copies.wait("rest")
    for i, lanes in enumerate(groups):
        if i + 1 < len(groups):
            project(groups[i + 1])
        attention(lanes)
    for src, dst in ((first, first_out), (q, q_out), (k, k_out), (v, v_out), (probs, probs_out), (mix, mix_out)):
        copies.start("end", src, dst)
    yo_ref[...] = dot_nt(mix[...], lo_ref[...]).astype(BF16)
    for lanes in chunks(d, 512):
        part_ref[:, lanes] = (dot(mix[...], wo[:, lanes]) + RATIO * dot(yo_ref[...], ro_ref[:, lanes])).astype(BF16)
    copies.finish()


def attend(length, tokens, gain, lefts, cosine, sine, right_o, rights, facs, left_o, weights):
    n, d = tokens.shape
    h = weights[0].shape[1]
    heads = h // HEAD_DIM
    ins = [(length, SMEM)] + [(x, None) for x in (tokens, gain, *lefts, cosine, sine, right_o, *rights, *facs, left_o)]
    ins += [(w, ANY) for w in weights]
    outs = [(shape((n, d), BF16), None)] + [(shape((n, RANK), BF16), None)] * 4 + [(shape((n, d), BF16), ANY)]
    outs += [(shape((n, h), BF16), ANY)] * 3 + [(shape((heads, n, n), BF16), ANY), (shape((n, h), BF16), ANY)]
    scratch = [pltpu.VMEM(w.shape, BF16) for w in weights] + [pltpu.VMEM((n, d), BF16)] + [pltpu.VMEM((n, h), BF16)] * 3
    scratch += [pltpu.VMEM((heads, n, n), BF16), pltpu.VMEM((n, h), BF16), sems(64)]
    return call(attend_kernel, ins, outs, scratch, "attend", 8 * n * d * h, 8 * d * h)


def mlp_kernel(core_ref, xh_ref, *refs):
    ins, refs = refs[:21], refs[21:]
    raw_ref, wg_ref, wu_ref, ps_ref, zd_ref, keep_ref, send_ref, act_out, wd_out, *refs = refs
    bufs, refs = refs[:21], refs[21:]
    raw, act, wd, wg, wu, gv, uv, av, second, gpd, gpg, gpu, cg, cu, loc_ref, mix_ref, sem = refs
    (
        x_ref, own_ref, got_ref, fo_ref, gain_ref, cot_ref, fd_ref, rd_ref, lg_ref, lu_ref, ldt_ref,
        rg_ref, ru_ref, fg_ref, fu_ref, ig_ref, iu_ref, dg_ref, du_ref, mg_ref, mu_ref,
    ) = bufs
    n, d = cot_ref.shape
    f = wd.shape[0]
    slots, each = raw.shape[0], raw.shape[1]
    pieces, height = raw_ref.shape[0], raw_ref.shape[1] // 2
    per = slots // 2
    rounds = pieces // (each * per)
    copies = Copies(sem)
    groups = chunks(f, 256)
    bounds = [(i * f // rounds) // 256 for i in range(rounds)] + [len(groups)]

    def fetch_weights(i):
        lanes = slice(bounds[i] * 256, bounds[i + 1] * 256)
        copies.start(("w", i), wg_ref.at[:, lanes], wg.at[:, lanes])
        copies.start(("w", i), wu_ref.at[:, lanes], wu.at[:, lanes])

    def fetch(i):
        for c in range(per * i, per * (i + 1)):
            copies.start(("raw", i), raw_ref.at[each * c : each * (c + 1)], raw.at[c % slots])
        if i:
            fetch_weights(i)

    ahead = (0, 1, 2, 3, 4, 8, 9, 11, 12)
    for i in ahead:
        copies.start("ahead", ins[i], bufs[i])
    fetch_weights(0)
    for i in range(len(ins)):
        if i not in ahead:
            copies.start("in", ins[i], bufs[i])
    fetch(0)
    fetch(1)
    copies.wait("ahead")
    gain, fo = row_of(gain_ref, slice(0, d)), fo_ref[...]
    for r in chunks(n, 16):
        hidden = x_ref[r, :].astype(F32) + (own_ref[r, :].astype(F32) + got_ref[r, :].astype(F32)) * fo
        second[r, :] = (hidden * unit_rows(hidden) * gain).astype(BF16)
    ag = dot_nt(second[...], lg_ref[...]).astype(BF16)
    au = dot_nt(second[...], lu_ref[...]).astype(BF16)
    ag2, au2 = ag * RATIO, au * RATIO

    def forward(j):
        lanes, slot = groups[j], j % 2
        gv[slot] = dot(second[...], wg[:, lanes]) + dot(ag2, rg_ref[:, lanes])
        uv[slot] = dot(second[...], wu[:, lanes]) + dot(au2, ru_ref[:, lanes])

    copies.wait(("w", 0))
    for j in range(bounds[1]):
        forward(j)
    copies.wait("in")
    fd = fd_ref[...]
    for r in chunks(n, 16):
        gpd[r, :] = (cot_ref[r, :].astype(F32) * fd).astype(BF16)
    zd = dot_nt(gpd[...], rd_ref[...]).astype(BF16)
    zd_ref[...] = zd
    zd2 = zd * RATIO

    def compact(c):
        y, half = c // 2, c % 2
        for side in range(2):
            at = (y * 16 + half * 4) * height + (xh_ref[0] ^ side) * (8 * height)
            block = jnp.concatenate([raw[c % slots, i, side * height : (side + 1) * height] for i in range(each)], axis=0)
            wd[pl.ds(pl.multiple_of(at, 16), 4 * height), :] = block

    def products(j):
        lanes, slot = groups[j], j % 2
        if j >= bounds[1]:
            forward(j)
        av[slot] = dot_nt(gpd[...], wd[lanes, :]) + dot(zd2, ldt_ref[:, lanes])

    def gates(j):
        lanes, slot = groups[j], j % 2
        fg, fu = fg_ref[:, lanes], fu_ref[:, lanes]
        sum_g, sum_u = jnp.zeros((8, 256), F32), jnp.zeros((8, 256), F32)
        for r in chunks(n, 16):
            g, u, grad_act = gv[slot, r, :] * fg, uv[slot, r, :] * fu, av[slot, r, :]
            sig = 1.0 / (1.0 + jnp.exp(-g))
            silu = g * sig
            act[r, lanes] = (silu * u).astype(BF16)
            grad_gate = grad_act * u * (sig + silu * (1.0 - sig))
            grad_up = grad_act * silu
            gpg[r, lanes] = (grad_gate * fg).astype(BF16)
            gpu[r, lanes] = (grad_up * fu).astype(BF16)
            prod_g, prod_u = grad_gate * g, grad_up * u
            sum_g = sum_g + prod_g[:8] + prod_g[8:]
            sum_u = sum_u + prod_u[:8] + prod_u[8:]
        for total, right, isq, gp, nc in ((sum_g, rg_ref, ig_ref, gpg, cg), (sum_u, ru_ref, iu_ref, gpu, cu)):
            s = col_sum(total)
            nc[:, lanes] = s
            gp[n:, lanes] = (-s * isq[:, lanes] * right[:, lanes]).astype(BF16)

    for i in range(rounds):
        copies.wait(("raw", i))
        copies.wait(("w", i))
        for c in range(per * i, per * (i + 1)):
            compact(c)
        if i + 2 < rounds:
            fetch(i + 2)
        for j in range(bounds[i], bounds[i + 1]):
            products(j)
            if j > bounds[i]:
                gates(j - 1)
        gates(bounds[i + 1] - 1)
    copies.start("end", wd, wd_out)
    copies.start("end", act, act_out)
    for i, (a, gp, isq, ld, mag, nc) in enumerate(((ag, gpg, ig_ref, dg_ref, mg_ref, cg), (au, gpu, iu_ref, du_ref, mu_ref, cu))):
        s = nc[...]
        loc_ref[:, i * f : (i + 1) * f] = (RATIO * (dot_tn(a, gp[:n, :]) - ld[...] * (s * isq[...]))).astype(BF16)
        v = s / row_of(mag, slice(0, f))
        rows = [v[:, lanes] for lanes in groups] + [jnp.zeros((RANK - len(groups), 256), F32)]
        loc_ref[:, 2 * f + 256 * i : 2 * f + 256 * (i + 1)] = jnp.concatenate(rows, axis=0).astype(BF16)
    sides = ((gpg, rg_ref, lg_ref, wg), (gpu, ru_ref, lu_ref, wu))
    zs = [dot_nt(gp[...], right[...]).astype(BF16) for gp, right, _, _ in sides]
    for lanes in chunks(d, 512):
        both = [dot_nt(gp[...], w[lanes, :]) for gp, _, _, w in sides]
        low = sum(dot(z, left[:, lanes]) for z, (_, _, left, _) in zip(zs, sides))
        ps_ref[:, lanes] = (both[0][:n] + both[1][:n] + RATIO * low[:n]).astype(BF16)
        for i, (part, z, (_, _, left, _)) in enumerate(zip(both, zs, sides)):
            out = dot_tn(z[:n], second[:, lanes]) + part[n:] + RATIO * dot(z[n:], left[:, lanes])
            mix_ref[:, i * d + lanes.start : i * d + lanes.stop] = (RATIO * out).astype(BF16)
    deal(core_ref, (loc_ref, mix_ref), keep_ref, send_ref)
    copies.finish()


def mlp(core, xh, tokens, own, got, fac_o, gain, cot, fac_d, right_d, lefts, left_dt, rights, facs, isqs, lds, mags, raw, weights):
    n, d = cot.shape
    f = weights[0].shape[1]
    given = (tokens, own, got, fac_o, gain, cot, fac_d, right_d, *lefts, left_dt, *rights, *facs, *isqs, *lds, *mags)
    ins = [(core, SMEM), (xh, SMEM)] + [(x, ANY) for x in (*given, raw, *weights)]
    wide = 2 * f + 512
    outs = [(shape((n, d), BF16), None), (shape((n, RANK), BF16), None)] + [(shape((RANK, wide // 2 + d), BF16), VMEM)] * 2
    outs += [(shape((n, f), BF16), ANY), (shape((f, d), BF16), ANY)]
    scratch = [pltpu.VMEM(x.shape, x.dtype) for x in given] + [
        pltpu.VMEM((4, 4, *raw.shape[1:]), BF16), pltpu.VMEM((n, f), BF16), pltpu.VMEM((f, d), BF16),
        pltpu.VMEM((d, f), BF16), pltpu.VMEM((d, f), BF16), *[pltpu.VMEM((2, n, 256), F32)] * 3,
        pltpu.VMEM((n, d), BF16), pltpu.VMEM((n, d), BF16), pltpu.VMEM((n + RANK, f), BF16), pltpu.VMEM((n + RANK, f), BF16),
        pltpu.VMEM((1, f), F32), pltpu.VMEM((1, f), F32), pltpu.VMEM((RANK, wide), BF16), pltpu.VMEM((RANK, 2 * d), BF16), sems(48),
    ]
    return call(mlp_kernel, ins, outs, scratch, "mlp", 10 * n * d * f, 6 * d * f, mib=62)


def down_kernel(ldt_ref, fd_ref, rd_ref, zd_ref, act_ref, cot_ref, wd_ref, pd_ref, sd_ref, dd_ref, td_ref, tl_ref, wd, lhs, cot_buf, sem):
    n, f = act_ref.shape
    d = cot_ref.shape[1]
    copies = Copies(sem)
    groups = chunks(d, 512)
    copies.start("act", act_ref, lhs.at[:n, :])
    for lanes in groups:
        copies.start(lanes.start, wd_ref.at[:, lanes], wd.at[:, lanes])
        copies.start(lanes.start, cot_ref.at[:, lanes], cot_buf.at[:, lanes])
    lhs[n:, :] = ldt_ref[...].astype(BF16)
    copies.wait("act")
    low = dot_nt(lhs[...], ldt_ref[...]).astype(BF16)
    tl_ref[...] = dot_tn(zd_ref[...], lhs[:n, :])
    for lanes in groups:
        copies.wait(lanes.start)
        out = dot(lhs[...], wd[:, lanes]) + RATIO * dot(low, rd_ref[:, lanes])
        pd = out[:n].astype(BF16)
        pd_ref[:, lanes] = pd
        dd_ref[:, lanes] = out[n:]
        cot = cot_buf[:, lanes].astype(F32)
        sd_ref[:, lanes] = col_sum(cot * pd.astype(F32)) * fd_ref[:, lanes]
        td_ref[:, lanes] = dot_tn(low[:n], cot * fd_ref[:, lanes])


def down_forward(act, left_dt, cot, fac_d, right_d, zd, w_down):
    n, f = act.shape
    d = cot.shape[1]
    ins = [(x, None) for x in (left_dt, fac_d, right_d, zd)] + [(x, ANY) for x in (act, cot, w_down)]
    outs = [(shape((n, d), BF16), None), (shape((1, d)), None), (shape((RANK, d)), None), (shape((RANK, d)), None), (shape((RANK, f)), None)]
    scratch = [pltpu.VMEM((f, d), BF16), pltpu.VMEM((n + RANK, f), BF16), pltpu.VMEM((n, d), BF16), sems(16)]
    return call(down_kernel, ins, outs, scratch, "down_forward", 2 * n * d * f, 2 * d * f)


def correct_kernel(s0_ref, s1_ref, isq_ref, mag_ref, rd_ref, dd_ref, td_ref, ldt_ref, tl_ref, wd_ref, loc_ref, mix_ref, wd, sem):
    f, d = wd.shape
    copies = Copies(sem)
    groups = chunks(f, 1024)
    for rows in groups:
        copies.start(rows.start, wd_ref.at[rows, :], wd.at[rows, :])
    s = s0_ref[...] + s1_ref[...]
    ncoef = -s * isq_ref[...]
    nr = (ncoef * rd_ref[...]).astype(BF16)
    m = dot_nt(nr, rd_ref[...])
    mix_ref[:, :d] = (RATIO * (td_ref[...] + dd_ref[...] * ncoef)).astype(BF16)
    v = 0.5 * s / row_of(mag_ref, slice(0, d))
    rows = [v[:, lanes] for lanes in chunks(d, 256)]
    mix_ref[:, d : d + 256] = jnp.concatenate(rows + [jnp.zeros((RANK - len(rows), 256), F32)], axis=0).astype(BF16)
    mix_ref[:, d + 256 :] = jnp.zeros((RANK, mix_ref.shape[1] - d - 256), BF16)
    loc_ref[:, f:] = jnp.zeros((RANK, loc_ref.shape[1] - f), BF16)
    for rows in groups:
        copies.wait(rows.start)
        out = tl_ref[:, rows] + dot_nt(nr, wd[rows, :]) + RATIO * dot(m, ldt_ref[:, rows])
        loc_ref[:, rows] = (RATIO * out).astype(BF16)


def down_correction(s0, s1, isq, mag, right_d, dd, td, left_dt, tl, w_down):
    f, d = w_down.shape
    ins = [(x, None) for x in (s0, s1, isq, mag, right_d, dd, td, left_dt, tl)] + [(w_down, ANY)]
    outs = [(shape((RANK, f + 256), BF16), None), (shape((RANK, d + 1024), BF16), None)]
    scratch = [pltpu.VMEM((f, d), BF16), sems(4)]
    return call(correct_kernel, ins, outs, scratch, "down_correction", 2 * RANK * d * f, 2 * d * f)


def back_kernel(
    core_ref, gain_ref, mo_ref, fo_ref, io_ref, ro_ref, do_ref, yo_ref,
    aq_ref, ak_ref, av_ref, lq_ref, lk_ref, lv_ref, cos_ref, sin_ref, rq_ref, rk_ref, rv_ref, fq_ref, fk_ref, fv_ref,
    iq_ref, ik_ref, iv_ref, dq_ref, dk_ref, dv_ref, mq_ref, mk_ref, mv_ref, lo_ref,
    locd_ref, mixd_ref,
    own_hbm, got_hbm, own_o_hbm, got_o_hbm, x_hbm, cot_hbm, q_ref, k_ref, v_ref, probs_ref, mix_ref, first_ref, wq_ref, wk_ref, wv_ref, wo_ref,
    pf0_ref, pf1_ref, pf2_ref, keep_ref, send_ref, gh_out,
    own_ref, got_ref, own_o_ref, got_o_ref, x_ref, cot_ref, q, k, v, probs, mix, first, wq, wk, wv, wo, gh, gpo, gpq, gpk, gpv, sq, sk, sv, loc_ref, mixed_ref, locd, mixd, sem,
):
    n, d = x_ref.shape
    span = wq_ref.shape[1]
    copies = Copies(sem)
    groups = chunks(span, 256)
    for src, dst in ((own_o_hbm, own_o_ref), (got_o_hbm, got_o_ref), (x_hbm, x_ref), (own_hbm, own_ref), (got_hbm, got_ref), (cot_hbm, cot_ref)):
        copies.start(0, src.at[: n // 2, :], dst.at[: n // 2, :])
    for src, dst in ((own_o_hbm, own_o_ref), (got_o_hbm, got_o_ref), (x_hbm, x_ref), (own_hbm, own_ref), (got_hbm, got_ref), (cot_hbm, cot_ref)):
        copies.start(n // 2, src.at[n // 2 :, :], dst.at[n // 2 :, :])
    copies.start("heads", wo_ref, wo)
    for src, dst in ((q_ref, q), (k_ref, k), (v_ref, v), (probs_ref, probs)):
        copies.start("heads", src, dst)
    for src, dst in ((wq_ref, wq), (wk_ref, wk), (wv_ref, wv)):
        copies.start("late", src, dst)
    copies.start("late", mix_ref, mix)
    copies.start("late", first_ref, first)
    gain, fo = row_of(gain_ref, slice(0, d)), fo_ref[...]
    sums = jnp.zeros((8, d), F32)
    for r in chunks(n, 16):
        copies.wait(r.start)
        value = (own_o_ref[r, :].astype(F32) + got_o_ref[r, :].astype(F32)) * fo
        hidden = x_ref[r, :].astype(F32) + value
        inverse = unit_rows(hidden)
        unit = hidden * inverse
        w2 = (own_ref[r, :].astype(F32) + got_ref[r, :].astype(F32)) * gain
        grad = cot_ref[r, :].astype(F32) + inverse * (w2 - unit * jnp.mean(w2 * unit, axis=-1, keepdims=True))
        gh[r, :] = grad
        gpo[r, :] = (grad * fo).astype(BF16)
        both = grad * value
        sums = sums + both[:8] + both[8:]
    copies.start("end", gh, gh_out)
    so = col_sum(sums)
    ncoef = -so * io_ref[...]
    gpo[n:, :] = (ncoef * ro_ref[...]).astype(BF16)
    zo = dot_nt(gpo[...], ro_ref[...]).astype(BF16)
    mixed_ref[:, 3 * d :] = (RATIO * (dot_tn(yo_ref[...], gpo[:n, :]) + do_ref[...] * ncoef)).astype(BF16)
    cosine, sine = cos_ref[...], -sin_ref[...]
    scale = HEAD_DIM**-0.5
    parts_o = []
    copies.wait("heads")
    for lanes in groups:
        both = dot_nt(gpo[...], wo[lanes, :]) + RATIO * dot(zo, lo_ref[:, lanes])
        grad_attn = both[:n].astype(BF16)
        parts_o.append(both[n:])
        for h in chunks(256, HEAD_DIM):
            at = slice(lanes.start + h.start, lanes.start + h.stop)
            ga, p_low = grad_attn[:, h], probs[at.start // HEAD_DIM]
            p = p_low.astype(F32)
            gprobs = dot_nt(ga, v[:, at])
            gscores = (p * (gprobs - jnp.sum(p * gprobs, axis=-1, keepdims=True))).astype(BF16)
            gq = rotate(dot(gscores, k[:, at]), cosine, sine) * scale
            gk = rotate(dot_tn(gscores, q[:, at]), cosine, sine)
            gv = dot_tn(p_low, ga)
            vq = rotate(q[:, at].astype(F32), cosine, sine) * (1.0 / scale)
            vk = rotate(k[:, at].astype(F32), cosine, sine)
            for grad, val, fac, isq, right, gp, s_ref in (
                (gq, vq, fq_ref, iq_ref, rq_ref, gpq, sq),
                (gk, vk, fk_ref, ik_ref, rk_ref, gpk, sk),
                (gv, v[:, at].astype(F32), fv_ref, iv_ref, rv_ref, gpv, sv),
            ):
                s = col_sum(grad * val)
                s_ref[:, at] = s
                gp[:n, at] = (grad * fac[:, at]).astype(BF16)
                gp[n:, at] = (-s * isq[:, at] * right[:, at]).astype(BF16)
    sides = ((gpq, rq_ref, lq_ref, wq), (gpk, rk_ref, lk_ref, wk), (gpv, rv_ref, lv_ref, wv))
    zs = [dot_nt(gp[...], right[...]).astype(BF16) for gp, right, _, _ in sides]
    copies.wait("late")
    for lanes in chunks(d, 512):
        both = [dot_nt(gp[...], w[lanes, :]) for gp, _, _, w in sides]
        low = sum(dot(z, left[:, lanes]) for z, (_, _, left, _) in zip(zs, sides))
        pf = (both[0][:n] + both[1][:n] + both[2][:n] + RATIO * low[:n]).astype(BF16)
        at = 0
        for ref in (pf0_ref, pf1_ref, pf2_ref):
            ref[:, lanes] = pf[at : at + ref.shape[0]]
            at += ref.shape[0]
        for i, (part, z, (_, _, left, _)) in enumerate(zip(both, zs, sides)):
            out = dot_tn(z[:n], first[:, lanes]) + part[n:] + RATIO * dot(z[n:], left[:, lanes])
            mixed_ref[:, i * d + lanes.start : i * d + lanes.stop] = (RATIO * out).astype(BF16)
    rows = []
    for i, (a, gp, isq, ld, mag, s_ref) in enumerate((
        (aq_ref, gpq, iq_ref, dq_ref, mq_ref, sq), (ak_ref, gpk, ik_ref, dk_ref, mk_ref, sk), (av_ref, gpv, iv_ref, dv_ref, mv_ref, sv),
    )):
        s = s_ref[...]
        loc_ref[:, i * span : (i + 1) * span] = (RATIO * (dot_tn(a[...], gp[:n, :]) - ld[...] * (s * isq[...]))).astype(BF16)
        v_row = s / row_of(mag, slice(0, span))
        rows += [v_row[:, lanes] for lanes in groups]
    out = dot_tn(zo[:n], mix[...]) + jnp.concatenate(parts_o, axis=1)
    loc_ref[:, 3 * span : 4 * span] = (RATIO * out).astype(BF16)
    locd[...] = locd_ref[...]
    locd[:, locd.shape[1] - 256 :] = tile_of(rows)
    v_row = 0.5 * so / row_of(mo_ref, slice(0, d))
    mixd[...] = mixd_ref[...]
    mixd[:, d + 256 : d + 512] = tile_of([v_row[:, lanes] for lanes in chunks(d, 256)])
    deal(core_ref, (loc_ref, locd, mixed_ref, mixd), keep_ref, send_ref)
    copies.finish()


def back(
    core, own, got, own_o, got_o, tokens, cot, gain, mag_o, fac_o, isq_o, right_o, ld_o, yo, als, lefts, cosine, sine,
    rights, facs, isqs, lds, mags, left_o, downs, qkv, probs, mix, first, weights,
):
    n, d = tokens.shape
    h = weights[0].shape[1]
    ins = [(core, SMEM)] + [(x, None) for x in (gain, mag_o, fac_o, isq_o, right_o, ld_o, yo)]
    ins += [(x, None) for x in (*als, *lefts, cosine, sine, *rights, *facs, *isqs, *lds, *mags, left_o, *downs)]
    ins += [(x, ANY) for x in (own, got, own_o, got_o, tokens, cot, *qkv, probs, mix, first, *weights)]
    wides = (4 * h, 4 * d)
    outs = [(shape((part, d), BF16), None) for part in PARTS]
    outs += [(shape((RANK, (sum(wides) + sum(x.shape[1] for x in downs)) // 2), BF16), VMEM)] * 2 + [(shape((n, d)), ANY)]
    head = pltpu.VMEM((n, h), BF16)
    scratch = [pltpu.VMEM((n, d), BF16)] * 6 + [head] * 3 + [pltpu.VMEM(probs.shape, BF16), head, pltpu.VMEM((n, d), BF16)] + [pltpu.VMEM(w.shape, BF16) for w in weights]
    scratch += [pltpu.VMEM((n, d), F32), pltpu.VMEM((n + RANK, d), BF16)] + [pltpu.VMEM((n + RANK, h), BF16)] * 3
    scratch += [pltpu.VMEM((1, h), F32)] * 3 + [pltpu.VMEM((RANK, w), BF16) for w in wides]
    scratch += [pltpu.VMEM(x.shape, BF16) for x in downs] + [sems(40)]
    return call(back_kernel, ins, outs, scratch, "back", 8 * n * d * h, 8 * d * h)


def layer_kernel(x_ref, own_o_ref, got_o_ref, fo_ref, own_ref, got_ref, fd_ref, out_ref):
    for r in chunks(x_ref.shape[0], 16):
        hidden = x_ref[r, :].astype(F32) + (own_o_ref[r, :].astype(F32) + got_o_ref[r, :].astype(F32)) * fo_ref[...]
        out_ref[r, :] = (hidden + (own_ref[r, :].astype(F32) + got_ref[r, :].astype(F32)) * fd_ref[...]).astype(BF16)


def layer_end(tokens, own_o, got_o, fac_o, own, got, fac_d):
    n, d = tokens.shape
    block = rows_of(128, d)
    ins = [(tokens, block), (own_o, block), (got_o, block), (fac_o, None), (own, block), (got, block), (fac_d, None)]
    return call(layer_kernel, ins, [(shape((n, d), BF16), block)], [], "layer_end", 6 * n * d, 12 * n * d, n // 128)[0]


def token_kernel(first, count, *refs):
    x_hbm, gh_hbm, gain_ref, *refs = refs
    owns, gots, refs = refs[:count], refs[count : 2 * count], refs[2 * count :]
    out_hbm, x_buf, gh_buf, out_buf, sem = refs[-5:]
    rows = slice(first, first + x_buf.shape[0])
    copies = Copies(sem)
    copies.start("in", x_hbm.at[rows, :], x_buf)
    copies.start("in", gh_hbm.at[rows, :], gh_buf)
    gain = row_of(gain_ref, slice(0, x_buf.shape[1]))
    places = [(own, got, r) for own, got in zip(owns, gots) for r in chunks(own.shape[0], 16)]
    copies.wait("in")
    for r, (own, got, to) in zip(chunks(x_buf.shape[0], 16), places):
        x = x_buf[r, :].astype(F32)
        inverse = unit_rows(x)
        unit = x * inverse
        w1 = (own[to, :].astype(F32) + got[to, :].astype(F32)) * gain
        out_buf[r, :] = (gh_buf[r, :] + inverse * (w1 - unit * jnp.mean(w1 * unit, axis=-1, keepdims=True))).astype(BF16)
    copies.start("out", out_buf, out_hbm.at[rows, :])
    copies.finish()


def token_end(tokens, grad_hidden, gain, own, got, first, before=None):
    n, d = tokens.shape
    count = sum(x.shape[0] for x in own)
    ins = [(tokens, ANY), (grad_hidden, ANY), (gain, None)] + [(x, None) for x in (*own, *got)] + ([] if before is None else [(before, ANY)])
    scratch = [pltpu.VMEM((count, d), BF16), pltpu.VMEM((count, d), F32), pltpu.VMEM((count, d), BF16), sems(3)]
    alias = {} if before is None else {len(ins) - 1: 0}
    kernel = functools.partial(token_kernel, first, len(own))
    return call(kernel, ins, [(shape((n, d), BF16), ANY)], scratch, "token_end", 10 * count * d, 12 * count * d, alias=alias)[0]


def shard_kernel(w_ref, left_ref, right_ref, out_ref):
    left, right = left_ref[...], right_ref[...]
    lw = dot(left, w_ref[...])
    ld = lw + RATIO * dot(dot_nt(left, left), right)
    out_ref[...] = square_sum(w_ref, slice(0, w_ref.shape[1])) + RATIO * col_sum(right * (lw + ld))


def shard_stats(w, left, right):
    return call(shard_kernel, [(w, None), (left, None), (right, None)], [(shape((1, w.shape[1])), None)], [], "shard_stats", w.size, w.size)[0]


def quarters_kernel(pieces, z_ref, keep0_ref, got0_ref, keep1_ref, got1_ref, *refs):
    outs, totals = refs[:4], refs[4:]
    for total, keep_ref, got_ref in zip(totals, (keep0_ref, keep1_ref), (got0_ref, got1_ref)):
        total[...] = (keep_ref[...].astype(F32) + got_ref[...].astype(F32)).astype(BF16)
    to = 0
    for which, at, w in pieces:
        q = w // 8
        for k in range(4):
            start = at + (z_ref[0] ^ k) * q
            outs[k][:, to : to + q] = totals[which][:, pl.ds(pl.multiple_of(start, 128), q)]
        to += q


def quarters(z, keeps, gots, pieces):
    width = sum(w for _, _, w in pieces) // 8
    outs = [(shape((RANK, width), BF16), VMEM)] * 4
    ins = [(z, SMEM), (keeps[0], VMEM), (gots[0], VMEM), (keeps[1], VMEM), (gots[1], VMEM)]
    scratch = [pltpu.VMEM(x.shape, BF16) for x in keeps]
    return call(functools.partial(quarters_kernel, pieces), ins, outs, scratch, "quarters", 0, width, mib=16)


def joined_kernel(widths, z_ref, *refs):
    ins, out_ref = refs[:4], refs[4]
    at = to = 0
    for w in widths:
        q = w // 8
        for k in range(4):
            out_ref[:, pl.ds(pl.multiple_of(to + (z_ref[0] ^ k) * q, 128), q)] = ins[k][:, at : at + q]
        at += q
        to += w // 2


def joined(z, parts, widths):
    width = sum(widths) // 2
    ins = [(z, SMEM)] + [(x, VMEM) for x in parts]
    return call(functools.partial(joined_kernel, widths), ins, [(shape((RANK, width), BF16), VMEM)], [], "joined", 0, width, mib=16)[0]


def unpack_kernel(widths, places, core_ref, half_ref, got_ref, *refs):
    whole, outs = refs[-1], refs[:-1]
    for side in range(2):
        @pl.when(core_ref[0] == side)
        def _():
            at = to = 0
            for w in widths:
                h = w // 2
                whole[:, to + side * h : to + (side + 1) * h] = half_ref[:, at : at + h].astype(F32)
                whole[:, to + (1 - side) * h : to + (2 - side) * h] = got_ref[:, at : at + h].astype(F32)
                at += h
                to += w
    for out, (start, count, row) in zip(outs, places):
        if row is None:
            out[...] = whole[:, start : start + count]
        else:
            for i in range(count // 128):
                at = start + i % 2 * 128
                out[i : i + 1, :] = whole[row + i // 2 : row + i // 2 + 1, at : at + 128]


def unpack(core, half, got, widths, places):
    outs = [(shape((RANK, count) if row is None else (count // 128, 128)), None) for _, count, row in places]
    total = sum(widths)
    ins = [(core, SMEM), (half, VMEM), (got, VMEM)]
    return call(functools.partial(unpack_kernel, widths, places), ins, outs, [pltpu.VMEM((RANK, total), F32)], "unpack", 0, total, mib=32)


def swap(x, axis_name, k):
    n = lax.axis_size(axis_name)
    return lax.ppermute(x, axis_name, [(i, i ^ k) for i in range(n)])


def tree(parts):
    while len(parts) > 1:
        parts = [parts[i] + parts[i + 1] for i in range(0, len(parts), 2)]
    return parts[0]


def xor_sum(x, axis_name):
    n = lax.axis_size(axis_name)
    return tree([x] + [swap(x, axis_name, k) for k in range(1, n)])


def after(x, *others):
    return lax.optimization_barrier((x,) + others)[0]


def rope_tables(span):
    half = HEAD_DIM // 2
    frequency = 10000.0 ** (-(np.arange(half, dtype=np.float64) * 2.0) / HEAD_DIM)
    angles = np.arange(span, dtype=np.float64)[:, None] * frequency[None, :]
    cosine, sine = np.cos(angles), np.sin(angles)
    return np.concatenate([cosine, cosine], 1).astype(np.float32), np.concatenate([-sine, sine], 1).astype(np.float32)


def body(
    tokens, lengths, cotangent, gain_attn, gain_ffn,
    w_query, w_key, w_value, w_output, w_gate, w_up, w_down,
    left_query, right_query, mag_query,
    left_key, right_key, mag_key,
    left_value, right_value, mag_value,
    left_output, right_output, mag_output,
    left_gate, right_gate, mag_gate,
    left_up, right_up, mag_up,
    left_down, right_down, mag_down,
):
    n, d = tokens.shape
    h, f = w_query.shape[1], w_gate.shape[1]
    cosine, sine = (jnp.asarray(t) for t in rope_tables(n))
    core, z, xh = (lax.axis_index(a).astype(jnp.int32)[None] for a in ("core", "z", "xh"))
    lq, lk, lv, lo, lg, lu, ld = (
        x.T for x in (left_query, left_key, left_value, left_output, left_gate, left_up, left_down)
    )
    gain1, gain2, mag_q, mag_k, mag_v, mag_o, mag_g, mag_u, mag_d = (
        x.reshape(-1, 128) for x in (gain_attn, gain_ffn, mag_query, mag_key, mag_value, mag_output, mag_gate, mag_up, mag_down)
    )
    shard = w_down.shape[0]
    left_shard = lax.dynamic_slice_in_dim(left_down, lax.axis_index(DP) * shard, shard, 0).T
    far = swap(w_down, "xh", 1)
    raw = lax.all_gather(jnp.concatenate([w_down, far], axis=0), ("y", "z", "core"), axis=0, tiled=False)
    sq_d = shard_stats(w_down, left_shard, right_down)
    sq_d = xor_sum(sq_d, ("xh", "mp"))

    (fq, iq, dq), (fk, ik, dk), (fv, iv, dv), (sq_o, do) = stats([
        (w_query, lq, right_query, mag_q), (w_key, lk, right_key, mag_k), (w_value, lv, right_value, mag_v),
        (w_output, lo, right_output, None),
    ])
    sq_d = after(sq_d, sq_o)
    sq_d = sq_d + swap(sq_d, "core", 1)
    sq_d = xor_sum(sq_d, "z")
    sq_o = sq_o + swap(sq_o, "mp", 1)
    fo, io = mag_output[None, :] * lax.rsqrt(sq_o), 1.0 / sq_o

    part_o, aq, ak, av, yo, first, q, k, v, probs, mix = attend(
        lengths, tokens, gain1, (lq, lk, lv), cosine, sine, right_output,
        (right_query, right_key, right_value), (fq, fk, fv), lo, (w_query, w_key, w_value, w_output),
    )
    got_o = swap(part_o, "mp", 1)
    sq_d = xor_sum(after(sq_d, part_o), "y")
    (fg, ig, dg), (fu, iu, du) = stats([(w_gate, lg, right_gate, mag_g), (w_up, lu, after(right_up, part_o), mag_u)])
    fd, idn = mag_down[None, :] * lax.rsqrt(sq_d), 1.0 / sq_d
    part_s, zd, keep_e, send_e, act, down = mlp(
        core, xh, tokens, part_o, got_o, fo, gain2, cotangent, fd, right_down, (lg, lu), ld, (right_gate, right_up),
        (fg, fu), (ig, iu), (dg, du), (mag_g, mag_u), raw, (w_gate, w_up),
    )
    got_s = swap(part_s, "mp", 1)
    part_d, s_d, dd, td, tl = down_forward(act, ld, cotangent, fd, right_down, zd, down)
    far_s = swap(s_d, ("xh", "mp"), 3)
    far_s, got_e = lax.optimization_barrier((far_s, swap(send_e, "core", 1)))
    loc_d, mix_d = down_correction(s_d, far_s, idn, mag_d, right_down, dd, td, ld, tl, down)
    we, wl, wd, me, ml, md = widths = [2 * f + 512, 4 * h, f + 256, 2 * d, 4 * d, d + 1024]
    got_d = swap(after(part_d, loc_d), "mp", 1)
    *part_f, keep_l, send_l, grad_hidden = back(
        core, part_s, got_s, part_o, got_o, tokens, cotangent, gain2, mag_o, fo, io, right_output, do, yo,
        (aq, ak, av), (lq, lk, lv), cosine, sine, (right_query, right_key, right_value), (fq, fk, fv), (iq, ik, iv),
        (dq, dk, dv), (mag_q, mag_k, mag_v), lo, (loc_d, mix_d),
        (q, k, v), probs, mix, first, (w_query, w_key, w_value, w_output),
    )
    pieces = [(0, 0, we), (1, 0, wl), (1, wl // 2, wd), (0, we // 2, me), (1, (wl + wd) // 2, ml), (1, (wl + wd + ml) // 2, md)]
    own, *sends = quarters(z, (keep_e, keep_l), (got_e, swap(send_l, "core", 1)), pieces)
    *sends, part_f[0], got_d = lax.optimization_barrier((*sends, part_f[0], got_d))
    got_f = [swap(part_f[0], "mp", 1)]
    layer_out = layer_end(tokens, part_o, got_o, fo, part_d, got_d, fd)
    got = [swap(x, "z", k + 1) for k, x in enumerate(sends)]
    own, layer_out, got_f[0] = lax.optimization_barrier((own, layer_out, got_f[0]))
    part = tree([own.astype(F32)] + [x.astype(F32) for x in got]).astype(BF16)
    cut = (we + wl + wd) // 8
    got = [swap(part, "y", k) for k in range(1, 4)]
    got_f.append(swap(after(part_f[1], got_f[0]), "mp", 1))
    some_tokens = token_end(tokens, grad_hidden, gain1, part_f[:1], got_f[:1], 0)
    part, some_tokens, got_f[1] = lax.optimization_barrier((part, some_tokens, got_f[1]))
    part = tree([part.astype(F32)] + [x.astype(F32) for x in got]).astype(BF16)
    mixed = part[:, cut :]
    far, near, across = swap(part, "xh", 1), swap(mixed, "mp", 1), swap(mixed, ("xh", "mp"), 3)
    got_f.append(swap(after(part_f[2], far, near, across), "mp", 1))
    total = part.astype(F32) + far.astype(F32)
    other = near.astype(F32) + across.astype(F32)
    part = jnp.concatenate([total[:, : cut], total[:, cut :] + other], axis=1).astype(BF16)
    got = [swap(part, "z", k) for k in range(1, 4)]
    part, got_f[2] = lax.optimization_barrier((part, got_f[2]))
    half = joined(z, [part] + got, widths)
    grad_tokens = token_end(tokens, grad_hidden, gain1, part_f[1:], got_f[1:], part_f[0].shape[0], some_tokens)
    vec_e, at_l = 2 * f, we
    at_d = at_l + wl
    vec_l = at_d + f
    at_me = at_d + wd
    at_ml = at_me + 2 * d
    at_md = at_ml + 4 * d
    places = [
        (at_ml, d, None), (at_l, h, None), (vec_l, h, 0),
        (at_ml + d, d, None), (at_l + h, h, None), (vec_l, h, 4),
        (at_ml + 2 * d, d, None), (at_l + 2 * h, h, None), (vec_l, h, 8),
        (at_l + 3 * h, h, None), (at_ml + 3 * d, d, None), (at_md + d + 256, d, 0),
        (at_me, d, None), (0, f, None), (vec_e, f, 0),
        (at_me + d, d, None), (f, f, None), (vec_e + 256, f, 0),
        (at_d, f, None), (at_md, d, None), (at_md + d, d, 0),
    ]
    outs = unpack(core, half, swap(half, "core", 1), widths, places)
    outs = [x.reshape(-1) if i % 3 == 2 else x.T if i % 3 == 0 else x for i, x in enumerate(outs)]
    return (layer_out, grad_tokens, *outs)


def solution(mesh):
    fine = Mesh(mesh.devices.reshape(4, 2, 4, 2, 2), ("y", "xh", "z", "core", "mp"))
    col, row, vec, rep = P(None, "mp"), P("mp", None), P("mp"), P()
    tok = P(DP, None)
    split, merged = (rep, col, vec), (row, rep, rep)
    return jax.shard_map(
        body,
        mesh=fine,
        in_specs=(tok, P(DP), tok, rep, rep, col, col, col, row, col, col, P(("mp",) + DP, None))
        + split * 3 + merged + split * 2 + merged,
        out_specs=(tok, tok) + split * 3 + merged + split * 2 + merged,
        check_vma=False,
    )
```

```python
import functools
import jax
import jax.numpy as jnp
import numpy as np
from jax import lax
from jax.experimental import pallas as pl
from jax.experimental.pallas import tpu as pltpu
from jax.sharding import Mesh, PartitionSpec as P

HEAD_DIM = 128
RANK = 16
RATIO = 2.0
EPSILON = 1e-05
STATS_WIDTH = 1536
PARTS = (96, 96, 64)
F32 = jnp.float32
BF16 = jnp.bfloat16
DP = ("y", "xh", "z", "core")
ANY = pl.BlockSpec(memory_space=pl.ANY)
SMEM = pl.BlockSpec(memory_space=pltpu.SMEM)
VMEM = pl.BlockSpec(memory_space=pltpu.VMEM)
MIB = 1024 * 1024


def dot(a, b, dims=((1,), (0,))):
    return lax.dot_general(a.astype(BF16), b.astype(BF16), (dims, ((), ())), preferred_element_type=F32)


def dot_nt(a, b):
    return dot(a, b, ((1,), (1,)))


def dot_tn(a, b):
    return dot(a, b, ((0,), (0,)))


def col_sum(v):
    return jnp.sum(v, axis=0, keepdims=True)


def chunks(n, size):
    return [slice(r, min(r + size, n)) for r in range(0, n, size)]


def shape(dims, dtype=F32):
    return jax.ShapeDtypeStruct(dims, dtype)


def row_of(ref, lanes):
    return jnp.concatenate([ref[i : i + 1, :] for i in range(lanes.start // 128, lanes.stop // 128)], axis=1)


def rows_of(height, width):
    return pl.BlockSpec((height, width), lambda j: (j, 0))


def full(x):
    return pl.BlockSpec(x.shape, lambda j, r=len(x.shape): (0,) * r, pipeline_mode=pl.Buffered(1))


def call(kernel, ins, outs, scratch, name, work, traffic, grid=1, mib=60, alias=None):
    return pl.pallas_call(
        kernel,
        grid=(grid,),
        in_specs=[full(x) if block is None else block for x, block in ins],
        out_specs=[full(x) if block is None else block for x, block in outs],
        out_shape=[x for x, _ in outs],
        scratch_shapes=scratch,
        input_output_aliases=alias or {},
        compiler_params=pltpu.CompilerParams(vmem_limit_bytes=mib * MIB),
        cost_estimate=pl.CostEstimate(flops=int(work), bytes_accessed=int(traffic), transcendentals=0),
        name=name,
    )(*[x for x, _ in ins])


class Copies:
    def __init__(self, sems):
        self.sems, self.used, self.waiting = sems, 0, {}

    def start(self, key, src, dst):
        copy = pltpu.make_async_copy(src, dst, self.sems.at[self.used])
        self.used += 1
        copy.start()
        self.waiting.setdefault(key, []).append(copy)

    def wait(self, key):
        for copy in self.waiting.pop(key, []):
            copy.wait()

    def finish(self):
        for key in list(self.waiting):
            self.wait(key)


def deal(core_ref, arrays, keep_ref, send_ref):
    for side in range(2):
        @pl.when(core_ref[0] == side)
        def _():
            at = 0
            for ref in arrays:
                w = ref.shape[1] // 2
                keep_ref[:, at : at + w] = ref[:, side * w : (side + 1) * w]
                send_ref[:, at : at + w] = ref[:, (1 - side) * w : (2 - side) * w]
                at += w


def sems(n):
    return pltpu.SemaphoreType.DMA((n,))


def square_sum(w_ref, lanes):
    depth = w_ref.shape[0]
    width = lanes.stop - lanes.start
    if depth % 128:
        v = w_ref[:, lanes].astype(F32)
        return col_sum(v * v)
    parts = []
    for c in chunks(width, 256):
        to = slice(lanes.start + c.start, lanes.start + c.stop)
        squares = jnp.zeros((8, c.stop - c.start), F32)
        for r in chunks(depth, 64):
            chunk = w_ref[r, to].astype(F32)
            squares = squares + jnp.sum((chunk * chunk).reshape(8, 8, c.stop - c.start), axis=0)
        parts.append(col_sum(squares))
    return jnp.concatenate(parts, axis=1)


def stats_kernel(kinds, *refs):
    count = len(kinds)
    w_refs, rest = refs[:count], list(refs[count:])
    ins = [[rest.pop(0) for _ in range(3 if whole else 2)] for whole in kinds]
    outs = [[rest.pop(0) for _ in range(3 if whole else 2)] for whole in kinds]
    bufs, sem = rest[:count], rest[count]
    copies = Copies(sem)
    todo = sorted((lanes.start, i, lanes) for i, w in enumerate(w_refs) for lanes in chunks(w.shape[1], STATS_WIDTH))
    for start, i, lanes in todo:
        copies.start((i, start), w_refs[i].at[:, lanes], bufs[i].at[:, lanes])
    lefts = [x[0][...].astype(BF16) for x in ins]
    grams = [dot_nt(left, left) for left in lefts]
    for start, i, lanes in todo:
        copies.wait((i, start))
        right = ins[i][1][:, lanes]
        lw = dot(lefts[i], bufs[i][:, lanes])
        ld = lw + RATIO * dot(grams[i], right)
        total = square_sum(bufs[i], lanes) + RATIO * col_sum(right * (lw + ld))
        if kinds[i]:
            fac_ref, isq_ref, ld_ref = outs[i]
            isq_ref[:, lanes] = 1.0 / total
            fac_ref[:, lanes] = row_of(ins[i][2], lanes) * lax.rsqrt(total)
        else:
            total_ref, ld_ref = outs[i]
            total_ref[:, lanes] = total
        ld_ref[:, lanes] = ld


def stats(projections):
    kinds = [p[3] is not None for p in projections]
    ins = [(p[0], ANY) for p in projections]
    outs = []
    for (w, left, right, mag), whole in zip(projections, kinds):
        ins += [(left, None), (right, None)] + ([(mag, None)] if whole else [])
        outs += [(shape((1, w.shape[1])), None)] * (2 if whole else 1) + [(shape((RANK, w.shape[1])), None)]
    size = sum(p[0].size for p in projections)
    scratch = [pltpu.VMEM(p[0].shape, BF16) for p in projections] + [sems(16)]
    flat = call(functools.partial(stats_kernel, kinds), ins, outs, scratch, "stats", 2 * RANK * size, 2 * size)
    given = []
    for whole in kinds:
        n = 3 if whole else 2
        given.append(flat[:n])
        flat = flat[n:]
    return given


def unit_rows(v):
    return lax.rsqrt(jnp.mean(v * v, axis=-1, keepdims=True) + EPSILON)


def rotate(v, cosine, sine):
    return v * cosine + pltpu.roll(v, HEAD_DIM // 2, 1) * sine


def attend_kernel(
    length_ref, x_ref, gain_ref, lq_ref, lk_ref, lv_ref, cos_ref, sin_ref, ro_ref, rq_ref, rk_ref, rv_ref, fq_ref, fk_ref, fv_ref, lo_ref,
    wq_ref, wk_ref, wv_ref, wo_ref,
    part_ref, aq_ref, ak_ref, av_ref, yo_ref, first_out, q_out, k_out, v_out, probs_out, mix_out,
    wq, wk, wv, wo, first, q, k, v, probs, mix, sem,
):
    n, d = x_ref.shape
    copies = Copies(sem)
    groups = chunks(wq_ref.shape[1], 256)
    head, rest = groups[0], slice(groups[1].start, groups[-1].stop)
    for key, lanes in (("head", head), ("rest", rest)):
        for w, src in ((wq, wq_ref), (wk, wk_ref), (wv, wv_ref)):
            copies.start(key, src.at[:, lanes], w.at[:, lanes])
    copies.start("rest", wo_ref, wo)
    everything = slice(0, d)
    gain = row_of(gain_ref, everything)
    for r in chunks(n, 16):
        x = x_ref[r, :].astype(F32)
        first[r, :] = (x * unit_rows(x) * gain).astype(BF16)
    for left, out in ((lq_ref, aq_ref), (lk_ref, ak_ref), (lv_ref, av_ref)):
        out[...] = dot_nt(first[...], left[...]).astype(BF16)
    cosine, sine = cos_ref[...], sin_ref[...]
    row = lax.broadcasted_iota(jnp.int32, (n, n), 0)
    col = lax.broadcasted_iota(jnp.int32, (n, n), 1)
    allowed = (col <= row) & (col < length_ref[0])

    def project(lanes):
        def one(w, a, right, fac):
            return (dot(first[...], w[:, lanes]) + RATIO * dot(a[...], right[:, lanes])) * fac[:, lanes]

        vq, vk = one(wq, aq_ref, rq_ref, fq_ref), one(wk, ak_ref, rk_ref, fk_ref)
        v[:, lanes] = one(wv, av_ref, rv_ref, fv_ref).astype(BF16)
        for h in chunks(256, HEAD_DIM):
            to = slice(lanes.start + h.start, lanes.start + h.stop)
            q[:, to] = (rotate(vq[:, h], cosine, sine) * HEAD_DIM**-0.5).astype(BF16)
            k[:, to] = rotate(vk[:, h], cosine, sine).astype(BF16)

    def attention(lanes):
        for h in chunks(256, HEAD_DIM):
            at = slice(lanes.start + h.start, lanes.start + h.stop)
            i = at.start // HEAD_DIM
            scores = jnp.where(allowed, dot_nt(q[:, at], k[:, at]), -1e30)
            e = jnp.exp(scores - jnp.max(scores, axis=-1, keepdims=True))
            probs[i] = (e * (1.0 / jnp.sum(e, axis=-1, keepdims=True))).astype(BF16)
            mix[:, at] = dot(probs[i], v[:, at]).astype(BF16)

    copies.wait("head")
    project(head)
    copies.wait("rest")
    for i, lanes in enumerate(groups):
        if i + 1 < len(groups):
            project(groups[i + 1])
        attention(lanes)
    for src, dst in ((first, first_out), (q, q_out), (k, k_out), (v, v_out), (probs, probs_out), (mix, mix_out)):
        copies.start("end", src, dst)
    yo_ref[...] = dot_nt(mix[...], lo_ref[...]).astype(BF16)
    for lanes in chunks(d, 512):
        part_ref[:, lanes] = (dot(mix[...], wo[:, lanes]) + RATIO * dot(yo_ref[...], ro_ref[:, lanes])).astype(BF16)
    copies.finish()


def attend(length, tokens, gain, lefts, cosine, sine, right_o, rights, facs, left_o, weights):
    n, d = tokens.shape
    h = weights[0].shape[1]
    heads = h // HEAD_DIM
    ins = [(length, SMEM)] + [(x, None) for x in (tokens, gain, *lefts, cosine, sine, right_o, *rights, *facs, left_o)]
    ins += [(w, ANY) for w in weights]
    outs = [(shape((n, d), BF16), None)] + [(shape((n, RANK), BF16), None)] * 4 + [(shape((n, d), BF16), ANY)]
    outs += [(shape((n, h), BF16), ANY)] * 3 + [(shape((heads, n, n), BF16), ANY), (shape((n, h), BF16), ANY)]
    scratch = [pltpu.VMEM(w.shape, BF16) for w in weights] + [pltpu.VMEM((n, d), BF16)] + [pltpu.VMEM((n, h), BF16)] * 3
    scratch += [pltpu.VMEM((heads, n, n), BF16), pltpu.VMEM((n, h), BF16), sems(64)]
    return call(attend_kernel, ins, outs, scratch, "attend", 8 * n * d * h, 8 * d * h)


def mlp_kernel(core_ref, xh_ref, *refs):
    ins, refs = refs[:21], refs[21:]
    raw_ref, wg_ref, wu_ref, ps_ref, zd_ref, keep_ref, send_ref, act_out, wd_out, *refs = refs
    bufs, refs = refs[:21], refs[21:]
    raw, act, wd, wg, wu, gv, uv, av, second, gpd, gpg, gpu, cg, cu, loc_ref, mix_ref, sem = refs
    (
        x_ref, own_ref, got_ref, fo_ref, gain_ref, cot_ref, fd_ref, rd_ref, lg_ref, lu_ref, ldt_ref,
        rg_ref, ru_ref, fg_ref, fu_ref, ig_ref, iu_ref, dg_ref, du_ref, mg_ref, mu_ref,
    ) = bufs
    n, d = cot_ref.shape
    f = wd.shape[0]
    slots, each = raw.shape[0], raw.shape[1]
    pieces, height = raw_ref.shape[0], raw_ref.shape[1] // 2
    per = slots // 2
    rounds = pieces // (each * per)
    copies = Copies(sem)
    groups = chunks(f, 256)
    bounds = [(i * f // rounds) // 256 for i in range(rounds)] + [len(groups)]

    def fetch_weights(i):
        lanes = slice(bounds[i] * 256, bounds[i + 1] * 256)
        copies.start(("w", i), wg_ref.at[:, lanes], wg.at[:, lanes])
        copies.start(("w", i), wu_ref.at[:, lanes], wu.at[:, lanes])

    def fetch(i):
        for c in range(per * i, per * (i + 1)):
            copies.start(("raw", i), raw_ref.at[each * c : each * (c + 1)], raw.at[c % slots])
        if i:
            fetch_weights(i)

    ahead = (0, 1, 2, 3, 4, 8, 9, 11, 12)
    for i in ahead:
        copies.start("ahead", ins[i], bufs[i])
    fetch_weights(0)
    for i in range(len(ins)):
        if i not in ahead:
            copies.start("in", ins[i], bufs[i])
    fetch(0)
    fetch(1)
    copies.wait("ahead")
    gain, fo = row_of(gain_ref, slice(0, d)), fo_ref[...]
    for r in chunks(n, 16):
        hidden = x_ref[r, :].astype(F32) + (own_ref[r, :].astype(F32) + got_ref[r, :].astype(F32)) * fo
        second[r, :] = (hidden * unit_rows(hidden) * gain).astype(BF16)
    ag = dot_nt(second[...], lg_ref[...]).astype(BF16)
    au = dot_nt(second[...], lu_ref[...]).astype(BF16)
    ag2, au2 = ag * RATIO, au * RATIO

    def forward(j):
        lanes, slot = groups[j], j % 2
        gv[slot] = dot(second[...], wg[:, lanes]) + dot(ag2, rg_ref[:, lanes])
        uv[slot] = dot(second[...], wu[:, lanes]) + dot(au2, ru_ref[:, lanes])

    copies.wait(("w", 0))
    for j in range(bounds[1]):
        forward(j)
    copies.wait("in")
    fd = fd_ref[...]
    for r in chunks(n, 16):
        gpd[r, :] = (cot_ref[r, :].astype(F32) * fd).astype(BF16)
    zd = dot_nt(gpd[...], rd_ref[...]).astype(BF16)
    zd_ref[...] = zd
    zd2 = zd * RATIO

    def compact(c):
        y, half = c // 2, c % 2
        for side in range(2):
            at = (y * 16 + half * 4) * height + (xh_ref[0] ^ side) * (8 * height)
            block = jnp.concatenate([raw[c % slots, i, side * height : (side + 1) * height] for i in range(each)], axis=0)
            wd[pl.ds(pl.multiple_of(at, 16), 4 * height), :] = block

    def products(j):
        lanes, slot = groups[j], j % 2
        if j >= bounds[1]:
            forward(j)
        av[slot] = dot_nt(gpd[...], wd[lanes, :]) + dot(zd2, ldt_ref[:, lanes])

    def gates(j):
        lanes, slot = groups[j], j % 2
        fg, fu = fg_ref[:, lanes], fu_ref[:, lanes]
        sum_g, sum_u = jnp.zeros((8, 256), F32), jnp.zeros((8, 256), F32)
        for r in chunks(n, 16):
            g, u, grad_act = gv[slot, r, :] * fg, uv[slot, r, :] * fu, av[slot, r, :]
            sig = 1.0 / (1.0 + jnp.exp(-g))
            silu = g * sig
            act[r, lanes] = (silu * u).astype(BF16)
            grad_gate = grad_act * u * (sig + silu * (1.0 - sig))
            grad_up = grad_act * silu
            gpg[r, lanes] = (grad_gate * fg).astype(BF16)
            gpu[r, lanes] = (grad_up * fu).astype(BF16)
            prod_g, prod_u = grad_gate * g, grad_up * u
            sum_g = sum_g + prod_g[:8] + prod_g[8:]
            sum_u = sum_u + prod_u[:8] + prod_u[8:]
        for total, right, isq, gp, nc in ((sum_g, rg_ref, ig_ref, gpg, cg), (sum_u, ru_ref, iu_ref, gpu, cu)):
            s = col_sum(total)
            nc[:, lanes] = s
            gp[n:, lanes] = (-s * isq[:, lanes] * right[:, lanes]).astype(BF16)

    for i in range(rounds):
        copies.wait(("raw", i))
        copies.wait(("w", i))
        for c in range(per * i, per * (i + 1)):
            compact(c)
        if i + 2 < rounds:
            fetch(i + 2)
        for j in range(bounds[i], bounds[i + 1]):
            products(j)
            if j > bounds[i]:
                gates(j - 1)
        gates(bounds[i + 1] - 1)
    copies.start("end", wd, wd_out)
    copies.start("end", act, act_out)
    for i, (a, gp, isq, ld, mag, nc) in enumerate(((ag, gpg, ig_ref, dg_ref, mg_ref, cg), (au, gpu, iu_ref, du_ref, mu_ref, cu))):
        s = nc[...]
        loc_ref[:, i * f : (i + 1) * f] = (RATIO * (dot_tn(a, gp[:n, :]) - ld[...] * (s * isq[...]))).astype(BF16)
        v = s / row_of(mag, slice(0, f))
        rows = [v[:, lanes] for lanes in groups] + [jnp.zeros((RANK - len(groups), 256), F32)]
        loc_ref[:, 2 * f + 256 * i : 2 * f + 256 * (i + 1)] = jnp.concatenate(rows, axis=0).astype(BF16)
    sides = ((gpg, rg_ref, lg_ref, wg), (gpu, ru_ref, lu_ref, wu))
    zs = [dot_nt(gp[...], right[...]).astype(BF16) for gp, right, _, _ in sides]
    for lanes in chunks(d, 256):
        both = [dot_nt(gp[...], w[lanes, :]) for gp, _, _, w in sides]
        low = sum(dot(z, left[:, lanes]) for z, (_, _, left, _) in zip(zs, sides))
        ps_ref[:, lanes] = (both[0][:n] + both[1][:n] + RATIO * low[:n]).astype(BF16)
        for i, (part, z, (_, _, left, _)) in enumerate(zip(both, zs, sides)):
            out = dot_tn(z[:n], second[:, lanes]) + part[n:] + RATIO * dot(z[n:], left[:, lanes])
            mix_ref[:, i * d + lanes.start : i * d + lanes.stop] = (RATIO * out).astype(BF16)
    deal(core_ref, (loc_ref, mix_ref), keep_ref, send_ref)
    copies.finish()


def mlp(core, xh, tokens, own, got, fac_o, gain, cot, fac_d, right_d, lefts, left_dt, rights, facs, isqs, lds, mags, raw, weights):
    n, d = cot.shape
    f = weights[0].shape[1]
    given = (tokens, own, got, fac_o, gain, cot, fac_d, right_d, *lefts, left_dt, *rights, *facs, *isqs, *lds, *mags)
    ins = [(core, SMEM), (xh, SMEM)] + [(x, ANY) for x in (*given, raw, *weights)]
    wide = 2 * f + 512
    outs = [(shape((n, d), BF16), None), (shape((n, RANK), BF16), None)] + [(shape((RANK, wide // 2 + d), BF16), VMEM)] * 2
    outs += [(shape((n, f), BF16), ANY), (shape((f, d), BF16), ANY)]
    scratch = [pltpu.VMEM(x.shape, x.dtype) for x in given] + [
        pltpu.VMEM((4, 4, *raw.shape[1:]), BF16), pltpu.VMEM((n, f), BF16), pltpu.VMEM((f, d), BF16),
        pltpu.VMEM((d, f), BF16), pltpu.VMEM((d, f), BF16), *[pltpu.VMEM((2, n, 256), F32)] * 3,
        pltpu.VMEM((n, d), BF16), pltpu.VMEM((n, d), BF16), pltpu.VMEM((n + RANK, f), BF16), pltpu.VMEM((n + RANK, f), BF16),
        pltpu.VMEM((1, f), F32), pltpu.VMEM((1, f), F32), pltpu.VMEM((RANK, wide), BF16), pltpu.VMEM((RANK, 2 * d), BF16), sems(48),
    ]
    return call(mlp_kernel, ins, outs, scratch, "mlp", 10 * n * d * f, 6 * d * f, mib=62)


def down_kernel(ldt_ref, fd_ref, rd_ref, zd_ref, act_ref, cot_ref, wd_ref, pd_ref, sd_ref, dd_ref, td_ref, tl_ref, wd, lhs, cot_buf, sem):
    n, f = act_ref.shape
    d = cot_ref.shape[1]
    copies = Copies(sem)
    groups = chunks(d, 512)
    copies.start("act", act_ref, lhs.at[:n, :])
    for lanes in groups:
        copies.start(lanes.start, wd_ref.at[:, lanes], wd.at[:, lanes])
        copies.start(lanes.start, cot_ref.at[:, lanes], cot_buf.at[:, lanes])
    lhs[n:, :] = ldt_ref[...].astype(BF16)
    copies.wait("act")
    low = dot_nt(lhs[...], ldt_ref[...]).astype(BF16)
    tl_ref[...] = dot_tn(zd_ref[...], lhs[:n, :])
    for lanes in groups:
        copies.wait(lanes.start)
        out = dot(lhs[...], wd[:, lanes]) + RATIO * dot(low, rd_ref[:, lanes])
        pd = out[:n].astype(BF16)
        pd_ref[:, lanes] = pd
        dd_ref[:, lanes] = out[n:]
        cot = cot_buf[:, lanes].astype(F32)
        sd_ref[:, lanes] = col_sum(cot * pd.astype(F32)) * fd_ref[:, lanes]
        td_ref[:, lanes] = dot_tn(low[:n], cot * fd_ref[:, lanes])


def down_forward(act, left_dt, cot, fac_d, right_d, zd, w_down):
    n, f = act.shape
    d = cot.shape[1]
    ins = [(x, None) for x in (left_dt, fac_d, right_d, zd)] + [(x, ANY) for x in (act, cot, w_down)]
    outs = [(shape((n, d), BF16), None), (shape((1, d)), None), (shape((RANK, d)), None), (shape((RANK, d)), None), (shape((RANK, f)), None)]
    scratch = [pltpu.VMEM((f, d), BF16), pltpu.VMEM((n + RANK, f), BF16), pltpu.VMEM((n, d), BF16), sems(16)]
    return call(down_kernel, ins, outs, scratch, "down_forward", 2 * n * d * f, 2 * d * f)


def correct_kernel(s0_ref, s1_ref, isq_ref, mag_ref, rd_ref, dd_ref, td_ref, ldt_ref, tl_ref, wd_ref, loc_ref, mix_ref, wd, sem):
    f, d = wd.shape
    copies = Copies(sem)
    groups = chunks(f, 1024)
    for rows in groups:
        copies.start(rows.start, wd_ref.at[rows, :], wd.at[rows, :])
    s = s0_ref[...] + s1_ref[...]
    ncoef = -s * isq_ref[...]
    nr = (ncoef * rd_ref[...]).astype(BF16)
    m = dot_nt(nr, rd_ref[...])
    mix_ref[:, :d] = (RATIO * (td_ref[...] + dd_ref[...] * ncoef)).astype(BF16)
    v = 0.5 * s / row_of(mag_ref, slice(0, d))
    rows = [v[:, lanes] for lanes in chunks(d, 256)]
    mix_ref[:, d : d + 256] = jnp.concatenate(rows + [jnp.zeros((RANK - len(rows), 256), F32)], axis=0).astype(BF16)
    mix_ref[:, d + 256 :] = jnp.zeros((RANK, mix_ref.shape[1] - d - 256), BF16)
    loc_ref[:, f:] = jnp.zeros((RANK, loc_ref.shape[1] - f), BF16)
    for rows in groups:
        copies.wait(rows.start)
        out = tl_ref[:, rows] + dot_nt(nr, wd[rows, :]) + RATIO * dot(m, ldt_ref[:, rows])
        loc_ref[:, rows] = (RATIO * out).astype(BF16)


def down_correction(s0, s1, isq, mag, right_d, dd, td, left_dt, tl, w_down):
    f, d = w_down.shape
    ins = [(x, None) for x in (s0, s1, isq, mag, right_d, dd, td, left_dt, tl)] + [(w_down, ANY)]
    outs = [(shape((RANK, f + 256), BF16), None), (shape((RANK, d + 1024), BF16), None)]
    scratch = [pltpu.VMEM((f, d), BF16), sems(4)]
    return call(correct_kernel, ins, outs, scratch, "down_correction", 2 * RANK * d * f, 2 * d * f)


def back_kernel(
    core_ref, gain_ref, mo_ref, fo_ref, io_ref, ro_ref, do_ref, yo_ref,
    aq_ref, ak_ref, av_ref, lq_ref, lk_ref, lv_ref, cos_ref, sin_ref, rq_ref, rk_ref, rv_ref, fq_ref, fk_ref, fv_ref,
    iq_ref, ik_ref, iv_ref, dq_ref, dk_ref, dv_ref, mq_ref, mk_ref, mv_ref, lo_ref,
    locd_ref, mixd_ref,
    own_hbm, got_hbm, own_o_hbm, got_o_hbm, x_hbm, cot_hbm, q_ref, k_ref, v_ref, probs_ref, mix_ref, first_ref, wq_ref, wk_ref, wv_ref, wo_ref,
    pf0_ref, pf1_ref, pf2_ref, keep_ref, send_ref, gh_out,
    own_ref, got_ref, own_o_ref, got_o_ref, x_ref, cot_ref, q, k, v, probs, mix, first, wq, wk, wv, wo, gh, gpo, gpq, gpk, gpv, sq, sk, sv, loc_ref, mixed_ref, sem,
):
    n, d = x_ref.shape
    span = wq_ref.shape[1]
    copies = Copies(sem)
    groups = chunks(span, 256)
    for src, dst in ((own_o_hbm, own_o_ref), (got_o_hbm, got_o_ref), (x_hbm, x_ref), (own_hbm, own_ref), (got_hbm, got_ref), (cot_hbm, cot_ref)):
        copies.start(0, src.at[: n // 2, :], dst.at[: n // 2, :])
    for src, dst in ((own_o_hbm, own_o_ref), (got_o_hbm, got_o_ref), (x_hbm, x_ref), (own_hbm, own_ref), (got_hbm, got_ref), (cot_hbm, cot_ref)):
        copies.start(n // 2, src.at[n // 2 :, :], dst.at[n // 2 :, :])
    copies.start("heads", wo_ref, wo)
    for src, dst in ((q_ref, q), (k_ref, k), (v_ref, v), (probs_ref, probs)):
        copies.start("heads", src, dst)
    for src, dst in ((wq_ref, wq), (wk_ref, wk), (wv_ref, wv)):
        copies.start("late", src, dst)
    copies.start("late", mix_ref, mix)
    copies.start("late", first_ref, first)
    gain, fo = row_of(gain_ref, slice(0, d)), fo_ref[...]
    sums = jnp.zeros((8, d), F32)
    for r in chunks(n, 16):
        copies.wait(r.start)
        value = (own_o_ref[r, :].astype(F32) + got_o_ref[r, :].astype(F32)) * fo
        hidden = x_ref[r, :].astype(F32) + value
        inverse = unit_rows(hidden)
        unit = hidden * inverse
        w2 = (own_ref[r, :].astype(F32) + got_ref[r, :].astype(F32)) * gain
        grad = cot_ref[r, :].astype(F32) + inverse * (w2 - unit * jnp.mean(w2 * unit, axis=-1, keepdims=True))
        gh[r, :] = grad
        gpo[r, :] = (grad * fo).astype(BF16)
        both = grad * value
        sums = sums + both[:8] + both[8:]
    copies.start("end", gh, gh_out)
    so = col_sum(sums)
    ncoef = -so * io_ref[...]
    gpo[n:, :] = (ncoef * ro_ref[...]).astype(BF16)
    zo = dot_nt(gpo[...], ro_ref[...]).astype(BF16)
    mixed_ref[:, 3 * d :] = (RATIO * (dot_tn(yo_ref[...], gpo[:n, :]) + do_ref[...] * ncoef)).astype(BF16)
    cosine, sine = cos_ref[...], -sin_ref[...]
    scale = HEAD_DIM**-0.5
    parts_o = []
    copies.wait("heads")
    for lanes in groups:
        both = dot_nt(gpo[...], wo[lanes, :]) + RATIO * dot(zo, lo_ref[:, lanes])
        grad_attn = both[:n].astype(BF16)
        parts_o.append(both[n:])
        for h in chunks(256, HEAD_DIM):
            at = slice(lanes.start + h.start, lanes.start + h.stop)
            ga, p_low = grad_attn[:, h], probs[at.start // HEAD_DIM]
            p = p_low.astype(F32)
            gprobs = dot_nt(ga, v[:, at])
            gscores = (p * (gprobs - jnp.sum(p * gprobs, axis=-1, keepdims=True))).astype(BF16)
            gq = rotate(dot(gscores, k[:, at]), cosine, sine) * scale
            gk = rotate(dot_tn(gscores, q[:, at]), cosine, sine)
            gv = dot_tn(p_low, ga)
            vq = rotate(q[:, at].astype(F32), cosine, sine) * (1.0 / scale)
            vk = rotate(k[:, at].astype(F32), cosine, sine)
            for grad, val, fac, isq, right, gp, s_ref in (
                (gq, vq, fq_ref, iq_ref, rq_ref, gpq, sq),
                (gk, vk, fk_ref, ik_ref, rk_ref, gpk, sk),
                (gv, v[:, at].astype(F32), fv_ref, iv_ref, rv_ref, gpv, sv),
            ):
                s = col_sum(grad * val)
                s_ref[:, at] = s
                gp[:n, at] = (grad * fac[:, at]).astype(BF16)
                gp[n:, at] = (-s * isq[:, at] * right[:, at]).astype(BF16)
    sides = ((gpq, rq_ref, lq_ref, wq), (gpk, rk_ref, lk_ref, wk), (gpv, rv_ref, lv_ref, wv))
    zs = [dot_nt(gp[...], right[...]).astype(BF16) for gp, right, _, _ in sides]
    copies.wait("late")
    for lanes in chunks(d, 256):
        both = [dot_nt(gp[...], w[lanes, :]) for gp, _, _, w in sides]
        low = sum(dot(z, left[:, lanes]) for z, (_, _, left, _) in zip(zs, sides))
        pf = (both[0][:n] + both[1][:n] + both[2][:n] + RATIO * low[:n]).astype(BF16)
        at = 0
        for ref in (pf0_ref, pf1_ref, pf2_ref):
            ref[:, lanes] = pf[at : at + ref.shape[0]]
            at += ref.shape[0]
        for i, (part, z, (_, _, left, _)) in enumerate(zip(both, zs, sides)):
            out = dot_tn(z[:n], first[:, lanes]) + part[n:] + RATIO * dot(z[n:], left[:, lanes])
            mixed_ref[:, i * d + lanes.start : i * d + lanes.stop] = (RATIO * out).astype(BF16)
    rows = []
    for i, (a, gp, isq, ld, mag, s_ref) in enumerate((
        (aq_ref, gpq, iq_ref, dq_ref, mq_ref, sq), (ak_ref, gpk, ik_ref, dk_ref, mk_ref, sk), (av_ref, gpv, iv_ref, dv_ref, mv_ref, sv),
    )):
        s = s_ref[...]
        loc_ref[:, i * span : (i + 1) * span] = (RATIO * (dot_tn(a[...], gp[:n, :]) - ld[...] * (s * isq[...]))).astype(BF16)
        v_row = s / row_of(mag, slice(0, span))
        rows += [v_row[:, lanes] for lanes in groups]
    out = dot_tn(zo[:n], mix[...]) + jnp.concatenate(parts_o, axis=1)
    loc_ref[:, 3 * span : 4 * span] = (RATIO * out).astype(BF16)
    v_row = so / row_of(mo_ref, slice(0, d))
    more = [v_row[:, lanes] for lanes in chunks(d, 256)]
    tiles = []
    for some in (rows, more):
        tiles.append(jnp.concatenate(some + [jnp.zeros((RANK - len(some), 256), F32)], axis=0))
    loc_ref[:, 4 * span :] = jnp.concatenate(tiles + [jnp.zeros((RANK, 512), F32)], axis=1).astype(BF16)
    deal(core_ref, (loc_ref, locd_ref, mixed_ref, mixd_ref), keep_ref, send_ref)
    copies.finish()


def back(
    core, own, got, own_o, got_o, tokens, cot, gain, mag_o, fac_o, isq_o, right_o, ld_o, yo, als, lefts, cosine, sine,
    rights, facs, isqs, lds, mags, left_o, downs, qkv, probs, mix, first, weights,
):
    n, d = tokens.shape
    h = weights[0].shape[1]
    ins = [(core, SMEM)] + [(x, None) for x in (gain, mag_o, fac_o, isq_o, right_o, ld_o, yo)]
    ins += [(x, None) for x in (*als, *lefts, cosine, sine, *rights, *facs, *isqs, *lds, *mags, left_o, *downs)]
    ins += [(x, ANY) for x in (own, got, own_o, got_o, tokens, cot, *qkv, probs, mix, first, *weights)]
    wides = (4 * h + 1024, 4 * d)
    outs = [(shape((part, d), BF16), None) for part in PARTS]
    outs += [(shape((RANK, (sum(wides) + sum(x.shape[1] for x in downs)) // 2), BF16), VMEM)] * 2 + [(shape((n, d)), ANY)]
    head = pltpu.VMEM((n, h), BF16)
    scratch = [pltpu.VMEM((n, d), BF16)] * 6 + [head] * 3 + [pltpu.VMEM(probs.shape, BF16), head, pltpu.VMEM((n, d), BF16)] + [pltpu.VMEM(w.shape, BF16) for w in weights]
    scratch += [pltpu.VMEM((n, d), F32), pltpu.VMEM((n + RANK, d), BF16)] + [pltpu.VMEM((n + RANK, h), BF16)] * 3
    scratch += [pltpu.VMEM((1, h), F32)] * 3 + [pltpu.VMEM((RANK, w), BF16) for w in wides] + [sems(40)]
    return call(back_kernel, ins, outs, scratch, "back", 8 * n * d * h, 8 * d * h)


def layer_kernel(x_ref, own_o_ref, got_o_ref, fo_ref, own_ref, got_ref, fd_ref, out_ref):
    for r in chunks(x_ref.shape[0], 16):
        hidden = x_ref[r, :].astype(F32) + (own_o_ref[r, :].astype(F32) + got_o_ref[r, :].astype(F32)) * fo_ref[...]
        out_ref[r, :] = (hidden + (own_ref[r, :].astype(F32) + got_ref[r, :].astype(F32)) * fd_ref[...]).astype(BF16)


def layer_end(tokens, own_o, got_o, fac_o, own, got, fac_d):
    n, d = tokens.shape
    block = rows_of(128, d)
    ins = [(tokens, block), (own_o, block), (got_o, block), (fac_o, None), (own, block), (got, block), (fac_d, None)]
    return call(layer_kernel, ins, [(shape((n, d), BF16), block)], [], "layer_end", 6 * n * d, 12 * n * d, n // 128)[0]


def token_kernel(first, count, *refs):
    x_hbm, gh_hbm, gain_ref, *refs = refs
    owns, gots, refs = refs[:count], refs[count : 2 * count], refs[2 * count :]
    out_hbm, x_buf, gh_buf, out_buf, sem = refs[-5:]
    rows = slice(first, first + x_buf.shape[0])
    copies = Copies(sem)
    copies.start("in", x_hbm.at[rows, :], x_buf)
    copies.start("in", gh_hbm.at[rows, :], gh_buf)
    gain = row_of(gain_ref, slice(0, x_buf.shape[1]))
    places = [(own, got, r) for own, got in zip(owns, gots) for r in chunks(own.shape[0], 16)]
    copies.wait("in")
    for r, (own, got, to) in zip(chunks(x_buf.shape[0], 16), places):
        x = x_buf[r, :].astype(F32)
        inverse = unit_rows(x)
        unit = x * inverse
        w1 = (own[to, :].astype(F32) + got[to, :].astype(F32)) * gain
        out_buf[r, :] = (gh_buf[r, :] + inverse * (w1 - unit * jnp.mean(w1 * unit, axis=-1, keepdims=True))).astype(BF16)
    copies.start("out", out_buf, out_hbm.at[rows, :])
    copies.finish()


def token_end(tokens, grad_hidden, gain, own, got, first, before=None):
    n, d = tokens.shape
    count = sum(x.shape[0] for x in own)
    ins = [(tokens, ANY), (grad_hidden, ANY), (gain, None)] + [(x, None) for x in (*own, *got)] + ([] if before is None else [(before, ANY)])
    scratch = [pltpu.VMEM((count, d), BF16), pltpu.VMEM((count, d), F32), pltpu.VMEM((count, d), BF16), sems(3)]
    alias = {} if before is None else {len(ins) - 1: 0}
    kernel = functools.partial(token_kernel, first, len(own))
    return call(kernel, ins, [(shape((n, d), BF16), ANY)], scratch, "token_end", 10 * count * d, 12 * count * d, alias=alias)[0]


def shard_kernel(w_ref, left_ref, right_ref, out_ref):
    left, right = left_ref[...], right_ref[...]
    lw = dot(left, w_ref[...])
    ld = lw + RATIO * dot(dot_nt(left, left), right)
    out_ref[...] = square_sum(w_ref, slice(0, w_ref.shape[1])) + RATIO * col_sum(right * (lw + ld))


def shard_stats(w, left, right):
    return call(shard_kernel, [(w, None), (left, None), (right, None)], [(shape((1, w.shape[1])), None)], [], "shard_stats", w.size, w.size)[0]


def quarters_kernel(pieces, z_ref, keep0_ref, got0_ref, keep1_ref, got1_ref, *refs):
    outs, totals = refs[:4], refs[4:]
    for total, keep_ref, got_ref in zip(totals, (keep0_ref, keep1_ref), (got0_ref, got1_ref)):
        total[...] = (keep_ref[...].astype(F32) + got_ref[...].astype(F32)).astype(BF16)
    to = 0
    for which, at, w in pieces:
        q = w // 8
        for k in range(4):
            start = at + (z_ref[0] ^ k) * q
            outs[k][:, to : to + q] = totals[which][:, pl.ds(pl.multiple_of(start, 128), q)]
        to += q


def quarters(z, keeps, gots, pieces):
    width = sum(w for _, _, w in pieces) // 8
    outs = [(shape((RANK, width), BF16), VMEM)] * 4
    ins = [(z, SMEM), (keeps[0], VMEM), (gots[0], VMEM), (keeps[1], VMEM), (gots[1], VMEM)]
    scratch = [pltpu.VMEM(x.shape, BF16) for x in keeps]
    return call(functools.partial(quarters_kernel, pieces), ins, outs, scratch, "quarters", 0, width, mib=16)


def joined_kernel(widths, z_ref, *refs):
    ins, out_ref = refs[:4], refs[4]
    at = to = 0
    for w in widths:
        q = w // 8
        for k in range(4):
            out_ref[:, pl.ds(pl.multiple_of(to + (z_ref[0] ^ k) * q, 128), q)] = ins[k][:, at : at + q]
        at += q
        to += w // 2


def joined(z, parts, widths):
    width = sum(widths) // 2
    ins = [(z, SMEM)] + [(x, VMEM) for x in parts]
    return call(functools.partial(joined_kernel, widths), ins, [(shape((RANK, width), BF16), VMEM)], [], "joined", 0, width, mib=16)[0]


def unpack_kernel(widths, places, core_ref, half_ref, got_ref, *refs):
    whole, outs = refs[-1], refs[:-1]
    for side in range(2):
        @pl.when(core_ref[0] == side)
        def _():
            at = to = 0
            for w in widths:
                h = w // 2
                whole[:, to + side * h : to + (side + 1) * h] = half_ref[:, at : at + h].astype(F32)
                whole[:, to + (1 - side) * h : to + (2 - side) * h] = got_ref[:, at : at + h].astype(F32)
                at += h
                to += w
    for out, (start, count, row) in zip(outs, places):
        if row is None:
            out[...] = whole[:, start : start + count]
        else:
            for i in range(count // 128):
                at = start + i % 2 * 128
                out[i : i + 1, :] = whole[row + i // 2 : row + i // 2 + 1, at : at + 128]


def unpack(core, half, got, widths, places):
    outs = [(shape((RANK, count) if row is None else (count // 128, 128)), None) for _, count, row in places]
    total = sum(widths)
    ins = [(core, SMEM), (half, VMEM), (got, VMEM)]
    return call(functools.partial(unpack_kernel, widths, places), ins, outs, [pltpu.VMEM((RANK, total), F32)], "unpack", 0, total, mib=32)


def swap(x, axis_name, k):
    n = lax.axis_size(axis_name)
    return lax.ppermute(x, axis_name, [(i, i ^ k) for i in range(n)])


def tree(parts):
    while len(parts) > 1:
        parts = [parts[i] + parts[i + 1] for i in range(0, len(parts), 2)]
    return parts[0]


def xor_sum(x, axis_name):
    n = lax.axis_size(axis_name)
    return tree([x] + [swap(x, axis_name, k) for k in range(1, n)])


def after(x, *others):
    return lax.optimization_barrier((x,) + others)[0]


def rope_tables(span):
    half = HEAD_DIM // 2
    frequency = 10000.0 ** (-(np.arange(half, dtype=np.float64) * 2.0) / HEAD_DIM)
    angles = np.arange(span, dtype=np.float64)[:, None] * frequency[None, :]
    cosine, sine = np.cos(angles), np.sin(angles)
    return np.concatenate([cosine, cosine], 1).astype(np.float32), np.concatenate([-sine, sine], 1).astype(np.float32)


def body(
    tokens, lengths, cotangent, gain_attn, gain_ffn,
    w_query, w_key, w_value, w_output, w_gate, w_up, w_down,
    left_query, right_query, mag_query,
    left_key, right_key, mag_key,
    left_value, right_value, mag_value,
    left_output, right_output, mag_output,
    left_gate, right_gate, mag_gate,
    left_up, right_up, mag_up,
    left_down, right_down, mag_down,
):
    n, d = tokens.shape
    h, f = w_query.shape[1], w_gate.shape[1]
    cosine, sine = (jnp.asarray(t) for t in rope_tables(n))
    core, z, xh = (lax.axis_index(a).astype(jnp.int32)[None] for a in ("core", "z", "xh"))
    lq, lk, lv, lo, lg, lu, ld = (
        x.T for x in (left_query, left_key, left_value, left_output, left_gate, left_up, left_down)
    )
    gain1, gain2, mag_q, mag_k, mag_v, mag_o, mag_g, mag_u, mag_d = (
        x.reshape(-1, 128) for x in (gain_attn, gain_ffn, mag_query, mag_key, mag_value, mag_output, mag_gate, mag_up, mag_down)
    )
    shard = w_down.shape[0]
    left_shard = lax.dynamic_slice_in_dim(left_down, lax.axis_index(DP) * shard, shard, 0).T
    far = swap(w_down, "xh", 1)
    raw = lax.all_gather(jnp.concatenate([w_down, far], axis=0), ("y", "z", "core"), axis=0, tiled=False)
    sq_d = shard_stats(w_down, left_shard, right_down)
    sq_d = xor_sum(sq_d, ("xh", "mp"))

    (fq, iq, dq), (fk, ik, dk), (fv, iv, dv), (sq_o, do) = stats([
        (w_query, lq, right_query, mag_q), (w_key, lk, right_key, mag_k), (w_value, lv, right_value, mag_v),
        (w_output, lo, right_output, None),
    ])
    sq_d = after(sq_d, sq_o)
    sq_d = sq_d + swap(sq_d, "core", 1)
    sq_d = xor_sum(sq_d, "z")
    sq_o = sq_o + swap(sq_o, "mp", 1)
    fo, io = mag_output[None, :] * lax.rsqrt(sq_o), 1.0 / sq_o

    part_o, aq, ak, av, yo, first, q, k, v, probs, mix = attend(
        lengths, tokens, gain1, (lq, lk, lv), cosine, sine, right_output,
        (right_query, right_key, right_value), (fq, fk, fv), lo, (w_query, w_key, w_value, w_output),
    )
    got_o = swap(part_o, "mp", 1)
    sq_d = xor_sum(after(sq_d, part_o), "y")
    (fg, ig, dg), (fu, iu, du) = stats([(w_gate, lg, right_gate, mag_g), (w_up, lu, after(right_up, part_o), mag_u)])
    fd, idn = mag_down[None, :] * lax.rsqrt(sq_d), 1.0 / sq_d
    part_s, zd, keep_e, send_e, act, down = mlp(
        core, xh, tokens, part_o, got_o, fo, gain2, cotangent, fd, right_down, (lg, lu), ld, (right_gate, right_up),
        (fg, fu), (ig, iu), (dg, du), (mag_g, mag_u), raw, (w_gate, w_up),
    )
    got_s = swap(part_s, "mp", 1)
    part_d, s_d, dd, td, tl = down_forward(act, ld, cotangent, fd, right_down, zd, down)
    far_s = swap(s_d, ("xh", "mp"), 3)
    far_s, got_e = lax.optimization_barrier((far_s, swap(send_e, "core", 1)))
    loc_d, mix_d = down_correction(s_d, far_s, idn, mag_d, right_down, dd, td, ld, tl, down)
    we, wl, wd, me, ml, md = widths = [2 * f + 512, 4 * h + 1024, f + 256, 2 * d, 4 * d, d + 1024]
    got_d = swap(after(part_d, loc_d), "mp", 1)
    *part_f, keep_l, send_l, grad_hidden = back(
        core, part_s, got_s, part_o, got_o, tokens, cotangent, gain2, mag_o, fo, io, right_output, do, yo,
        (aq, ak, av), (lq, lk, lv), cosine, sine, (right_query, right_key, right_value), (fq, fk, fv), (iq, ik, iv),
        (dq, dk, dv), (mag_q, mag_k, mag_v), lo, (loc_d, mix_d),
        (q, k, v), probs, mix, first, (w_query, w_key, w_value, w_output),
    )
    pieces = [(0, 0, we), (1, 0, wl), (1, wl // 2, wd), (0, we // 2, me), (1, (wl + wd) // 2, ml), (1, (wl + wd + ml) // 2, md)]
    own, *sends = quarters(z, (keep_e, keep_l), (got_e, swap(send_l, "core", 1)), pieces)
    *sends, part_f[0], got_d = lax.optimization_barrier((*sends, part_f[0], got_d))
    got_f = [swap(part_f[0], "mp", 1)]
    layer_out = layer_end(tokens, part_o, got_o, fo, part_d, got_d, fd)
    got = [swap(x, "z", k + 1) for k, x in enumerate(sends)]
    own, layer_out, got_f[0] = lax.optimization_barrier((own, layer_out, got_f[0]))
    part = tree([own.astype(F32)] + [x.astype(F32) for x in got]).astype(BF16)
    cut = (we + wl + wd) // 8
    got = [swap(part, "y", k) for k in range(1, 4)]
    got_f.append(swap(after(part_f[1], got_f[0]), "mp", 1))
    some_tokens = token_end(tokens, grad_hidden, gain1, part_f[:1], got_f[:1], 0)
    part, some_tokens, got_f[1] = lax.optimization_barrier((part, some_tokens, got_f[1]))
    part = tree([part.astype(F32)] + [x.astype(F32) for x in got]).astype(BF16)
    mixed = part[:, cut :]
    far, near, across = swap(part, "xh", 1), swap(mixed, "mp", 1), swap(mixed, ("xh", "mp"), 3)
    got_f.append(swap(after(part_f[2], far, near, across), "mp", 1))
    grad_tokens = token_end(tokens, grad_hidden, gain1, part_f[1:], got_f[1:], part_f[0].shape[0], some_tokens)
    total = part.astype(F32) + far.astype(F32)
    other = near.astype(F32) + across.astype(F32)
    part = jnp.concatenate([total[:, : cut], total[:, cut :] + other], axis=1).astype(BF16)
    got = [swap(part, "z", k) for k in range(1, 4)]
    part, grad_tokens = lax.optimization_barrier((part, grad_tokens))
    half = joined(z, [part] + got, widths)
    vec_e, at_l = 2 * f, we
    vec_l, at_d = at_l + 4 * h, at_l + wl
    at_me = at_d + wd
    at_ml = at_me + 2 * d
    at_md = at_ml + 4 * d
    places = [
        (at_ml, d, None), (at_l, h, None), (vec_l, h, 0),
        (at_ml + d, d, None), (at_l + h, h, None), (vec_l, h, 4),
        (at_ml + 2 * d, d, None), (at_l + 2 * h, h, None), (vec_l, h, 8),
        (at_l + 3 * h, h, None), (at_ml + 3 * d, d, None), (vec_l + 256, d, 0),
        (at_me, d, None), (0, f, None), (vec_e, f, 0),
        (at_me + d, d, None), (f, f, None), (vec_e + 256, f, 0),
        (at_d, f, None), (at_md, d, None), (at_md + d, d, 0),
    ]
    outs = unpack(core, half, swap(half, "core", 1), widths, places)
    outs = [x.reshape(-1) if i % 3 == 2 else x.T if i % 3 == 0 else x for i, x in enumerate(outs)]
    return (layer_out, grad_tokens, *outs)


def solution(mesh):
    fine = Mesh(mesh.devices.reshape(4, 2, 4, 2, 2), ("y", "xh", "z", "core", "mp"))
    col, row, vec, rep = P(None, "mp"), P("mp", None), P("mp"), P()
    tok = P(DP, None)
    split, merged = (rep, col, vec), (row, rep, rep)
    return jax.shard_map(
        body,
        mesh=fine,
        in_specs=(tok, P(DP), tok, rep, rep, col, col, col, row, col, col, P(("mp",) + DP, None))
        + split * 3 + merged + split * 2 + merged,
        out_specs=(tok, tok) + split * 3 + merged + split * 2 + merged,
        check_vma=False,
    )
```
